32 devices in a mesh: members: 2 (over y), lat: 4 (over z), lon: 2 (over x), lev: 2 (over core).
Axes of the slice: x: 2, y: 2, z: 4, core: 2. Of those that a mesh axis runs over, the one named last changes fastest.
Arguments:
- wind_east: float32 [8, 360, 2880], P(('members', 'lev'), 'lat', 'lon'), parts along dimension 0, may hold values from -6 to 6
- wind_north: float32 [8, 360, 2880], P(('members', 'lev'), 'lat', 'lon'), parts along dimension 0, may hold values from -6 to 6
- thickness: float32 [8, 360, 2880], P(('members', 'lev'), 'lat', 'lon'), parts along dimension 0, may hold values from -6 to 6
- geopot: float32 [8, 360, 2880], P(('members', 'lev'), 'lat', 'lon'), parts along dimension 0, may hold values from -6 to 6
- surface_geopot: float32 [360, 2880], P('lat', 'lon'), may hold values from -6 to 6
- mean_depth: float32 [4], P('lev'), may hold values from 0.5 to 2
- kept_modes: int32 [180], replicated, may hold values from 1 to 360
- slot_table: int32 [180], replicated, may hold values from 0 to 179, as said below
Outputs:
- east_final: float32 [8, 360, 2880], P(('members', 'lev'), 'lat', 'lon'), parts along dimension 0
- north_final: float32 [8, 360, 2880], P(('members', 'lev'), 'lat', 'lon'), parts along dimension 0
- thick_new: float32 [8, 360, 2880], P(('members', 'lev'), 'lat', 'lon'), parts along dimension 0
- geo_new: float32 [8, 360, 2880], P(('members', 'lev'), 'lat', 'lon'), parts along dimension 0
- spectra: float32 [2, 8, 180, 720], P(None, ('members', 'lev'), 'lat', 'lon'), parts along dimension 1
The draws below stay inside these ranges and needn't reach their ends.
There are 2 independent parts, one for each index of `members`. The reference program is written for one: setup_inputs(seed, part) draws one part's arguments, and reference() takes and returns one part's arrays. A program takes and returns all parts, laid end to end along the dimension named above; an argument that names none is the same for every part. Nothing has to cross between parts.
Inputs may be any that keep to these rules, and one draw needn't show every extreme that they name: `slot_table`: every slot 0 to 179 is named once; slot s belongs to latitude device s // 45. Of the 90 polar rows held by latitude device d, 45 name slots of device d and 45 name slots of the device half the lat axis away, (d + 4 / 2) mod 4.
All inputs are finite; a program needn't handle non-finite values.
Results may differ from the reference program's by a relative error of at most 0.00019.
Values sent between devices are 32-bit elements; how exact they have to be, the bound alone decides.
No kernel may reach another device: no remote copies, remote signals or barrier semaphores. Data moves between devices by JAX's collectives and lax.ppermute only.
A program may use at most 64 MiB of HBM per device.

```python
import math
import jax
import jax.numpy as jnp

NLON = 2880
KMAX = 360
LAT_DEV = 90
NLAT = 360
LEVELS = 4
NP = 90
HELP = 45


def draw_kept_modes(key, part):
    row_rank = jnp.arange(2 * NP, dtype=jnp.int32)
    from_pole = jnp.where(row_rank < NP, row_rank, 2 * NP - 1 - row_rank)
    ramp_value = 1 + (KMAX - 1) * from_pole // (NP - 1)
    jitter_span = max(1, KMAX // 16)
    jitter = jax.random.randint(jax.random.fold_in(key, 7), (2 * NP,), -jitter_span, jitter_span + 1)
    kept_count = jnp.clip(ramp_value + jitter, 1, KMAX)
    kept_count = jnp.where(from_pole == NP - 1, KMAX, kept_count)
    kept_count = jnp.where(from_pole == 0, 1, kept_count)
    return kept_count.astype(jnp.int32)


def draw_slot_table(key, part):
    lat_devices = NLAT // LAT_DEV
    owners = 2 * NP // LAT_DEV
    split_keys = jax.random.split(jax.random.fold_in(key, 12), owners)
    row_ranks = jax.vmap(lambda one_key: jax.random.permutation(one_key, LAT_DEV))(split_keys)
    row_ranks = row_ranks.reshape(-1).astype(jnp.int32)
    owner_block = jnp.arange(2 * NP, dtype=jnp.int32) // LAT_DEV
    owner_device = jnp.where(owner_block < lat_devices // 4, owner_block, owner_block + lat_devices // 2)
    partner_device = (owner_device + lat_devices // 2) % lat_devices
    target_device = jnp.where(row_ranks < HELP, owner_device, partner_device)
    position = row_ranks % HELP
    return (target_device * HELP + position).astype(jnp.int32)


def levels(own_key, shape, cuts, least, top_value):
    gain, own = 1.0, jax.random.fold_in(own_key, 6)
    for dim, parts in cuts:
        draws = jnp.exp(jax.random.uniform(jax.random.fold_in(own, dim), (parts,), jnp.float32, least / len(cuts), top_value / len(cuts)))
        gain = gain * jnp.repeat(draws, shape[dim] // parts).reshape([-1 if axis == dim else 1 for axis in range(len(shape))])
    return gain


def normal_values(key, extent, scale, most, cuts=(), kind=jnp.bfloat16):
    values = scale * jax.random.normal(key, extent, jnp.float32)
    if cuts:
        values = values * levels(key, extent, cuts, -0.22, 0.18)
    return jnp.clip(values, -most, most).astype(kind)


def setup_inputs(seed: int = 0, part: int = 0) -> dict:
    streams_of = jax.random.split(jax.random.key(seed), 9)
    part_splits = jax.random.split(jax.random.fold_in(streams_of[8], part), 9)
    return {
        "wind_east": normal_values(part_splits[0], (LEVELS, NLAT, NLON), 1.0, 6.0, ((0, 2), (1, 4), (2, 2)), jnp.float32),
        "wind_north": normal_values(part_splits[1], (LEVELS, NLAT, NLON), 1.0, 6.0, ((0, 2), (1, 4), (2, 2)), jnp.float32),
        "thickness": normal_values(part_splits[2], (LEVELS, NLAT, NLON), 1.0, 6.0, ((0, 2), (1, 4), (2, 2)), jnp.float32),
        "geopot": normal_values(part_splits[3], (LEVELS, NLAT, NLON), 1.0, 6.0, ((0, 2), (1, 4), (2, 2)), jnp.float32),
        "surface_geopot": normal_values(streams_of[4], (NLAT, NLON), 1.0, 6.0, ((0, 4), (1, 2)), jnp.float32),
        "mean_depth": jnp.clip(jnp.exp(math.log(2.0) - 1.3862944 * jax.random.uniform(streams_of[5], (LEVELS,), jnp.float32) ** levels(streams_of[5], (LEVELS,), ((0, 2),), -0.2, 0.2)), 0.5, 2.0),
        "kept_modes": draw_kept_modes(jax.random.fold_in(streams_of[8], 71), part),
        "slot_table": draw_slot_table(jax.random.fold_in(streams_of[8], 71), part),
    }


STEP_FACTOR = 0.15
CORIOLIS = 0.2
GRAVITY = 0.25


def east_diff(stacked):
    return jnp.roll(stacked, -1, axis=-1) - jnp.roll(stacked, 1, axis=-1)


def north_diff(stacked):
    padded = jnp.pad(stacked, ((0, 0), (1, 1), (0, 0)))
    return padded[:, 2:, :] - padded[:, :-2, :]


def reference(wind_east, wind_north, thickness, geopot, surface_geopot, mean_depth, kept_modes, slot_table):
    lam_step = 2.0 * math.pi / NLON
    phi_step = math.pi / NLAT
    latitude = -0.5 * math.pi + (jnp.arange(NLAT, dtype=jnp.float32) + 0.5) * phi_step
    coslat = jnp.cos(latitude)[:, None]
    sinlat = jnp.sin(latitude)[:, None]
    east_coef = STEP_FACTOR / coslat
    north_coef = STEP_FACTOR * lam_step / phi_step
    east_new = wind_east - east_coef * east_diff(geopot) + CORIOLIS * sinlat * wind_north
    north_new = wind_north - north_coef * north_diff(geopot) - CORIOLIS * sinlat * wind_east
    polar_rows = jnp.concatenate([jnp.arange(NP), jnp.arange(NLAT - NP, NLAT)]).astype(jnp.int32)
    wind_pair = jnp.stack([east_new, north_new])
    polar_part = wind_pair[:, :, polar_rows, :]
    transform = jnp.fft.rfft(polar_part, axis=-1)[..., :KMAX]
    wavenumber = jnp.arange(KMAX)
    weight = jnp.where(wavenumber == 0, 1.0, 2.0) / NLON
    keep_mask = wavenumber[None, :] < kept_modes[:, None]
    factor = jnp.where(keep_mask, weight[None, :], 0.0)
    cos_part = jnp.real(transform) * factor
    sin_part = -jnp.imag(transform) * factor
    ordered = jnp.concatenate([cos_part, sin_part], axis=-1)
    spectra = jnp.zeros_like(ordered).at[:, :, slot_table, :].set(ordered)
    masked = jnp.where(keep_mask, transform, jnp.zeros_like(transform))
    masked = jnp.pad(masked, ((0, 0), (0, 0), (0, 0), (0, NLON // 2 + 1 - KMAX)))
    filtered = jnp.fft.irfft(masked, n=NLON, axis=-1)
    wind_pair = wind_pair.at[:, :, polar_rows, :].set(filtered)
    east_final = wind_pair[0]
    north_final = wind_pair[1]
    divergence = east_coef * east_diff(east_final) + (north_coef / coslat) * north_diff(north_final * coslat)
    thick_new = thickness - mean_depth[:, None, None] * divergence
    column = jnp.cumsum(thick_new[::-1], axis=0)[::-1]
    geo_new = surface_geopot[None] + GRAVITY * column
    return (east_final, north_final, thick_new, geo_new, spectra)
```

```python
import functools
import math

import jax
import jax.numpy as jnp
import numpy as np
from jax import lax
from jax.experimental import pallas as pl
from jax.experimental.pallas import tpu as pltpu
from jax.sharding import PartitionSpec as P

KMAX = 360
HALF = 384
WIDE = 2 * HALF

STEP_FACTOR = 0.15
CORIOLIS = 0.2
GRAVITY = 0.25

VMEM_BYTES = 40 * 1024 * 1024


def round_up(value, step):
    return -(-value // step) * step


class Sizes:
    def __init__(self, shape, counts):
        self.lev, self.lat, self.lon = shape
        self.n_lat, self.n_lon, self.n_lev = counts["lat"], counts["lon"], counts["lev"]
        self.nlat, self.nlon = self.lat * self.n_lat, self.lon * self.n_lon
        self.polar = self.nlat // 4
        self.help = self.lat // 2
        self.half_axis = self.n_lat // 2
        self.rim = self.lat + 2
        self.rows = round_up(self.lev * self.rim, 8)
        self.mm_rows = round_up(self.rows, 16)
        self.ext = round_up(self.lon + 4, 128)
        self.tile = next(t for t in (384, 256, 128) if self.ext % t == 0)
        self.tiles = self.ext // self.tile
        self.spec_width = 2 * KMAX // self.n_lon
        self.spec_rows = round_up(self.help, 8)


def basis_tables(z):
    lane = np.arange(z.ext)
    column = np.where(lane == z.ext - 1, -1, lane)
    used = (lane <= z.lon) | (lane == z.ext - 1)
    k = np.arange(KMAX)
    angle = (column[:, None] * k[None, :] % z.nlon) * (2.0 * np.pi / z.nlon)
    full = np.zeros((z.ext, WIDE))
    full[:, :KMAX] = np.cos(angle)
    full[:, HALF : HALF + KMAX] = np.sin(angle)
    full = np.where(used[:, None], full, 0.0).astype(np.float32)
    high = full.astype(jnp.bfloat16)
    low = (full - high.astype(np.float32)).astype(jnp.bfloat16)
    return high, low


def phase_table(z):
    k = np.arange(KMAX)
    table = np.zeros((z.n_lon, 8, HALF), np.float32)
    for place in range(z.n_lon):
        angle = (place * z.lon * k % z.nlon) * (2.0 * np.pi / z.nlon)
        table[place, 0, :KMAX] = np.cos(angle)
        table[place, 1, :KMAX] = np.sin(angle)
    return table


def row_table(z):
    lam_step = np.float32(2.0 * math.pi / z.nlon)
    phi_step = np.float32(math.pi / z.nlat)
    latitude = np.float32(-0.5 * math.pi) + (
        np.arange(z.nlat, dtype=np.float32) + np.float32(0.5)
    ) * phi_step
    cosine = np.cos(latitude.astype(np.float64)).astype(np.float32)
    sine = np.sin(latitude.astype(np.float64)).astype(np.float32)
    north_coef = np.float32(STEP_FACTOR) * lam_step / phi_step
    per_row = np.stack([np.float32(STEP_FACTOR) / cosine, sine, cosine, north_coef / cosine], axis=1)
    per_row = np.pad(per_row, ((1, 1), (0, 4)))
    table = np.zeros((z.n_lat, z.rows, 8), np.float32)
    for place in range(z.n_lat):
        block = per_row[place * z.lat : place * z.lat + z.rim]
        for level in range(z.lev):
            table[place, level * z.rim : (level + 1) * z.rim] = block
    return table


def split(x):
    high = x.astype(jnp.bfloat16)
    low = (x - high.astype(jnp.float32)).astype(jnp.bfloat16)
    return high, low


def mm(a, b):
    return jnp.dot(a, b, preferred_element_type=jnp.float32)


def product(both, high_basis, low_basis):
    rows = both.shape[0] // 2
    main = mm(both, high_basis)
    return main[:rows] + main[rows:] + mm(both[:rows], low_basis)


def roll(x, shift):
    return pltpu.roll(x, shift % x.shape[1], 1)


def east_diff(x):
    return roll(x, -1) - roll(x, 1)


def put_lane(x, at, column):
    lane = lax.broadcasted_iota(jnp.int32, x.shape, 1)
    return jnp.where(lane == at, column, x)


def forward_turn(payload, phase_ref, lon_index):
    cos, sin = phase_ref[lon_index, 0:1], phase_ref[lon_index, 1:2]
    a, b = payload[:, :HALF], payload[:, HALF:]
    return a * cos - b * sin, a * sin + b * cos


def polar_rows(z, lat_index, shape_rows):
    flat = lax.broadcasted_iota(jnp.int32, (shape_rows, 1), 0)
    level = jnp.zeros_like(flat)
    for one in range(1, z.lev):
        level = level + (flat >= one * z.rim).astype(jnp.int32)
    inner = flat - level * z.rim
    row = lat_index * z.lat + inner - 1
    south = (row >= 0) & (row < z.polar)
    north = (row >= z.nlat - z.polar) & (row < z.nlat)
    inside = flat < z.lev * z.rim
    polar = (south | north) & inside
    number = jnp.where(south, row, row - (z.nlat - 2 * z.polar))
    number = jnp.where(polar, number, -1)
    own = (inner >= 1) & (inner <= z.lat) & inside
    return polar, number, own, level


def look_up(number, table_ref):
    table = table_ref[...].astype(jnp.float32)
    lane = lax.broadcasted_iota(jnp.int32, (number.shape[0], table.shape[1]), 1)
    return jnp.sum(jnp.where(lane == number, table, 0.0), axis=1, keepdims=True)


def coefficients(z, sums, number, kept_ref):
    lane = lax.broadcasted_iota(jnp.int32, (1, WIDE), 1)
    k = jnp.where(lane < HALF, lane, lane - HALF)
    weight = jnp.where(k == 0, 1.0 / z.nlon, 2.0 / z.nlon).astype(jnp.float32)
    kept = look_up(number, kept_ref)
    keep = (k.astype(jnp.float32) < kept) & (k < KMAX)
    return jnp.where(keep, sums * weight, 0.0)


def store_spectra(z, coef, number, own, level, slot_ref, lat_index, lon_index, keep_ref, send_ref):
    rows = coef.shape[0]
    slot = look_up(number, slot_ref).astype(jnp.int32)
    partner = lax.rem(lat_index + z.half_axis, z.n_lat)
    usable = own & (number >= 0)
    mine = slot - lat_index * z.help
    theirs = slot - partner * z.help
    place = jnp.full_like(slot, -1)
    base = level * (2 * z.spec_rows)
    place = jnp.where(usable & (mine >= 0) & (mine < z.help), base + mine, place)
    place = jnp.where(
        usable & (theirs >= 0) & (theirs < z.help), base + z.spec_rows + theirs, place
    )
    places = round_up(z.lev * 2 * z.spec_rows, 128)
    lane = lax.broadcasted_iota(jnp.int32, (rows, places), 1)
    chosen = (lane == place).astype(jnp.float32)
    part = jnp.zeros((rows, z.spec_width), jnp.float32)
    for one in range(z.n_lon):
        first = one * z.spec_width
        first = first if first < KMAX else first - KMAX + HALF
        part = jnp.where(lon_index == one, coef[:, first : first + z.spec_width], part)
    ordered = lax.dot_general(
        chosen,
        part,
        (((0,), (0,)), ((), ())),
        precision=lax.Precision.HIGHEST,
        preferred_element_type=jnp.float32,
    )
    for lev in range(z.lev):
        at = lev * 2 * z.spec_rows
        keep_ref[lev] = ordered[at : at + z.help]
        send_ref[lev] = ordered[at + z.spec_rows : at + z.spec_rows + z.help]


def east_forward(
    z, we_ref, wn_ref, g_ref, row_ref, phase_ref, high_ref, low_ref,
    payload_ref, down_ref, up_ref, rows_ref, both_ref,
):
    lat_index, lon_index = lax.axis_index("lat"), lax.axis_index("lon")
    step = pl.program_id(0)
    last = z.lon - 1

    @pl.when(step == 0)
    def _():
        rows_ref[...] = jnp.zeros_like(rows_ref)
        for lev in range(z.lev):
            table = row_ref[lat_index, 1 : 1 + z.lat]
            pad = jnp.zeros((z.lat, z.ext - z.lon), jnp.float32)
            g = jnp.concatenate([g_ref[lev], pad], axis=1)
            we = jnp.concatenate([we_ref[lev], pad], axis=1)
            wn = jnp.concatenate([wn_ref[lev], pad], axis=1)
            new = we - table[:, 0:1] * east_diff(g) + CORIOLIS * table[:, 1:2] * wn
            rows_ref[pl.ds(lev * z.rim + 1, z.lat), :] = new
            for part, (source, row) in enumerate(
                ((g_ref, z.lat - 2), (g_ref, z.lat - 1), (we_ref, z.lat - 1), (wn_ref, z.lat - 1))
            ):
                down_ref[pl.ds(4 * lev + part, 1), :] = source[lev, pl.ds(row, 1), :]
            for part, (source, row) in enumerate(((g_ref, 0), (g_ref, 1), (we_ref, 0), (wn_ref, 0))):
                up_ref[pl.ds(4 * lev + part, 1), :] = source[lev, pl.ds(row, 1), :]
        high, low = split(rows_ref[...])
        both_ref[: z.mm_rows] = high
        both_ref[z.mm_rows :] = low

    tile = high_ref.shape[1]
    sums = product(both_ref[...], high_ref[...], low_ref[...])[: z.rows]
    for one in range(WIDE // tile):

        @pl.when(step == one)
        def _(one=one):
            payload_ref[:, one * tile : (one + 1) * tile] = sums

    @pl.when(step == WIDE // tile - 1)
    def _():
        a, b = forward_turn(payload_ref[...], phase_ref, lon_index)
        payload_ref[:, :HALF] = a
        payload_ref[:, HALF:] = b
        for lev in range(z.lev):
            at = pl.ds(lev * z.rim + 1, z.lat)
            spare = payload_ref[at, HALF - 128 : HALF]
            edges = (
                g_ref[lev, :, last - 1 : last],
                g_ref[lev, :, last : last + 1],
                we_ref[lev, :, last : last + 1],
                wn_ref[lev, :, last : last + 1],
                g_ref[lev, :, 0:1],
                g_ref[lev, :, 1:2],
                we_ref[lev, :, 0:1],
                wn_ref[lev, :, 0:1],
            )
            for n, edge in enumerate(edges):
                spare = put_lane(spare, KMAX - HALF + 128 + n, edge)
            payload_ref[at, HALF - 128 : HALF] = spare


def north_forward(
    z, we_ref, wn_ref, g_ref, above_ref, below_ref, row_ref, phase_ref, high_ref, low_ref,
    payload_ref, north_ref, g_rows, rows_ref, both_ref,
):
    lat_index, lon_index = lax.axis_index("lat"), lax.axis_index("lon")
    step = pl.program_id(0)

    @pl.when(step == 0)
    def _():
        rows_ref[...] = jnp.zeros_like(rows_ref)
        coef = STEP_FACTOR * (2.0 * math.pi / z.nlon) / (math.pi / z.nlat)
        for lev in range(z.lev):
            table = row_ref[lat_index]
            g_rows[pl.ds(8, z.lat), :] = g_ref[lev]
            g_rows[pl.ds(6, 2), :] = above_ref[pl.ds(4 * lev, 2), :]
            g_rows[pl.ds(8 + z.lat, 2), :] = below_ref[pl.ds(4 * lev, 2), :]
            for first, count, we, wn in (
                (0, 1, above_ref[pl.ds(4 * lev + 2, 1), :], above_ref[pl.ds(4 * lev + 3, 1), :]),
                (1, z.lat, we_ref[lev], wn_ref[lev]),
                (1 + z.lat, 1, below_ref[pl.ds(4 * lev + 2, 1), :], below_ref[pl.ds(4 * lev + 3, 1), :]),
            ):
                diff = g_rows[pl.ds(8 + first, count), :] - g_rows[pl.ds(6 + first, count), :]
                sine = table[first : first + count, 1:2]
                new = wn - coef * diff - CORIOLIS * sine * we
                rows_ref[pl.ds(lev * z.rim + first, count), : z.lon] = new
        north_ref[...] = rows_ref[: z.rows, : z.lon]
        high, low = split(rows_ref[...])
        both_ref[: z.mm_rows] = high
        both_ref[z.mm_rows :] = low

    tile = high_ref.shape[1]
    sums = product(both_ref[...], high_ref[...], low_ref[...])[: z.rows]
    for one in range(WIDE // tile):

        @pl.when(step == one)
        def _(one=one):
            payload_ref[:, one * tile : (one + 1) * tile] = sums

    @pl.when(step == WIDE // tile - 1)
    def _():
        a, b = forward_turn(payload_ref[...], phase_ref, lon_index)
        payload_ref[:, :HALF] = a
        payload_ref[:, HALF:] = b


def prepare_coefficients(
    z, own_ref, arrived, kept_ref, slot_ref, phase_ref, keep_ref, send_ref, both_ref, lat_index, lon_index
):
    sums = own_ref[...]
    for one in arrived:
        sums = sums + one[...]
    polar, number, own, level = polar_rows(z, lat_index, z.rows)
    coef = coefficients(z, sums, number, kept_ref)
    store_spectra(z, coef, number, own, level, slot_ref, lat_index, lon_index, keep_ref, send_ref)
    cos, sin = phase_ref[lon_index, 0:1], phase_ref[lon_index, 1:2]
    a, b = coef[:, :HALF], coef[:, HALF:]
    local = jnp.concatenate([a * cos + b * sin, b * cos - a * sin], axis=1)
    local = jnp.concatenate(
        [local, jnp.zeros((z.mm_rows - z.rows, WIDE), jnp.float32)], axis=0
    )
    high, low = split(local)
    both_ref[: z.mm_rows] = high
    both_ref[z.mm_rows :] = low


def east_inverse(
    z, depth_ref, we_ref, wn_ref, g_ref, thick_ref, row_ref, phase_ref, kept_ref, slot_ref, own_ref, *rest
):
    arrived, rest = rest[: z.n_lon - 1], rest[z.n_lon - 1 :]
    high_ref, low_ref, final_ref, part_ref, keep_ref, send_ref, both_ref, filtered_ref = rest
    lat_index, lon_index = lax.axis_index("lat"), lax.axis_index("lon")
    step = pl.program_id(0)

    @pl.when(step == 0)
    def _():
        prepare_coefficients(
            z, own_ref, arrived, kept_ref, slot_ref, phase_ref, keep_ref, send_ref, both_ref,
            lat_index, lon_index,
        )

    rows = product(both_ref[...], high_ref[...], low_ref[...])[: z.rows]
    for one in range(z.tiles):

        @pl.when(step == one)
        def _(one=one):
            filtered_ref[:, one * z.tile : (one + 1) * z.tile] = rows

    @pl.when(step == z.tiles - 1)
    def _():
        from_left, from_right = arrived[0], arrived[-1]
        polar_all = polar_rows(z, lat_index, z.rows)[0].astype(jnp.float32)
        del polar_all
        row = lat_index * z.lat + lax.broadcasted_iota(jnp.int32, (z.lat, 1), 0)
        polar = (row < z.polar) | (row >= z.nlat - z.polar)
        for lev in range(z.lev):
            at = pl.ds(lev * z.rim + 1, z.lat)
            table = row_ref[lat_index, 1 : 1 + z.lat]
            left = from_left[at, HALF - 128 : HALF]
            right = from_right[at, HALF - 128 : HALF]
            first = KMAX - HALF + 128
            pad = jnp.zeros((z.lat, z.ext - z.lon), jnp.float32)

            def widened(ref, left_of, right_of):
                x = jnp.concatenate([ref[lev], pad], axis=1)
                tail = x[:, z.ext - 128 :]
                at_right = z.lon - (z.ext - 128)
                for n, lane in enumerate(right_of):
                    tail = put_lane(tail, at_right + n, right[:, first + lane : first + lane + 1])
                for n, lane in enumerate(left_of):
                    tail = put_lane(tail, 127 - n, left[:, first + lane : first + lane + 1])
                return jnp.concatenate([x[:, : z.ext - 128], tail], axis=1)

            g = widened(g_ref, (1, 0), (4, 5))
            we = widened(we_ref, (2,), (6,))
            wn = widened(wn_ref, (3,), (7,))
            new = we - table[:, 0:1] * east_diff(g) + CORIOLIS * table[:, 1:2] * wn
            final = jnp.where(polar, filtered_ref[at, :], new)
            final_ref[lev] = final[:, : z.lon]
            change = depth_ref[lev] * (table[:, 0:1] * east_diff(final)[:, : z.lon])
            part_ref[lev] = thick_ref[lev] - change


def north_inverse(
    z, depth_ref, north_ref, part_ref, surface_ref, row_ref, phase_ref, kept_ref, slot_ref, own_ref, *rest
):
    arrived, rest = rest[: z.n_lon - 1], rest[z.n_lon - 1 :]
    (
        high_ref, low_ref, final_ref, thick_ref, geo_ref, column_ref, keep_ref, send_ref,
        both_ref, rows_ref,
    ) = rest
    lat_index, lon_index = lax.axis_index("lat"), lax.axis_index("lon")

    @pl.when(pl.program_id(0) == 0)
    def _():
        prepare_coefficients(
            z, own_ref, arrived, kept_ref, slot_ref, phase_ref, keep_ref, send_ref, both_ref,
            lat_index, lon_index,
        )

    filtered = product(both_ref[...], high_ref[...], low_ref[...])[: z.rows]
    polar = polar_rows(z, lat_index, z.rows)[0]
    rows_ref[...] = jnp.where(polar, filtered, north_ref[...])
    for lev in range(z.lev):
        final_ref[lev] = rows_ref[pl.ds(lev * z.rim + 1, z.lat), :]
    rows_ref[...] = rows_ref[...] * row_ref[lat_index, :, 2:3]
    column = None
    for lev in reversed(range(z.lev)):
        diff = (
            rows_ref[pl.ds(lev * z.rim + 2, z.lat), :] - rows_ref[pl.ds(lev * z.rim, z.lat), :]
        )
        scale = row_ref[lat_index, 1 : 1 + z.lat, 3:4]
        thick = part_ref[lev] - depth_ref[lev] * (scale * diff)
        thick_ref[lev] = thick
        column = thick if column is None else column + thick
        geo_ref[lev] = surface_ref[...] + GRAVITY * column
    column_ref[...] = column


def whole(shape):
    return pl.BlockSpec(shape, lambda i: (0,) * len(shape))


def call(kernel, grid, in_specs, out_specs, out_shape, scratch, cost):
    return pl.pallas_call(
        kernel,
        grid=(grid,),
        in_specs=in_specs,
        out_specs=out_specs,
        out_shape=[jax.ShapeDtypeStruct(s, jnp.float32) for s in out_shape],
        scratch_shapes=scratch,
        compiler_params=pltpu.CompilerParams(vmem_limit_bytes=VMEM_BYTES),
        cost_estimate=pl.CostEstimate(flops=cost[0], bytes_accessed=cost[1], transcendentals=0),
    )


def shifted(block, axis, distance):
    count = lax.axis_size(axis)
    return lax.ppermute(block, axis, [(i, (i + distance) % count) for i in range(count)])


def local(
    wind_east, wind_north, thickness, geopot, surface_geopot, mean_depth, kept_modes, slot_table
):
    z = Sizes(thickness.shape, {axis: lax.axis_size(axis) for axis in ("lat", "lon", "lev")})
    lat_index = lax.axis_index("lat")
    field = (z.lev, z.lat, z.lon)
    high, low = basis_tables(z)
    forward = (jnp.asarray(high), jnp.asarray(low))
    inverse = (jnp.asarray(np.ascontiguousarray(high.T)), jnp.asarray(np.ascontiguousarray(low.T)))
    phase = jnp.asarray(phase_table(z))
    per_row = jnp.asarray(row_table(z))
    kept = kept_modes[None, :]
    slots = slot_table[None, :]
    payload = (z.rows, WIDE)
    rims = (4 * z.lev, z.lon)
    spec = (z.lev, z.help, z.spec_width)
    tile = 256
    forward_specs = [pl.BlockSpec((z.ext, tile), lambda i: (0, i))] * 2
    inverse_specs = [pl.BlockSpec((WIDE, z.tile), lambda i: (0, i))] * 2
    smem = pl.BlockSpec(memory_space=pltpu.SMEM)
    flops = 6 * z.mm_rows * z.ext * WIDE
    basis_bytes = 4 * z.ext * WIDE
    both_columns = pltpu.VMEM((2 * z.mm_rows, z.ext), jnp.bfloat16)
    both_waves = pltpu.VMEM((2 * z.mm_rows, WIDE), jnp.bfloat16)

    east_share, to_below, to_above = call(
        functools.partial(east_forward, z),
        WIDE // tile,
        [whole(field)] * 3 + [whole(per_row.shape), whole(phase.shape)] + forward_specs,
        [whole(payload), whole(rims), whole(rims)],
        [payload, rims, rims],
        [pltpu.VMEM((z.mm_rows, z.ext), jnp.float32), both_columns],
        (flops, basis_bytes + 4 * 4 * math.prod(field)),
    )(wind_east, wind_north, geopot, per_row, phase, *forward)
    east_others = [shifted(east_share, "lon", s) for s in range(1, z.n_lon)]
    from_above = lax.ppermute(to_below, "lat", [(i, i + 1) for i in range(z.n_lat - 1)])
    from_below = lax.ppermute(to_above, "lat", [(i + 1, i) for i in range(z.n_lat - 1)])

    north_share, north_new = call(
        functools.partial(north_forward, z),
        WIDE // tile,
        [whole(field)] * 3
        + [whole(rims)] * 2
        + [whole(per_row.shape), whole(phase.shape)]
        + forward_specs,
        [whole(payload), whole((z.rows, z.lon))],
        [payload, (z.rows, z.lon)],
        [
            pltpu.VMEM((round_up(z.lat + 16, 8), z.lon), jnp.float32),
            pltpu.VMEM((z.mm_rows, z.ext), jnp.float32),
            both_columns,
        ],
        (flops, basis_bytes + 4 * 4 * math.prod(field)),
    )(wind_east, wind_north, geopot, from_above, from_below, per_row, phase, *forward)
    north_others = [shifted(north_share, "lon", s) for s in range(1, z.n_lon)]

    small = [whole(per_row.shape), whole(phase.shape), whole(kept.shape), whole(slots.shape)]
    shares = [whole(payload)] * z.n_lon
    east_final, thick_part, east_keep, east_send = call(
        functools.partial(east_inverse, z),
        z.tiles,
        [smem] + [whole(field)] * 4 + small + shares + inverse_specs,
        [whole(field), whole(field), whole(spec), whole(spec)],
        [field, field, spec, spec],
        [both_waves, pltpu.VMEM((z.rows, z.ext), jnp.float32)],
        (flops, basis_bytes + 4 * 7 * math.prod(field)),
    )(
        mean_depth, wind_east, wind_north, geopot, thickness, per_row, phase, kept, slots,
        east_share, *east_others, *inverse,
    )

    polar_devices = [
        i for i in range(z.n_lat) if i < z.n_lat // 4 or i >= z.n_lat - z.n_lat // 4
    ]
    to_helper = [(i, (i + z.half_axis) % z.n_lat) for i in polar_devices]
    east_arrived = lax.ppermute(east_send, "lat", to_helper)

    columns = pl.BlockSpec((z.lev, z.lat, z.tile), lambda i: (0, 0, i))
    flat = pl.BlockSpec((z.lat, z.tile), lambda i: (0, i))
    north_final, thick_new, geo_base, column, north_keep, north_send = call(
        functools.partial(north_inverse, z),
        z.tiles,
        [smem, pl.BlockSpec((z.rows, z.tile), lambda i: (0, i)), columns, flat]
        + small
        + shares
        + inverse_specs,
        [columns, columns, columns, flat, whole(spec), whole(spec)],
        [field, field, field, field[1:], spec, spec],
        [both_waves, pltpu.VMEM((z.rows, z.tile), jnp.float32)],
        (flops, basis_bytes + 4 * 6 * math.prod(field)),
    )(
        mean_depth, north_new, thick_part, surface_geopot, per_row, phase, kept, slots,
        north_share, *north_others, *inverse,
    )
    north_arrived = lax.ppermute(north_send, "lat", to_helper)

    geo_new = geo_base
    for distance in range(1, z.n_lev):
        deeper = lax.ppermute(
            column, "lev", [(i, i - distance) for i in range(distance, z.n_lev)]
        )
        geo_new = geo_new + GRAVITY * deeper[None]
    is_polar = (lat_index < z.n_lat // 4) | (lat_index >= z.n_lat - z.n_lat // 4)
    spectra = jnp.stack(
        [
            jnp.where(is_polar, east_keep, east_arrived),
            jnp.where(is_polar, north_keep, north_arrived),
        ]
    )
    return (east_final, north_final, thick_new, geo_new, spectra)


def solution(mesh):
    field = P(("members", "lev"), "lat", "lon")
    return jax.shard_map(
        local,
        mesh=mesh,
        in_specs=(field, field, field, field, P("lat", "lon"), P("lev"), P(), P()),
        out_specs=(field, field, field, field, P(None, ("members", "lev"), "lat", "lon")),
        check_vma=False,
    )
```

```python
import functools
import math

import jax
import jax.numpy as jnp
import numpy as np
from jax import lax
from jax.experimental import pallas as pl
from jax.experimental.pallas import tpu as pltpu
from jax.sharding import PartitionSpec as P

KMAX = 360
HALF = 384
WIDE = 2 * HALF
SPARE = HALF - 128
BLOCK = 256

STEP_FACTOR = 0.15
CORIOLIS = 0.2
GRAVITY = 0.25

MIB = 1024 * 1024

EAST_COEF, SINE, COSINE, NORTH_COEF, LEVEL, POLAR, NUMBER, OWN = range(8)


def round_up(value, step):
    return -(-value // step) * step


class Sizes:
    def __init__(self, shape, counts):
        self.lev, self.lat, self.lon = shape
        self.n_lat, self.n_lon, self.n_lev = counts["lat"], counts["lon"], counts["lev"]
        self.nlat, self.nlon = self.lat * self.n_lat, self.lon * self.n_lon
        self.polar = self.nlat // 4
        self.help = self.lat // 2
        self.half_axis = self.n_lat // 2
        self.own = self.lat * self.lev
        self.rows = self.own + 2 * self.lev
        assert self.rows % 8 == 0
        self.mm_rows = round_up(self.rows, 16)
        self.ext = round_up(self.lon + 4, BLOCK)
        self.blocks = self.ext // BLOCK
        self.spec_width = 2 * KMAX // self.n_lon
        self.spec_rows = round_up(self.help * self.lev, 8)


def high_low(x):
    x = x.astype(np.float32)
    high = x.astype(jnp.bfloat16)
    return high, (x - high.astype(np.float32)).astype(jnp.bfloat16)


def basis_tables(z):
    k = np.arange(KMAX)
    angle = (np.arange(BLOCK)[:, None] * k[None, :] % z.nlon) * (2.0 * np.pi / z.nlon)
    full = np.zeros((BLOCK, WIDE))
    full[:, :KMAX] = np.cos(angle)
    full[:, HALF : HALF + KMAX] = np.sin(angle)
    high, low = high_low(full)
    forward = np.concatenate([high, high, low], axis=0)
    inverse = np.concatenate([high.T, high.T, low.T], axis=0)
    return forward, inverse


def phase_table(z):
    k = np.arange(KMAX)
    table = np.zeros((z.n_lon, round_up(2 * z.blocks + 2, 8), HALF), np.float32)
    for place in range(z.n_lon):
        for n, column in enumerate([*range(0, z.ext, BLOCK), -1]):
            angle = ((place * z.lon + column) * k % z.nlon) * (2.0 * np.pi / z.nlon)
            table[place, 2 * n, :KMAX] = np.cos(angle)
            table[place, 2 * n + 1, :KMAX] = np.sin(angle)
    return table


def row_table(z):
    lam_step = np.float32(2.0 * math.pi / z.nlon)
    phi_step = np.float32(math.pi / z.nlat)
    latitude = np.float32(-0.5 * math.pi) + (
        np.arange(z.nlat, dtype=np.float32) + np.float32(0.5)
    ) * phi_step
    cosine = np.cos(latitude.astype(np.float64)).astype(np.float32)
    sine = np.sin(latitude.astype(np.float64)).astype(np.float32)
    north_coef = np.float32(STEP_FACTOR) * lam_step / phi_step
    table = np.zeros((z.n_lat, z.rows, 8), np.float32)
    for place in range(z.n_lat):
        for flat in range(z.rows):
            inner, level = flat // z.lev, flat % z.lev
            inner = -1 if inner == z.lat + 1 else inner
            row = place * z.lat + inner
            one = table[place, flat]
            one[LEVEL], one[NUMBER] = level, -1
            one[OWN] = 0 <= inner < z.lat
            if 0 <= row < z.nlat:
                one[EAST_COEF] = np.float32(STEP_FACTOR) / cosine[row]
                one[SINE], one[COSINE] = sine[row], cosine[row]
                one[NORTH_COEF] = north_coef / cosine[row]
                if row < z.polar:
                    one[POLAR], one[NUMBER] = 1, row
                elif row >= z.nlat - z.polar:
                    one[POLAR], one[NUMBER] = 1, row - (z.nlat - 2 * z.polar)
    return table


def store_split(lhs_ref, first_row, x):
    rows, width = x.shape
    high = x.astype(jnp.bfloat16)
    low = (x - high.astype(jnp.float32)).astype(jnp.bfloat16)
    at = slice(first_row, first_row + rows)
    lhs_ref[at, :width] = high
    lhs_ref[at, width : 2 * width] = low
    lhs_ref[at, 2 * width :] = high


def pad_rows(x, rows):
    return jnp.concatenate([x, jnp.zeros((rows - x.shape[0], x.shape[1]), x.dtype)], axis=0)


def phase_of(phase_ref, n):
    lon_index = lax.axis_index("lon")
    return phase_ref[lon_index, 2 * n : 2 * n + 1], phase_ref[lon_index, 2 * n + 1 : 2 * n + 2]


def forward_sums(z, x, basis_ref, phase_ref, lhs_ref, payload_ref):
    for block in range(z.blocks):
        part = pad_rows(x[:, block * BLOCK : (block + 1) * BLOCK], z.mm_rows)
        store_split(lhs_ref, block * z.mm_rows, part)
    sums = jnp.dot(lhs_ref[...], basis_ref[...], preferred_element_type=jnp.float32)
    real = imag = None
    for block in range(z.blocks):
        cos, sin = phase_of(phase_ref, block)
        part = sums[block * z.mm_rows : block * z.mm_rows + z.rows]
        a, b = part[:, :HALF], part[:, HALF:]
        more_real, more_imag = a * cos - b * sin, a * sin + b * cos
        real = more_real if real is None else real + more_real
        imag = more_imag if imag is None else imag + more_imag
    payload_ref[:, :HALF] = real
    payload_ref[:, HALF:] = imag


def inverse_blocks(z, coef, basis_ref, phase_ref, lhs_ref):
    a, b = coef[:, :HALF], coef[:, HALF:]
    for block in range(z.blocks):
        cos, sin = phase_of(phase_ref, block)
        turned = jnp.concatenate([a * cos + b * sin, b * cos - a * sin], axis=1)
        store_split(lhs_ref, block * z.mm_rows, pad_rows(turned, z.mm_rows))
    rows = jnp.dot(lhs_ref[...], basis_ref[...], preferred_element_type=jnp.float32)
    cos, sin = phase_of(phase_ref, z.blocks)
    before = jnp.sum(a * cos + b * sin, axis=1, keepdims=True)
    return [rows[n * z.mm_rows : n * z.mm_rows + z.rows] for n in range(z.blocks)], before


def roll(x, shift, axis):
    return pltpu.roll(x, shift % x.shape[axis], axis)


def east_diff(x):
    return roll(x, -1, 1) - roll(x, 1, 1)


def flat_rows(z, ref):
    return ref[...].reshape(z.own, ref.shape[2])


def widen(z, x):
    return jnp.concatenate([x, jnp.zeros((x.shape[0], z.ext - x.shape[1]), x.dtype)], axis=1)


def put_lane(x, at, column):
    lane = lax.broadcasted_iota(jnp.int32, x.shape, 1)
    return jnp.where(lane == at, column, x)


def column_of(row_ref, which):
    return row_ref[lax.axis_index("lat"), :, which : which + 1]


def look_up(number, table_ref):
    table = table_ref[...].astype(jnp.float32)
    lane = lax.broadcasted_iota(jnp.int32, (number.shape[0], table.shape[1]), 1)
    return jnp.sum(jnp.where(lane == number, table, 0.0), axis=1, keepdims=True)


def add_shares(refs):
    total = refs[0][...]
    for ref in refs[1:]:
        total = total + ref[...]
    return total


def coefficients(z, sums, number, kept_ref):
    lane = lax.broadcasted_iota(jnp.int32, (1, WIDE), 1)
    k = jnp.where(lane < HALF, lane, lane - HALF)
    weight = jnp.where(k == 0, 1.0 / z.nlon, 2.0 / z.nlon).astype(jnp.float32)
    keep = (k.astype(jnp.float32) < look_up(number, kept_ref)) & (k < KMAX)
    return jnp.where(keep, sums * weight, 0.0)


def store_spectra(z, coef, number, row_ref, slot_ref, keep_ref, send_ref):
    lat_index, lon_index = lax.axis_index("lat"), lax.axis_index("lon")
    slot = look_up(number, slot_ref).astype(jnp.int32)
    level = column_of(row_ref, LEVEL).astype(jnp.int32)
    usable = (column_of(row_ref, OWN) > 0.0) & (number >= 0)
    mine = slot - lat_index * z.help
    theirs = slot - lax.rem(lat_index + z.half_axis, z.n_lat) * z.help
    place = jnp.full_like(slot, -1)
    place = jnp.where(usable & (mine >= 0) & (mine < z.help), mine * z.lev + level, place)
    place = jnp.where(
        usable & (theirs >= 0) & (theirs < z.help), z.spec_rows + theirs * z.lev + level, place
    )
    lane = lax.broadcasted_iota(jnp.int32, (z.rows, round_up(2 * z.spec_rows, 128)), 1)
    chosen = (lane == place).astype(jnp.float32)
    part = jnp.zeros((z.rows, z.spec_width), jnp.float32)
    for one in range(z.n_lon):
        first = one * z.spec_width
        first = first if first < KMAX else first - KMAX + HALF
        part = jnp.where(lon_index == one, coef[:, first : first + z.spec_width], part)
    ordered = lax.dot_general(
        chosen,
        part,
        (((0,), (0,)), ((), ())),
        precision=lax.Precision.HIGHEST,
        preferred_element_type=jnp.float32,
    )
    count = z.help * z.lev
    keep_ref[...] = ordered[:count].reshape(keep_ref.shape)
    send_ref[...] = ordered[z.spec_rows : z.spec_rows + count].reshape(send_ref.shape)


def filter_coefficients(z, share_refs, row_ref, kept_ref, slot_ref, keep_ref, send_ref):
    number = column_of(row_ref, NUMBER).astype(jnp.int32)
    coef = coefficients(z, add_shares(share_refs), number, kept_ref)
    store_spectra(z, coef, number, row_ref, slot_ref, keep_ref, send_ref)
    return coef


def depths(z, depth_ref, row_ref):
    level = column_of(row_ref, LEVEL)[: z.own]
    depth = jnp.zeros_like(level)
    for lev in range(z.lev):
        depth = jnp.where(level == lev, depth_ref[lev], depth)
    return depth


def east_forward(
    z, we_hbm, wn_hbm, g_hbm, row_ref, phase_ref, basis_ref,
    payload_ref, down_ref, up_ref, we_ref, wn_ref, g_ref, lhs_ref, sems,
):
    last = z.lon - 1
    edge = 2 * z.lev
    copies = [
        pltpu.make_async_copy(source, target, sems.at[n])
        for n, (source, target) in enumerate(((g_hbm, g_ref), (we_hbm, we_ref), (wn_hbm, wn_ref)))
    ]
    for copy in copies:
        copy.start()
    for copy in copies:
        copy.wait()
    g, we, wn = flat_rows(z, g_ref), flat_rows(z, we_ref), flat_rows(z, wn_ref)
    coef, sine = column_of(row_ref, EAST_COEF)[: z.own], column_of(row_ref, SINE)[: z.own]
    new = widen(z, we + CORIOLIS * sine * wn) - coef * east_diff(widen(z, g))
    tail = put_lane(new[:, z.ext - 128 :], 127, 0.0)
    new = jnp.concatenate([new[:, : z.ext - 128], tail], axis=1)
    forward_sums(z, pad_rows(new, z.rows), basis_ref, phase_ref, lhs_ref, payload_ref)
    cos, sin = phase_of(phase_ref, z.blocks)
    before = -coef * g[:, 0:1]
    payload_ref[: z.own, :HALF] += before * cos
    payload_ref[: z.own, HALF:] += before * sin
    spare = payload_ref[: z.own, SPARE:HALF]
    edges = ((g, last - 1), (g, last), (we, last), (wn, last), (g, 0), (g, 1), (we, 0), (wn, 0))
    for n, (x, column) in enumerate(edges):
        spare = put_lane(spare, KMAX - SPARE + n, x[:, column : column + 1])
    payload_ref[: z.own, SPARE:HALF] = spare
    down_ref[:edge] = g[z.own - edge :]
    down_ref[edge : edge + z.lev] = we[z.own - z.lev :]
    down_ref[edge + z.lev :] = wn[z.own - z.lev :]
    up_ref[:edge] = g[:edge]
    up_ref[edge : edge + z.lev] = we[: z.lev]
    up_ref[edge + z.lev :] = wn[: z.lev]


def north_forward(
    z, we_ref, wn_ref, g_ref, above_ref, below_ref, row_ref, phase_ref, basis_ref,
    payload_ref, north_ref, g_rows, lhs_ref,
):
    edge = 2 * z.lev
    coef = STEP_FACTOR * (2.0 * math.pi / z.nlon) / (math.pi / z.nlat)
    sine = column_of(row_ref, SINE)
    g = flat_rows(z, g_ref)
    g_rows[: z.own] = g
    g_rows[z.own : z.own + z.lev] = below_ref[: z.lev]
    g_rows[z.own + z.lev :] = above_ref[z.lev : edge]
    whole_g = g_rows[...]
    diff = roll(whole_g, -z.lev, 0) - roll(whole_g, z.lev, 0)
    north_ref[: z.own] = (
        flat_rows(z, wn_ref) - coef * diff[: z.own] - CORIOLIS * sine[: z.own] * flat_rows(z, we_ref)
    )
    for at, diff, ref in (
        (z.own, below_ref[z.lev : edge] - g[z.own - z.lev :], below_ref),
        (z.own + z.lev, g[: z.lev] - above_ref[: z.lev], above_ref),
    ):
        we, wn = ref[edge : edge + z.lev], ref[edge + z.lev :]
        north_ref[at : at + z.lev] = wn - coef * diff - CORIOLIS * sine[at : at + z.lev] * we
    forward_sums(z, widen(z, north_ref[...]), basis_ref, phase_ref, lhs_ref, payload_ref)


def east_inverse(
    z, depth_ref, we_ref, wn_ref, g_ref, thick_ref, row_ref, phase_ref, kept_ref, slot_ref, *rest
):
    shares, rest = rest[: z.n_lon], rest[z.n_lon :]
    basis_ref, final_ref, part_ref, keep_ref, send_ref, lhs_ref = rest
    coef = filter_coefficients(z, shares, row_ref, kept_ref, slot_ref, keep_ref, send_ref)
    blocks, before = inverse_blocks(z, coef, basis_ref, phase_ref, lhs_ref)
    filtered = jnp.concatenate(blocks, axis=1)[: z.own]
    tail = put_lane(filtered[:, z.ext - 128 :], 127, before[: z.own])
    filtered = jnp.concatenate([filtered[:, : z.ext - 128], tail], axis=1)

    first = KMAX - SPARE
    left, right = shares[1][: z.own, SPARE:HALF], shares[-1][: z.own, SPARE:HALF]
    at_right = z.lon - (z.ext - 128)

    def rimmed(ref, left_of, right_of):
        x = widen(z, flat_rows(z, ref))
        tail = x[:, z.ext - 128 :]
        for n, lane in enumerate(right_of):
            tail = put_lane(tail, at_right + n, right[:, first + lane : first + lane + 1])
        for n, lane in enumerate(left_of):
            tail = put_lane(tail, 127 - n, left[:, first + lane : first + lane + 1])
        return jnp.concatenate([x[:, : z.ext - 128], tail], axis=1)

    g = rimmed(g_ref, (1, 0), (4, 5))
    we, wn = rimmed(we_ref, (2,), (6,)), rimmed(wn_ref, (3,), (7,))
    coef, sine = column_of(row_ref, EAST_COEF)[: z.own], column_of(row_ref, SINE)[: z.own]
    new = we - coef * east_diff(g) + CORIOLIS * sine * wn
    final = jnp.where(column_of(row_ref, POLAR)[: z.own] > 0.0, filtered, new)
    final_ref[...] = final[:, : z.lon].reshape(final_ref.shape)
    change = depths(z, depth_ref, row_ref) * coef * east_diff(final)[:, : z.lon]
    part_ref[...] = flat_rows(z, thick_ref) - change


def north_inverse(
    z, depth_ref, north_ref, part_ref, surface_ref, row_ref, phase_ref, kept_ref, slot_ref, *rest
):
    shares, rest = rest[: z.n_lon], rest[z.n_lon :]
    basis_ref, final_ref, thick_ref, geo_ref, column_ref, keep_ref, send_ref, lhs_ref = rest
    coef = filter_coefficients(z, shares, row_ref, kept_ref, slot_ref, keep_ref, send_ref)
    blocks, _ = inverse_blocks(z, coef, basis_ref, phase_ref, lhs_ref)
    scale = depths(z, depth_ref, row_ref) * column_of(row_ref, NORTH_COEF)[: z.own]
    for block, filtered in enumerate(blocks):
        at = slice(block * BLOCK, min((block + 1) * BLOCK, z.lon))
        filtered = filtered[:, : at.stop - at.start]
        final = jnp.where(column_of(row_ref, POLAR) > 0.0, filtered, north_ref[:, at])
        final_ref[:, :, at] = final[: z.own].reshape(z.lat, z.lev, at.stop - at.start)
        scaled = final * column_of(row_ref, COSINE)
        diff = (roll(scaled, -z.lev, 0) - roll(scaled, z.lev, 0))[: z.own]
        thick = part_ref[:, at] - scale * diff
        thick_ref[:, :, at] = thick.reshape(z.lat, z.lev, at.stop - at.start)
    column = None
    for lev in reversed(range(z.lev)):
        one = thick_ref[:, lev, :]
        column = one if column is None else column + one
        geo_ref[:, lev, :] = surface_ref[...] + GRAVITY * column
    column_ref[...] = column


def call(kernel, n_in, out_shape, scratch, spaces=None, vmem=24):
    vmem_spec = pl.BlockSpec(memory_space=pltpu.VMEM)
    spaces = spaces or {}
    return pl.pallas_call(
        kernel,
        in_specs=[
            pl.BlockSpec(memory_space=spaces[n]) if n in spaces else vmem_spec for n in range(n_in)
        ],
        out_specs=[vmem_spec] * len(out_shape),
        out_shape=[jax.ShapeDtypeStruct(s, jnp.float32) for s in out_shape],
        scratch_shapes=scratch,
        compiler_params=pltpu.CompilerParams(vmem_limit_bytes=vmem * MIB),
        cost_estimate=pl.CostEstimate(flops=1, bytes_accessed=1, transcendentals=0),
    )


def shifted(block, axis, distance):
    count = lax.axis_size(axis)
    return lax.ppermute(block, axis, [(i, (i + distance) % count) for i in range(count)])


def level_inside(x):
    return jnp.swapaxes(x, -3, -2)


def local(
    wind_east, wind_north, thickness, geopot, surface_geopot, mean_depth, kept_modes, slot_table
):
    z = Sizes(thickness.shape, {axis: lax.axis_size(axis) for axis in ("lat", "lon", "lev")})
    lat_index = lax.axis_index("lat")
    wind_east, wind_north, thickness, geopot = (
        level_inside(x) for x in (wind_east, wind_north, thickness, geopot)
    )
    field = (z.lat, z.lev, z.lon)
    forward, inverse = (jnp.asarray(x) for x in basis_tables(z))
    phase = jnp.asarray(phase_table(z))
    per_row = jnp.asarray(row_table(z))
    kept = kept_modes[None, :]
    slots = slot_table[None, :]
    payload = (z.rows, WIDE)
    rims = (4 * z.lev, z.lon)
    spec = (z.help, z.lev, z.spec_width)
    columns_lhs = pltpu.VMEM((z.blocks * z.mm_rows, 3 * BLOCK), jnp.bfloat16)
    waves_lhs = pltpu.VMEM((z.blocks * z.mm_rows, 3 * WIDE), jnp.bfloat16)

    east_share, to_below, to_above = call(
        functools.partial(east_forward, z),
        6,
        [payload, rims, rims],
        [pltpu.VMEM(field, jnp.float32)] * 3 + [columns_lhs, pltpu.SemaphoreType.DMA((3,))],
        {n: pltpu.HBM for n in range(3)},
    )(wind_east, wind_north, geopot, per_row, phase, forward)
    east_others = [shifted(east_share, "lon", s) for s in range(1, z.n_lon)]

    odd = lat_index % 2 == 1
    met = []
    for start in range(2):
        pairs = [(i, i + 1) for i in range(start, z.n_lat - 1, 2)]
        rim = jnp.where(odd == (start == 1), to_below, to_above)
        met.append(lax.ppermute(rim, "lat", pairs + [(b, a) for a, b in pairs]))
    from_above, from_below = jnp.where(odd, met[0], met[1]), jnp.where(odd, met[1], met[0])

    north_share, north_new = call(
        functools.partial(north_forward, z),
        8,
        [payload, (z.rows, z.lon)],
        [pltpu.VMEM((z.rows, z.lon), jnp.float32), columns_lhs],
    )(wind_east, wind_north, geopot, from_above, from_below, per_row, phase, forward)
    north_others = [shifted(north_share, "lon", s) for s in range(1, z.n_lon)]

    east_final, thick_part, east_keep, east_send = call(
        functools.partial(east_inverse, z),
        10 + z.n_lon,
        [field, (z.own, z.lon), spec, spec],
        [waves_lhs],
        {0: pltpu.SMEM},
    )(
        mean_depth, wind_east, wind_north, geopot, thickness, per_row, phase, kept, slots,
        east_share, *east_others, inverse,
    )

    polar_devices = [
        i for i in range(z.n_lat) if i < z.n_lat // 4 or i >= z.n_lat - z.n_lat // 4
    ]
    to_helper = [(i, (i + z.half_axis) % z.n_lat) for i in polar_devices]
    east_arrived = lax.ppermute(east_send, "lat", to_helper)

    north_final, thick_new, geo_base, column, north_keep, north_send = call(
        functools.partial(north_inverse, z),
        9 + z.n_lon,
        [field, field, field, (z.lat, z.lon), spec, spec],
        [waves_lhs],
        {0: pltpu.SMEM},
    )(
        mean_depth, north_new, thick_part, surface_geopot, per_row, phase, kept, slots,
        north_share, *north_others, inverse,
    )
    north_arrived = lax.ppermute(north_send, "lat", to_helper)

    geo_new = geo_base
    for distance in range(1, z.n_lev):
        deeper = lax.ppermute(
            column, "lev", [(i, i - distance) for i in range(distance, z.n_lev)]
        )
        geo_new = geo_new + GRAVITY * deeper[:, None]
    is_polar = (lat_index < z.n_lat // 4) | (lat_index >= z.n_lat - z.n_lat // 4)
    spectra = jnp.stack(
        [
            jnp.where(is_polar, east_keep, east_arrived),
            jnp.where(is_polar, north_keep, north_arrived),
        ]
    )
    return tuple(level_inside(x) for x in (east_final, north_final, thick_new, geo_new, spectra))


def solution(mesh):
    field = P(("members", "lev"), "lat", "lon")
    return jax.shard_map(
        local,
        mesh=mesh,
        in_specs=(field, field, field, field, P("lat", "lon"), P("lev"), P(), P()),
        out_specs=(field, field, field, field, P(None, ("members", "lev"), "lat", "lon")),
        check_vma=False,
    )
```

```python
import functools
import math

import jax
import jax.numpy as jnp
import numpy as np
from jax import lax
from jax.experimental import pallas as pl
from jax.experimental.pallas import tpu as pltpu
from jax.sharding import PartitionSpec as P

KMAX = 360
HALF = 384
WIDE = 2 * HALF
SPARE = HALF - 128
BLOCK = 256
INVERSE_BLOCK = 768

STEP_FACTOR = 0.15
CORIOLIS = 0.2
GRAVITY = 0.25

MIB = 1024 * 1024

EAST_COEF, SINE, COSINE, NORTH_COEF, LEVEL, POLAR, NUMBER, OWN = range(8)


def round_up(value, step):
    return -(-value // step) * step


class Sizes:
    def __init__(self, shape, counts):
        self.lev, self.lat, self.lon = shape
        self.n_lat, self.n_lon, self.n_lev = counts["lat"], counts["lon"], counts["lev"]
        self.nlat, self.nlon = self.lat * self.n_lat, self.lon * self.n_lon
        self.polar = self.nlat // 4
        self.help = self.lat // 2
        self.half_axis = self.n_lat // 2
        self.own = self.lat * self.lev
        self.rows = self.own + 2 * self.lev
        assert self.rows % 8 == 0
        self.mm_rows = round_up(self.rows, 16)
        self.ext = round_up(self.lon + 4, BLOCK)
        self.blocks = self.ext // BLOCK
        self.inverse_block = min(INVERSE_BLOCK, self.ext)
        assert self.ext % self.inverse_block == 0
        self.spec_width = 2 * KMAX // self.n_lon


def high_low(x):
    x = x.astype(np.float32)
    high = x.astype(jnp.bfloat16)
    return high, (x - high.astype(np.float32)).astype(jnp.bfloat16)


def basis_tables(z):
    k = np.arange(KMAX)
    angle = (np.arange(z.inverse_block)[:, None] * k[None, :] % z.nlon) * (2.0 * np.pi / z.nlon)
    full = np.zeros((z.inverse_block, WIDE))
    full[:, :KMAX] = np.cos(angle)
    full[:, HALF : HALF + KMAX] = np.sin(angle)
    high, low = high_low(full)
    forward = np.concatenate([high[:BLOCK], high[:BLOCK], low[:BLOCK]], axis=0)
    inverse = np.concatenate([high.T, high.T, low.T], axis=0)
    return forward, inverse


def phase_table(z):
    k = np.arange(KMAX)
    table = np.zeros((z.n_lon, round_up(2 * z.blocks + 2, 8), HALF), np.float32)
    for place in range(z.n_lon):
        for n, column in enumerate([*range(0, z.ext, BLOCK), -1]):
            angle = ((place * z.lon + column) * k % z.nlon) * (2.0 * np.pi / z.nlon)
            table[place, 2 * n, :KMAX] = np.cos(angle)
            table[place, 2 * n + 1, :KMAX] = np.sin(angle)
    return table


def row_table(z):
    lam_step = np.float32(2.0 * math.pi / z.nlon)
    phi_step = np.float32(math.pi / z.nlat)
    latitude = np.float32(-0.5 * math.pi) + (
        np.arange(z.nlat, dtype=np.float32) + np.float32(0.5)
    ) * phi_step
    cosine = np.cos(latitude.astype(np.float64)).astype(np.float32)
    sine = np.sin(latitude.astype(np.float64)).astype(np.float32)
    north_coef = np.float32(STEP_FACTOR) * lam_step / phi_step
    table = np.zeros((z.n_lat, z.rows, 8), np.float32)
    for place in range(z.n_lat):
        for flat in range(z.rows):
            inner, level = flat // z.lev, flat % z.lev
            inner = -1 if inner == z.lat + 1 else inner
            row = place * z.lat + inner
            one = table[place, flat]
            one[LEVEL], one[NUMBER] = level, -1
            one[OWN] = 0 <= inner < z.lat
            if 0 <= row < z.nlat:
                one[EAST_COEF] = np.float32(STEP_FACTOR) / cosine[row]
                one[SINE], one[COSINE] = sine[row], cosine[row]
                one[NORTH_COEF] = north_coef / cosine[row]
                if row < z.polar:
                    one[POLAR], one[NUMBER] = 1, row
                elif row >= z.nlat - z.polar:
                    one[POLAR], one[NUMBER] = 1, row - (z.nlat - 2 * z.polar)
    return table


def store_split(lhs_ref, first_row, x):
    rows, width = x.shape
    high = x.astype(jnp.bfloat16)
    low = (x - high.astype(jnp.float32)).astype(jnp.bfloat16)
    at = slice(first_row, first_row + rows)
    lhs_ref[at, :width] = high
    lhs_ref[at, width : 2 * width] = low
    lhs_ref[at, 2 * width :] = high


def pad_rows(x, rows):
    return jnp.concatenate([x, jnp.zeros((rows - x.shape[0], x.shape[1]), x.dtype)], axis=0)


def phase_of(phase_ref, n):
    return phase_ref[2 * n : 2 * n + 1], phase_ref[2 * n + 1 : 2 * n + 2]


def store_blocks(z, x, lhs_ref):
    for block in range(z.blocks):
        part = pad_rows(x[:, block * BLOCK : (block + 1) * BLOCK], z.mm_rows)
        store_split(lhs_ref, block * z.mm_rows, part)


def turn_blocks(z, sums, phase_ref, out_ref):
    rows = sums.shape[0] // z.blocks
    real = imag = None
    for block in range(z.blocks):
        cos, sin = phase_of(phase_ref, block)
        part = sums[block * rows : block * rows + out_ref.shape[0]]
        a, b = part[:, :HALF], part[:, HALF:]
        more_real, more_imag = a * cos - b * sin, a * sin + b * cos
        real = more_real if real is None else real + more_real
        imag = more_imag if imag is None else imag + more_imag
    out_ref[:, :HALF] = real
    out_ref[:, HALF:] = imag


def inverse_blocks(z, coef, basis_ref, phase_ref, lhs_ref):
    a, b = coef[:, :HALF], coef[:, HALF:]
    width = z.inverse_block
    blocks = range(z.ext // width)
    for block in blocks:
        cos, sin = phase_of(phase_ref, block * width // BLOCK)
        turned = jnp.concatenate([a * cos + b * sin, b * cos - a * sin], axis=1)
        store_split(lhs_ref, block * z.mm_rows, pad_rows(turned, z.mm_rows))
    rows = jnp.dot(lhs_ref[...], basis_ref[...], preferred_element_type=jnp.float32)
    cos, sin = phase_of(phase_ref, z.blocks)
    before = jnp.sum(a * cos + b * sin, axis=1, keepdims=True)
    return [rows[n * z.mm_rows : n * z.mm_rows + coef.shape[0]] for n in blocks], before


def roll(x, shift, axis):
    return pltpu.roll(x, shift % x.shape[axis], axis)


def east_diff(x):
    return roll(x, -1, 1) - roll(x, 1, 1)


def flat_rows(z, ref):
    return ref[...].reshape(z.own, ref.shape[2])


def widen(z, x):
    return jnp.concatenate([x, jnp.zeros((x.shape[0], z.ext - x.shape[1]), x.dtype)], axis=1)


def put_lane(x, at, column):
    lane = lax.broadcasted_iota(jnp.int32, x.shape, 1)
    return jnp.where(lane == at, column, x)


def column_of(row_ref, which):
    return row_ref[:, which : which + 1]


def north_factor(z):
    return STEP_FACTOR * (2.0 * math.pi / z.nlon) / (math.pi / z.nlat)


def look_up(number, table_ref):
    table = table_ref[...].astype(jnp.float32)
    lane = lax.broadcasted_iota(jnp.int32, (number.shape[0], table.shape[1]), 1)
    return jnp.sum(jnp.where(lane == number, table, 0.0), axis=1, keepdims=True)


def coefficients(z, sums, number, kept_ref):
    lane = lax.broadcasted_iota(jnp.int32, (1, WIDE), 1)
    k = jnp.where(lane < HALF, lane, lane - HALF)
    weight = jnp.where(k == 0, 1.0 / z.nlon, 2.0 / z.nlon).astype(jnp.float32)
    keep = (k.astype(jnp.float32) < look_up(number, kept_ref)) & (k < KMAX)
    return jnp.where(keep, sums * weight, 0.0)


def in_slot_order(z, values, number, row_ref, slot_ref, distance):
    rows, count = values.shape[0], z.help * z.lev
    owner = lax.rem(lax.axis_index("lat") + distance, z.n_lat)
    place = look_up(number, slot_ref).astype(jnp.int32) - owner * z.help
    own = (column_of(row_ref, OWN)[:rows] > 0.0) & (number >= 0)
    place = jnp.where(own & (place >= 0) & (place < z.help), place, -count)
    place = place * z.lev + column_of(row_ref, LEVEL)[:rows].astype(jnp.int32)
    lane = lax.broadcasted_iota(jnp.int32, (rows, round_up(count, 128)), 1)
    ordered = lax.dot_general(
        (lane == place).astype(jnp.float32),
        values,
        (((0,), (0,)), ((), ())),
        precision=lax.Precision.HIGHEST,
        preferred_element_type=jnp.float32,
    )
    return ordered[:count]


def sector_part(z, coef, place):
    part = None
    for one in range(z.n_lon):
        first = one * z.spec_width
        first = first if first < KMAX else first - KMAX + HALF
        this = coef[:, first : first + z.spec_width]
        part = this if part is None else jnp.where(place == one, this, part)
    return part


def depths(z, depth_ref, row_ref):
    level = column_of(row_ref, LEVEL)[: z.own]
    depth = jnp.zeros_like(level)
    for lev in range(z.lev):
        depth = jnp.where(level == lev, depth_ref[lev], depth)
    return depth


def store_rims(z, ref, g, we, wn, last):
    edge = 2 * z.lev
    ref[:edge] = g[z.own - edge :] if last else g[:edge]
    ref[edge : edge + z.lev] = we[z.own - z.lev :] if last else we[: z.lev]
    ref[edge + z.lev :] = wn[z.own - z.lev :] if last else wn[: z.lev]


def east_forward(
    z, we_hbm, wn_hbm, g_hbm, row_hbm, phase_hbm, basis_hbm,
    share_ref, even_ref, odd_ref, we_ref, wn_ref, g_ref, row_ref, phase_ref, basis_ref, lhs_ref, sems,
):
    pairs = (
        (row_hbm.at[lax.axis_index("lat")], row_ref),
        (phase_hbm.at[lax.axis_index("lon")], phase_ref),
        (g_hbm, g_ref),
        (we_hbm, we_ref),
        (wn_hbm, wn_ref),
        (basis_hbm, basis_ref),
    )
    copies = [pltpu.make_async_copy(*pair, sems.at[n]) for n, pair in enumerate(pairs)]
    for copy in copies:
        copy.start()
    for copy in copies[:-1]:
        copy.wait()
    g, we, wn = flat_rows(z, g_ref), flat_rows(z, we_ref), flat_rows(z, wn_ref)
    coef, sine = column_of(row_ref, EAST_COEF)[: z.own], column_of(row_ref, SINE)[: z.own]
    new = widen(z, we + CORIOLIS * sine * wn) - coef * east_diff(widen(z, g))
    tail = put_lane(new[:, z.ext - 128 :], 127, 0.0)
    store_blocks(z, jnp.concatenate([new[:, : z.ext - 128], tail], axis=1), lhs_ref)

    odd = lax.rem(lax.axis_index("lat"), 2) == 1
    last, flat = z.lat - 1, (z.lev, z.lon)
    far = (g_ref[last - 1], g_ref[last], we_ref[last], wn_ref[last])
    near = (g_ref[0], g_ref[1], we_ref[0], wn_ref[0])
    for n, (bottom, top) in enumerate(zip(far, near, strict=True)):
        at = slice(n * z.lev, (n + 1) * z.lev)
        even_ref[at] = jnp.where(odd, top, bottom).reshape(flat)
        odd_ref[at] = jnp.where(odd, bottom, top).reshape(flat)

    copies[-1].wait()
    sums = jnp.dot(lhs_ref[...], basis_ref[...], preferred_element_type=jnp.float32)
    turn_blocks(z, sums, phase_ref, share_ref)
    cos, sin = phase_of(phase_ref, z.blocks)
    before = -coef * g[:, 0:1]
    share_ref[:, :HALF] += before * cos
    share_ref[:, HALF:] += before * sin
    spare = share_ref[:, SPARE:HALF]
    last = z.lon - 1
    edges = ((g, last - 1), (g, last), (we, last), (wn, last), (g, 0), (g, 1), (we, 0), (wn, 0))
    for n, (x, column) in enumerate(edges):
        spare = put_lane(spare, KMAX - SPARE + n, x[:, column : column + 1])
    share_ref[:, SPARE:HALF] = spare


def north_forward(
    z, we_ref, wn_ref, g_ref, even_ref, odd_ref, row_ref, phase_ref, basis_ref, kept_ref, slot_ref, *rest
):
    share_ref, north_ref, sends, (g_rows, lhs_ref) = rest[0], rest[1], rest[2:-2], rest[-2:]
    edge, lev = 2 * z.lev, z.lev
    odd = lax.rem(lax.axis_index("lat"), 2) == 1
    below = jnp.where(odd, odd_ref[...], even_ref[...])
    above = jnp.where(odd, even_ref[...], odd_ref[...])
    coef, sine = north_factor(z), CORIOLIS * column_of(row_ref, SINE)
    own = flat_rows(z, g_ref)
    g_rows[: z.own] = own
    g_rows[z.own : z.own + lev] = below[:lev]
    g_rows[z.own + lev :] = above[lev:edge]
    g = g_rows[...]
    diff = (roll(g, -lev, 0) - roll(g, lev, 0))[: z.own]
    north_ref[: z.own] = flat_rows(z, wn_ref) - coef * diff - sine[: z.own] * flat_rows(z, we_ref)
    for at, diff, rim in (
        (z.own, below[lev:edge] - own[z.own - lev :], below),
        (z.own + lev, own[:lev] - above[:lev], above),
    ):
        we, wn = rim[edge : edge + lev], rim[edge + lev :]
        north_ref[at : at + lev] = wn - coef * diff - sine[at : at + lev] * we
    store_blocks(z, widen(z, north_ref[...]), lhs_ref)
    sums = jnp.dot(lhs_ref[...], basis_ref[...], preferred_element_type=jnp.float32)
    turn_blocks(z, sums, phase_ref, share_ref)
    number = column_of(row_ref, NUMBER).astype(jnp.int32)
    masked = coefficients(z, share_ref[...], number, kept_ref)
    ordered = in_slot_order(z, masked, number, row_ref, slot_ref, z.half_axis)
    for distance, send_ref in enumerate(sends):
        place = lax.rem(lax.axis_index("lon") + distance, z.n_lon)
        send_ref[...] = sector_part(z, ordered, place).reshape(send_ref.shape)


def east_inverse(
    z, depth_ref, we_ref, wn_ref, g_ref, thick_ref, row_ref, phase_ref, kept_ref, slot_ref, *rest
):
    shares, rest = rest[: z.n_lon], rest[z.n_lon :]
    basis_ref, final_ref, part_ref, keep_ref, send_ref, lhs_ref = rest
    number = column_of(row_ref, NUMBER)[: z.own].astype(jnp.int32)
    coef = coefficients(z, sum(ref[...] for ref in shares), number, kept_ref)
    part = sector_part(z, coef, lax.axis_index("lon"))
    for distance, ref in ((0, keep_ref), (z.half_axis, send_ref)):
        ref[...] = in_slot_order(z, part, number, row_ref, slot_ref, distance).reshape(ref.shape)
    blocks, before = inverse_blocks(z, coef, basis_ref, phase_ref, lhs_ref)
    filtered = jnp.concatenate(blocks, axis=1)
    tail = put_lane(filtered[:, z.ext - 128 :], 127, before)
    filtered = jnp.concatenate([filtered[:, : z.ext - 128], tail], axis=1)

    first = KMAX - SPARE
    left, right = shares[1][:, SPARE:HALF], shares[-1][:, SPARE:HALF]
    at_right = z.lon - (z.ext - 128)

    def rimmed(ref, left_of, right_of):
        x = widen(z, flat_rows(z, ref))
        tail = x[:, z.ext - 128 :]
        for n, lane in enumerate(right_of):
            tail = put_lane(tail, at_right + n, right[:, first + lane : first + lane + 1])
        for n, lane in enumerate(left_of):
            tail = put_lane(tail, 127 - n, left[:, first + lane : first + lane + 1])
        return jnp.concatenate([x[:, : z.ext - 128], tail], axis=1)

    g = rimmed(g_ref, (1, 0), (4, 5))
    we, wn = rimmed(we_ref, (2,), (6,)), rimmed(wn_ref, (3,), (7,))
    coef, sine = column_of(row_ref, EAST_COEF)[: z.own], column_of(row_ref, SINE)[: z.own]
    new = we - coef * east_diff(g) + CORIOLIS * sine * wn
    final = jnp.where(column_of(row_ref, POLAR)[: z.own] > 0.0, filtered, new)
    final_ref[...] = final[:, : z.lon].reshape(final_ref.shape)
    change = depths(z, depth_ref, row_ref) * coef * east_diff(final)[:, : z.lon]
    part_ref[...] = flat_rows(z, thick_ref) - change


def on_polar_band(z):
    lat_index = lax.axis_index("lat")
    return (lat_index < z.n_lat // 4) | (lat_index >= z.n_lat - z.n_lat // 4)


def north_inverse(
    z, depth_ref, north_ref, part_ref, row_ref, phase_ref, kept_ref, slot_ref, *rest
):
    shares, arrived, rest = rest[: z.n_lon], rest[z.n_lon : 2 * z.n_lon], rest[2 * z.n_lon :]
    basis_ref, final_ref, thick_ref, column_ref, spectra_ref, lhs_ref = rest
    number = column_of(row_ref, NUMBER).astype(jnp.int32)
    coef = coefficients(z, sum(ref[...] for ref in shares), number, kept_ref)
    part = sector_part(z, coef, lax.axis_index("lon"))
    keep = in_slot_order(z, part, number, row_ref, slot_ref, 0).reshape(spectra_ref.shape)
    spectra_ref[...] = jnp.where(on_polar_band(z), keep, sum(ref[...] for ref in arrived))
    blocks, _ = inverse_blocks(z, coef, basis_ref, phase_ref, lhs_ref)
    scale = depths(z, depth_ref, row_ref) * column_of(row_ref, NORTH_COEF)[: z.own]
    for block, filtered in enumerate(blocks):
        at = slice(block * z.inverse_block, min((block + 1) * z.inverse_block, z.lon))
        filtered = filtered[:, : at.stop - at.start]
        final = jnp.where(column_of(row_ref, POLAR) > 0.0, filtered, north_ref[:, at])
        final_ref[:, :, at] = final[: z.own].reshape(z.lat, z.lev, at.stop - at.start)
        scaled = final * column_of(row_ref, COSINE)
        diff = (roll(scaled, -z.lev, 0) - roll(scaled, z.lev, 0))[: z.own]
        thick = part_ref[:, at] - scale * diff
        thick_ref[:, :, at] = thick.reshape(z.lat, z.lev, at.stop - at.start)
    column_ref[...] = sum(thick_ref[:, lev, :] for lev in range(z.lev))


def join_spectra(z, keep_ref, arrived_ref, north_ref, spectra_ref):
    spectra_ref[0] = jnp.where(on_polar_band(z), keep_ref[...], arrived_ref[...])
    spectra_ref[1] = north_ref[...]


def close(z, thick_ref, surface_ref, spectra_ref, *rest):
    del spectra_ref
    deeper, geo_ref = rest[:-1], rest[-1]
    column = sum(ref[...] for ref in deeper) if deeper else 0.0
    for lev in reversed(range(z.lev)):
        column = column + thick_ref[:, lev, :]
        geo_ref[:, lev, :] = surface_ref[...] + GRAVITY * column


def call(kernel, n_in, out_shape, scratch, micros, spaces=None, vmem=24):
    vmem_spec = pl.BlockSpec(memory_space=pltpu.VMEM)
    spaces = spaces or {}
    return pl.pallas_call(
        kernel,
        in_specs=[
            pl.BlockSpec(memory_space=spaces[n]) if n in spaces else vmem_spec for n in range(n_in)
        ],
        out_specs=[vmem_spec] * len(out_shape),
        out_shape=[
            jax.ShapeDtypeStruct(s, jnp.float32) if isinstance(s, tuple) else s for s in out_shape
        ],
        scratch_shapes=scratch,
        compiler_params=pltpu.CompilerParams(vmem_limit_bytes=vmem * MIB),
        cost_estimate=pl.CostEstimate(
            flops=int(micros * 1.15e9), bytes_accessed=0, transcendentals=0
        ),
    )


def shifted(block, axis, distance):
    count = lax.axis_size(axis)
    return lax.ppermute(block, axis, [(i, (i + distance) % count) for i in range(count)])


def level_inside(x):
    return jnp.swapaxes(x, -3, -2)


def local(
    wind_east, wind_north, thickness, geopot, surface_geopot, mean_depth, kept_modes, slot_table
):
    z = Sizes(thickness.shape, {axis: lax.axis_size(axis) for axis in ("lat", "lon", "lev")})
    wind_east, wind_north, thickness, geopot = (
        level_inside(x) for x in (wind_east, wind_north, thickness, geopot)
    )
    field = (z.lat, z.lev, z.lon)
    forward, inverse = (jnp.asarray(x) for x in basis_tables(z))
    phase = jnp.asarray(phase_table(z))
    per_row = jnp.asarray(row_table(z))
    kept = kept_modes[None, :]
    slots = slot_table[None, :]
    payload = (z.rows, WIDE)
    rims = (4 * z.lev, z.lon)
    spec = (z.help, z.lev, z.spec_width)
    waves_lhs = pltpu.VMEM((z.ext // z.inverse_block * z.mm_rows, 3 * WIDE), jnp.bfloat16)

    row_shape, phase_shape = per_row.shape[1:], phase.shape[1:]
    in_hbm = [
        pltpu.with_memory_space_constraint(x, pltpu.HBM)
        for x in (wind_east, wind_north, geopot, per_row, phase, forward)
    ]
    columns_lhs = pltpu.VMEM((z.blocks * z.mm_rows, 3 * BLOCK), jnp.bfloat16)
    waves_lhs = pltpu.VMEM((z.ext // z.inverse_block * z.mm_rows, 3 * WIDE), jnp.bfloat16)

    east_share, to_even, to_odd, wind_east, wind_north, geopot, per_row, phase, forward = call(
        functools.partial(east_forward, z),
        6,
        [(z.own, WIDE), rims, rims]
        + [field, field, field, row_shape, phase_shape]
        + [jax.ShapeDtypeStruct(forward.shape, forward.dtype)],
        [columns_lhs, pltpu.SemaphoreType.DMA((6,))],
        4,
        {n: pltpu.HBM for n in range(6)},
    )(*in_hbm)
    east_shares = [east_share] + [shifted(east_share, "lon", s) for s in range(1, z.n_lon)]
    met = []
    for start, rim in enumerate((to_even, to_odd)):
        pairs = [(i, i + 1) for i in range(start, z.n_lat - 1, 2)]
        met.append(lax.ppermute(rim, "lat", pairs + [(b, a) for a, b in pairs]))

    north_share, north_new, *north_sends = call(
        functools.partial(north_forward, z),
        10,
        [(z.rows, WIDE), (z.rows, z.lon)] + [spec] * z.n_lon,
        [pltpu.VMEM((z.rows, z.lon), jnp.float32), columns_lhs],
        0.2,
    )(wind_east, wind_north, geopot, *met, per_row, phase, forward, kept, slots)
    north_shares = [north_share] + [shifted(north_share, "lon", s) for s in range(1, z.n_lon)]

    polar_bands = [i for i in range(z.n_lat) if i < z.n_lat // 4 or i >= z.n_lat - z.n_lat // 4]
    to_helper = [(i, (i + z.half_axis) % z.n_lat) for i in polar_bands]
    north_arrived = []
    for distance, send in enumerate(north_sends):
        route = [
            (a * z.n_lon + lon, b * z.n_lon + (lon + distance) % z.n_lon)
            for a, b in to_helper
            for lon in range(z.n_lon)
        ]
        north_arrived.append(lax.ppermute(send, ("lat", "lon"), route))

    east_final, thick_part, east_keep, east_send = call(
        functools.partial(east_inverse, z),
        10 + z.n_lon,
        [field, (z.own, z.lon), spec, spec],
        [waves_lhs],
        1,
        {0: pltpu.SMEM},
    )(
        mean_depth, wind_east, wind_north, geopot, thickness, per_row, phase, kept, slots,
        *east_shares, inverse,
    )
    east_arrived = lax.ppermute(east_send, "lat", to_helper)

    north_final, thick_new, column, north_spectra = call(
        functools.partial(north_inverse, z),
        8 + 2 * z.n_lon,
        [field, field, (z.lat, z.lon), spec],
        [waves_lhs],
        2,
        {0: pltpu.SMEM},
    )(
        mean_depth, north_new, thick_part, per_row, phase, kept, slots,
        *north_shares, *north_arrived, inverse,
    )

    deeper = [
        lax.ppermute(column, "lev", [(i, i - distance) for i in range(distance, z.n_lev)])
        for distance in range(1, z.n_lev)
    ]
    (spectra,) = call(functools.partial(join_spectra, z), 3, [(2, *spec)], [], 4.2)(
        east_keep, east_arrived, north_spectra
    )
    (geo_new,) = call(functools.partial(close, z), 3 + len(deeper), [field], [], 1)(
        thick_new, surface_geopot, spectra, *deeper
    )
    return tuple(level_inside(x) for x in (east_final, north_final, thick_new, geo_new, spectra))


def solution(mesh):
    field = P(("members", "lev"), "lat", "lon")
    return jax.shard_map(
        local,
        mesh=mesh,
        in_specs=(field, field, field, field, P("lat", "lon"), P("lev"), P(), P()),
        out_specs=(field, field, field, field, P(None, ("members", "lev"), "lat", "lon")),
        check_vma=False,
    )
```

```python
import functools
import math

import jax
import jax.numpy as jnp
import numpy as np
from jax import lax
from jax.experimental import pallas as pl
from jax.experimental.pallas import tpu as pltpu
from jax.sharding import PartitionSpec as P

KMAX = 360
HALF = 384
WIDE = 2 * HALF
SPARE = HALF - 128
BLOCK = 256
INVERSE_BLOCK = 768

STEP_FACTOR = 0.15
CORIOLIS = 0.2
GRAVITY = 0.25

MIB = 1024 * 1024

EAST_COEF, SINE, COSINE, NORTH_COEF, LEVEL, POLAR, NUMBER, OWN = range(8)


def round_up(value, step):
    return -(-value // step) * step


class Sizes:
    def __init__(self, shape, counts):
        self.lev, self.lat, self.lon = shape
        self.n_lat, self.n_lon, self.n_lev = counts["lat"], counts["lon"], counts["lev"]
        self.nlat, self.nlon = self.lat * self.n_lat, self.lon * self.n_lon
        self.polar = self.nlat // 4
        self.help = self.lat // 2
        self.half_axis = self.n_lat // 2
        self.own = self.lat * self.lev
        self.rows = self.own + 2 * self.lev
        assert self.rows % 8 == 0
        self.mm_rows = round_up(self.rows, 16)
        self.ext = round_up(self.lon + 4, BLOCK)
        self.blocks = self.ext // BLOCK
        self.inverse_block = min(INVERSE_BLOCK, self.ext)
        assert self.ext % self.inverse_block == 0
        self.spec_width = 2 * KMAX // self.n_lon
        self.helped = self.help * self.lev
        self.ahead = round_up(self.helped, 8)


def high_low(x):
    x = x.astype(np.float32)
    high = x.astype(jnp.bfloat16)
    return high, (x - high.astype(np.float32)).astype(jnp.bfloat16)


def basis_tables(z):
    k = np.arange(KMAX)
    angle = (np.arange(z.inverse_block)[:, None] * k[None, :] % z.nlon) * (2.0 * np.pi / z.nlon)
    full = np.zeros((z.inverse_block, WIDE))
    full[:, :KMAX] = np.cos(angle)
    full[:, HALF : HALF + KMAX] = np.sin(angle)
    high, low = high_low(full)
    forward = np.concatenate([high[:BLOCK], high[:BLOCK], low[:BLOCK]], axis=0)
    inverse = np.concatenate([high.T, high.T, low.T], axis=0)
    return forward, inverse


def phase_table(z):
    k = np.arange(KMAX)
    table = np.zeros((z.n_lon, round_up(2 * z.blocks + 2, 8), HALF), np.float32)
    for place in range(z.n_lon):
        for n, column in enumerate([*range(0, z.ext, BLOCK), -1]):
            angle = ((place * z.lon + column) * k % z.nlon) * (2.0 * np.pi / z.nlon)
            table[place, 2 * n, :KMAX] = np.cos(angle)
            table[place, 2 * n + 1, :KMAX] = np.sin(angle)
    return table


def row_table(z):
    lam_step = np.float32(2.0 * math.pi / z.nlon)
    phi_step = np.float32(math.pi / z.nlat)
    latitude = np.float32(-0.5 * math.pi) + (
        np.arange(z.nlat, dtype=np.float32) + np.float32(0.5)
    ) * phi_step
    cosine = np.cos(latitude.astype(np.float64)).astype(np.float32)
    sine = np.sin(latitude.astype(np.float64)).astype(np.float32)
    north_coef = np.float32(STEP_FACTOR) * lam_step / phi_step
    table = np.zeros((z.n_lat, z.rows, 8), np.float32)
    for place in range(z.n_lat):
        for flat in range(z.rows):
            inner, level = flat // z.lev, flat % z.lev
            inner = -1 if inner == z.lat + 1 else inner
            row = place * z.lat + inner
            one = table[place, flat]
            one[LEVEL], one[NUMBER] = level, -1
            one[OWN] = 0 <= inner < z.lat
            if 0 <= row < z.nlat:
                one[EAST_COEF] = np.float32(STEP_FACTOR) / cosine[row]
                one[SINE], one[COSINE] = sine[row], cosine[row]
                one[NORTH_COEF] = north_coef / cosine[row]
                if row < z.polar:
                    one[POLAR], one[NUMBER] = 1, row
                elif row >= z.nlat - z.polar:
                    one[POLAR], one[NUMBER] = 1, row - (z.nlat - 2 * z.polar)
    return table


def on_polar_band(z):
    lat_index = lax.axis_index("lat")
    return (lat_index < z.n_lat // 4) | (lat_index >= z.n_lat - z.n_lat // 4)


def store_split(lhs_ref, first_row, x):
    rows, width = x.shape
    high = x.astype(jnp.bfloat16)
    low = (x - high.astype(jnp.float32)).astype(jnp.bfloat16)
    at = slice(first_row, first_row + rows)
    lhs_ref[at, :width] = high
    lhs_ref[at, width : 2 * width] = low
    lhs_ref[at, 2 * width :] = high


def pad_rows(x, rows):
    return jnp.concatenate([x, jnp.zeros((rows - x.shape[0], x.shape[1]), x.dtype)], axis=0)


def phase_of(phase_ref, n):
    return phase_ref[2 * n : 2 * n + 1], phase_ref[2 * n + 1 : 2 * n + 2]


def forward_sums(z, x, basis_ref, phase_ref, lhs_ref, out_ref, at=slice(None)):
    count = round_up(x.shape[0], 16)
    for block in range(z.blocks):
        part = pad_rows(x[:, block * BLOCK : (block + 1) * BLOCK], count)
        store_split(lhs_ref, block * count, part)
    lhs = lhs_ref[: z.blocks * count]
    sums = jnp.dot(lhs, basis_ref[...], preferred_element_type=jnp.float32)
    real = imag = None
    for block in range(z.blocks):
        cos, sin = phase_of(phase_ref, block)
        part = sums[block * count : block * count + x.shape[0]]
        a, b = part[:, :HALF], part[:, HALF:]
        more_real, more_imag = a * cos - b * sin, a * sin + b * cos
        real = more_real if real is None else real + more_real
        imag = more_imag if imag is None else imag + more_imag
    out_ref[at, :HALF] = real
    out_ref[at, HALF:] = imag


def inverse_rows(z, coef, basis_ref, phase_ref, lhs_ref, out_ref, at=slice(None)):
    a, b = coef[:, :HALF], coef[:, HALF:]
    count, width = round_up(coef.shape[0], 16), z.inverse_block
    blocks = range(z.ext // width)
    for block in blocks:
        cos, sin = phase_of(phase_ref, block * width // BLOCK)
        turned = jnp.concatenate([a * cos + b * sin, b * cos - a * sin], axis=1)
        store_split(lhs_ref, block * count, pad_rows(turned, count))
    lhs = lhs_ref[: len(blocks) * count]
    rows = jnp.dot(lhs, basis_ref[...], preferred_element_type=jnp.float32)
    for block in blocks:
        out_ref[at, block * width : (block + 1) * width] = rows[
            block * count : block * count + coef.shape[0]
        ]


def roll(x, shift, axis):
    return pltpu.roll(x, shift % x.shape[axis], axis)


def east_diff(x):
    return roll(x, -1, 1) - roll(x, 1, 1)


def flat_rows(z, ref):
    return ref[...].reshape(z.own, ref.shape[2])


def widen(z, x):
    return jnp.concatenate([x, jnp.zeros((x.shape[0], z.ext - x.shape[1]), x.dtype)], axis=1)


def put_lane(x, at, column):
    lane = lax.broadcasted_iota(jnp.int32, x.shape, 1)
    return jnp.where(lane == at, column, x)


def column_of(row_ref, which):
    return row_ref[:, which : which + 1]


def north_factor(z):
    return STEP_FACTOR * (2.0 * math.pi / z.nlon) / (math.pi / z.nlat)


def look_up(number, table_ref):
    table = table_ref[...].astype(jnp.float32)
    lane = lax.broadcasted_iota(jnp.int32, (number.shape[0], table.shape[1]), 1)
    return jnp.sum(jnp.where(lane == number, table, 0.0), axis=1, keepdims=True)


def coefficients(z, sums, kept):
    lane = lax.broadcasted_iota(jnp.int32, (1, WIDE), 1)
    k = jnp.where(lane < HALF, lane, lane - HALF)
    weight = jnp.where(k == 0, 1.0 / z.nlon, 2.0 / z.nlon).astype(jnp.float32)
    keep = (k.astype(jnp.float32) < kept) & (k < KMAX)
    return jnp.where(keep, sums * weight, 0.0)


def slot_order(z, number, row_ref, slot_ref):
    lat_index = lax.axis_index("lat")
    slot = look_up(number, slot_ref).astype(jnp.int32)
    theirs = slot - lax.rem(lat_index + z.half_axis, z.n_lat) * z.help
    mine = slot - lat_index * z.help
    level = column_of(row_ref, LEVEL).astype(jnp.int32)
    flat = lax.broadcasted_iota(jnp.int32, slot.shape, 0)
    place = jnp.where((mine >= 0) & (mine < z.help), z.helped + mine * z.lev + level, -1)
    place = jnp.where((theirs >= 0) & (theirs < z.help), theirs * z.lev + level, place)
    place = jnp.where(number >= 0, place, -1)
    place = jnp.where(flat < z.own, place, flat)
    lane = lax.broadcasted_iota(jnp.int32, (z.rows, round_up(z.rows, 128)), 1)
    return (lane == place).astype(jnp.float32)


def reorder(chosen, values):
    return lax.dot_general(
        chosen,
        values,
        (((0,), (0,)), ((), ())),
        precision=lax.Precision.HIGHEST,
        preferred_element_type=jnp.float32,
    )


def sector_part(z, coef, place):
    part = None
    for one in range(z.n_lon):
        first = one * z.spec_width
        first = first if first < KMAX else first - KMAX + HALF
        this = coef[:, first : first + z.spec_width]
        part = this if part is None else jnp.where(place == one, this, part)
    return part


def depths(z, depth_ref, row_ref):
    level = column_of(row_ref, LEVEL)[: z.own]
    depth = jnp.zeros_like(level)
    for lev in range(z.lev):
        depth = jnp.where(level == lev, depth_ref[lev], depth)
    return depth


def store_rims(z, ref, g, we, wn, last):
    edge = 2 * z.lev
    ref[:edge] = g[z.own - edge :] if last else g[:edge]
    ref[edge : edge + z.lev] = we[z.own - z.lev :] if last else we[: z.lev]
    ref[edge + z.lev :] = wn[z.own - z.lev :] if last else wn[: z.lev]


def east_forward(
    z, we_hbm, wn_hbm, g_hbm, row_hbm, phase_hbm, basis_hbm,
    share_ref, even_ref, odd_ref, we_ref, wn_ref, g_ref, row_ref, phase_ref, basis_ref, lhs_ref, sems,
):
    pairs = (
        (row_hbm.at[lax.axis_index("lat")], row_ref),
        (phase_hbm.at[lax.axis_index("lon")], phase_ref),
        (g_hbm, g_ref),
        (we_hbm, we_ref),
        (wn_hbm, wn_ref),
        (basis_hbm, basis_ref),
    )
    copies = [pltpu.make_async_copy(*pair, sems.at[n]) for n, pair in enumerate(pairs)]
    for copy in copies:
        copy.start()
    for copy in copies[:-1]:
        copy.wait()
    g, we, wn = flat_rows(z, g_ref), flat_rows(z, we_ref), flat_rows(z, wn_ref)
    odd = lax.rem(lax.axis_index("lat"), 2) == 1
    last, flat = z.lat - 1, (z.lev, z.lon)
    far = (g_ref[last - 1], g_ref[last], we_ref[last], wn_ref[last])
    near = (g_ref[0], g_ref[1], we_ref[0], wn_ref[0])
    for n, (bottom, top) in enumerate(zip(far, near, strict=True)):
        at = slice(n * z.lev, (n + 1) * z.lev)
        even_ref[at] = jnp.where(odd, top, bottom).reshape(flat)
        odd_ref[at] = jnp.where(odd, bottom, top).reshape(flat)

    copies[-1].wait()

    @pl.when(on_polar_band(z))
    def _():
        coef, sine = column_of(row_ref, EAST_COEF)[: z.own], column_of(row_ref, SINE)[: z.own]
        new = widen(z, we + CORIOLIS * sine * wn) - coef * east_diff(widen(z, g))
        tail = put_lane(new[:, z.ext - 128 :], 127, 0.0)
        new = jnp.concatenate([new[:, : z.ext - 128], tail], axis=1)
        forward_sums(z, new, basis_ref, phase_ref, lhs_ref, share_ref)
        cos, sin = phase_of(phase_ref, z.blocks)
        before = -coef * g[:, 0:1]
        share_ref[:, :HALF] += before * cos
        share_ref[:, HALF:] += before * sin

    @pl.when(jnp.logical_not(on_polar_band(z)))
    def _():
        share_ref[...] = jnp.zeros_like(share_ref)

    spare = share_ref[:, SPARE:HALF]
    last = z.lon - 1
    edges = ((g, last - 1), (g, last), (we, last), (wn, last), (g, 0), (g, 1), (we, 0), (wn, 0))
    for n, (x, column) in enumerate(edges):
        spare = put_lane(spare, KMAX - SPARE + n, x[:, column : column + 1])
    share_ref[:, SPARE:HALF] = spare


def north_forward(
    z, we_ref, wn_ref, g_ref, even_ref, odd_ref, row_ref, phase_ref, basis_ref, kept_ref, slot_ref, *rest
):
    ahead_ref, rest_ref, north_ref, chosen_ref, g_rows, lhs_ref, share_ref = rest
    edge, lev = 2 * z.lev, z.lev
    odd = lax.rem(lax.axis_index("lat"), 2) == 1
    below = jnp.where(odd, odd_ref[...], even_ref[...])
    above = jnp.where(odd, even_ref[...], odd_ref[...])
    coef, sine = north_factor(z), CORIOLIS * column_of(row_ref, SINE)
    own = flat_rows(z, g_ref)
    g_rows[: z.own] = own
    g_rows[z.own : z.own + lev] = below[:lev]
    g_rows[z.own + lev :] = above[lev:edge]
    g = g_rows[...]
    diff = (roll(g, -lev, 0) - roll(g, lev, 0))[: z.own]
    north_ref[: z.own] = flat_rows(z, wn_ref) - coef * diff - sine[: z.own] * flat_rows(z, we_ref)
    for at, diff, rim in (
        (z.own, below[lev:edge] - own[z.own - lev :], below),
        (z.own + lev, own[:lev] - above[:lev], above),
    ):
        we, wn = rim[edge : edge + lev], rim[edge + lev :]
        north_ref[at : at + lev] = wn - coef * diff - sine[at : at + lev] * we
    number = column_of(row_ref, NUMBER).astype(jnp.int32)
    kept = look_up(number, kept_ref)

    @pl.when(on_polar_band(z))
    def _():
        forward_sums(z, widen(z, north_ref[...]), basis_ref, phase_ref, lhs_ref, share_ref)
        share_ref[:, SPARE:HALF] = put_lane(share_ref[:, SPARE:HALF], KMAX - SPARE, kept)
        chosen = slot_order(z, number, row_ref, slot_ref)
        ordered = reorder(chosen, share_ref[...])
        ahead_ref[...] = ordered[: z.ahead]
        rest_ref[...] = ordered[z.ahead : z.rows]
        chosen_ref[...] = chosen

    @pl.when(jnp.logical_not(on_polar_band(z)))
    def _():
        beyond = slice(z.own - z.ahead, z.rows - z.ahead)
        ahead_ref[...] = jnp.zeros_like(ahead_ref)
        rest_ref[...] = jnp.zeros_like(rest_ref)
        chosen_ref[...] = jnp.zeros_like(chosen_ref)
        rows = widen(z, north_ref[z.own :])
        forward_sums(z, rows, basis_ref, phase_ref, lhs_ref, rest_ref, beyond)
        rest_ref[beyond, SPARE:HALF] = put_lane(
            rest_ref[beyond, SPARE:HALF], KMAX - SPARE, kept[z.own :]
        )


def east_inverse(
    z, depth_ref, we_ref, wn_ref, g_ref, thick_ref, row_ref, phase_ref, kept_ref, chosen_ref, *rest
):
    shares, rest = rest[: z.n_lon], rest[z.n_lon :]
    basis_ref, final_ref, part_ref, keep_ref, send_ref, lhs_ref, rows_ref = rest
    coef, sine = column_of(row_ref, EAST_COEF)[: z.own], column_of(row_ref, SINE)[: z.own]

    @pl.when(on_polar_band(z))
    def _():
        number = column_of(row_ref, NUMBER)[: z.own].astype(jnp.int32)
        waves = coefficients(z, sum(ref[...] for ref in shares), look_up(number, kept_ref))
        part = sector_part(z, waves, lax.axis_index("lon"))
        ordered = reorder(chosen_ref[: z.own], part)
        send_ref[...] = ordered[: z.helped].reshape(send_ref.shape)
        keep_ref[...] = ordered[z.helped : 2 * z.helped].reshape(keep_ref.shape)
        inverse_rows(z, waves, basis_ref, phase_ref, lhs_ref, rows_ref)
        cos, sin = phase_of(phase_ref, z.blocks)
        before = jnp.sum(waves[:, :HALF] * cos + waves[:, HALF:] * sin, axis=1, keepdims=True)
        rows_ref[:, z.ext - 128 :] = put_lane(rows_ref[:, z.ext - 128 :], 127, before)

    @pl.when(jnp.logical_not(on_polar_band(z)))
    def _():
        send_ref[...] = jnp.zeros_like(send_ref)
        keep_ref[...] = jnp.zeros_like(keep_ref)
        first = KMAX - SPARE
        left, right = shares[1][:, SPARE:HALF], shares[-1][:, SPARE:HALF]
        at_right = z.lon - (z.ext - 128)

        def rimmed(ref, left_of, right_of):
            x = widen(z, flat_rows(z, ref))
            tail = x[:, z.ext - 128 :]
            for n, lane in enumerate(right_of):
                tail = put_lane(tail, at_right + n, right[:, first + lane : first + lane + 1])
            for n, lane in enumerate(left_of):
                tail = put_lane(tail, 127 - n, left[:, first + lane : first + lane + 1])
            return jnp.concatenate([x[:, : z.ext - 128], tail], axis=1)

        g = rimmed(g_ref, (1, 0), (4, 5))
        we, wn = rimmed(we_ref, (2,), (6,)), rimmed(wn_ref, (3,), (7,))
        rows_ref[...] = we - coef * east_diff(g) + CORIOLIS * sine * wn

    final = rows_ref[...]
    final_ref[...] = final[:, : z.lon].reshape(final_ref.shape)
    change = depths(z, depth_ref, row_ref) * coef * east_diff(final)[:, : z.lon]
    part_ref[...] = flat_rows(z, thick_ref) - change


def send_spectra(z, east_ref, *rest):
    shares, send_ref = rest[:-1], rest[-1]
    kept = shares[0][:, KMAX : KMAX + 1]
    coef = coefficients(z, sum(ref[...] for ref in shares), kept)
    part = sector_part(z, coef, lax.axis_index("lon"))
    send_ref[0] = east_ref[...]
    send_ref[1] = part[: z.helped].reshape(east_ref.shape)


def north_inverse(z, depth_ref, north_ref, part_ref, row_ref, phase_ref, chosen_ref, *rest):
    ahead, shares, rest = rest[: z.n_lon], rest[z.n_lon : 2 * z.n_lon], rest[2 * z.n_lon :]
    basis_ref, final_ref, thick_ref, column_ref, keep_ref, lhs_ref, sums_ref, rows_ref = rest

    @pl.when(on_polar_band(z))
    def _():
        sums_ref[: z.ahead] = sum(ref[...] for ref in ahead)
        sums_ref[z.ahead : z.rows] = sum(ref[...] for ref in shares)
        sums_ref[z.rows :] = jnp.zeros((sums_ref.shape[0] - z.rows, WIDE), jnp.float32)
        sums = sums_ref[...]
        kept = [ahead[0][:, KMAX : KMAX + 1], shares[0][:, KMAX : KMAX + 1]]
        waves = coefficients(z, sums, pad_rows(jnp.concatenate(kept, axis=0), sums.shape[0]))
        part = sector_part(z, waves, lax.axis_index("lon"))
        keep_ref[...] = part[z.helped : 2 * z.helped].reshape(keep_ref.shape)
        high = waves.astype(jnp.bfloat16)
        low = (waves - high.astype(jnp.float32)).astype(jnp.bfloat16)
        chosen = chosen_ref[...].astype(jnp.bfloat16)
        waves = jnp.dot(chosen, high, preferred_element_type=jnp.float32) + jnp.dot(
            chosen, low, preferred_element_type=jnp.float32
        )
        inverse_rows(z, waves, basis_ref, phase_ref, lhs_ref, rows_ref)
        beyond = slice(z.own, z.rows)
        polar = column_of(row_ref, POLAR)[beyond] > 0.0
        rows_ref[beyond, : z.lon] = jnp.where(polar, rows_ref[beyond, : z.lon], north_ref[beyond])

    @pl.when(jnp.logical_not(on_polar_band(z)))
    def _():
        keep_ref[...] = jnp.zeros_like(keep_ref)
        beyond = slice(z.own, z.rows)
        at = slice(z.own - z.ahead, z.rows - z.ahead)
        waves = coefficients(z, sum(ref[at] for ref in shares), shares[0][at, KMAX : KMAX + 1])
        inverse_rows(z, waves, basis_ref, phase_ref, lhs_ref, rows_ref, beyond)
        polar = column_of(row_ref, POLAR)[beyond] > 0.0
        rows_ref[beyond, : z.lon] = jnp.where(polar, rows_ref[beyond, : z.lon], north_ref[beyond])
        rows_ref[: z.own, : z.lon] = north_ref[: z.own]

    final = rows_ref[:, : z.lon]
    final_ref[...] = final[: z.own].reshape(final_ref.shape)
    scaled = final * column_of(row_ref, COSINE)
    diff = (roll(scaled, -z.lev, 0) - roll(scaled, z.lev, 0))[: z.own]
    scale = depths(z, depth_ref, row_ref) * column_of(row_ref, NORTH_COEF)[: z.own]
    thick_ref[...] = (part_ref[...] - scale * diff).reshape(thick_ref.shape)
    column_ref[...] = sum(thick_ref[:, lev, :] for lev in range(z.lev))


def join_spectra(z, east_ref, north_ref, arrived_ref, spectra_ref):
    polar = on_polar_band(z)
    spectra_ref[0] = jnp.where(polar, east_ref[...], arrived_ref[0])
    spectra_ref[1] = jnp.where(polar, north_ref[...], arrived_ref[1])


def close(z, thick_ref, surface_ref, spectra_ref, *rest):
    del spectra_ref
    deeper, geo_ref = rest[:-1], rest[-1]
    column = sum(ref[...] for ref in deeper) if deeper else 0.0
    for lev in reversed(range(z.lev)):
        column = column + thick_ref[:, lev, :]
        geo_ref[:, lev, :] = surface_ref[...] + GRAVITY * column


def call(kernel, n_in, out_shape, scratch, micros, spaces=None, vmem=24):
    vmem_spec = pl.BlockSpec(memory_space=pltpu.VMEM)
    spaces = spaces or {}
    return pl.pallas_call(
        kernel,
        in_specs=[
            pl.BlockSpec(memory_space=spaces[n]) if n in spaces else vmem_spec for n in range(n_in)
        ],
        out_specs=[vmem_spec] * len(out_shape),
        out_shape=[
            jax.ShapeDtypeStruct(s, jnp.float32) if isinstance(s, tuple) else s for s in out_shape
        ],
        scratch_shapes=scratch,
        compiler_params=pltpu.CompilerParams(vmem_limit_bytes=vmem * MIB),
        cost_estimate=pl.CostEstimate(
            flops=int(micros * 1.15e9), bytes_accessed=0, transcendentals=0
        ),
    )


def shifted(block, axis, distance):
    count = lax.axis_size(axis)
    return lax.ppermute(block, axis, [(i, (i + distance) % count) for i in range(count)])


def level_inside(x):
    return jnp.swapaxes(x, -3, -2)


def local(
    wind_east, wind_north, thickness, geopot, surface_geopot, mean_depth, kept_modes, slot_table
):
    z = Sizes(thickness.shape, {axis: lax.axis_size(axis) for axis in ("lat", "lon", "lev")})
    wind_east, wind_north, thickness, geopot = (
        level_inside(x) for x in (wind_east, wind_north, thickness, geopot)
    )
    field = (z.lat, z.lev, z.lon)
    forward, inverse = (jnp.asarray(x) for x in basis_tables(z))
    phase = jnp.asarray(phase_table(z))
    per_row = jnp.asarray(row_table(z))
    kept = kept_modes[None, :]
    slots = slot_table[None, :]
    payload = (z.rows, WIDE)
    rims = (4 * z.lev, z.lon)
    spec = (z.help, z.lev, z.spec_width)
    waves_lhs = pltpu.VMEM((z.ext // z.inverse_block * z.mm_rows, 3 * WIDE), jnp.bfloat16)

    row_shape, phase_shape = per_row.shape[1:], phase.shape[1:]
    in_hbm = [
        pltpu.with_memory_space_constraint(x, pltpu.HBM)
        for x in (wind_east, wind_north, geopot, per_row, phase, forward)
    ]
    columns_lhs = pltpu.VMEM((z.blocks * z.mm_rows, 3 * BLOCK), jnp.bfloat16)
    waves_lhs = pltpu.VMEM((z.ext // z.inverse_block * z.mm_rows, 3 * WIDE), jnp.bfloat16)

    east_share, to_even, to_odd, wind_east, wind_north, geopot, per_row, phase, forward = call(
        functools.partial(east_forward, z),
        6,
        [(z.own, WIDE), rims, rims]
        + [field, field, field, row_shape, phase_shape]
        + [jax.ShapeDtypeStruct(forward.shape, forward.dtype)],
        [columns_lhs, pltpu.SemaphoreType.DMA((6,))],
        4,
        {n: pltpu.HBM for n in range(6)},
    )(*in_hbm)
    east_shares = [east_share] + [shifted(east_share, "lon", s) for s in range(1, z.n_lon)]
    met = []
    for start, rim in enumerate((to_even, to_odd)):
        pairs = [(i, i + 1) for i in range(start, z.n_lat - 1, 2)]
        met.append(lax.ppermute(rim, "lat", pairs + [(b, a) for a, b in pairs]))

    places = round_up(z.rows, 128)
    north_ahead, north_rest, north_new, chosen = call(
        functools.partial(north_forward, z),
        10,
        [(z.ahead, WIDE), (z.rows - z.ahead, WIDE), (z.rows, z.lon), (z.rows, places)],
        [
            pltpu.VMEM((z.rows, z.lon), jnp.float32),
            columns_lhs,
            pltpu.VMEM((z.rows, WIDE), jnp.float32),
        ],
        0.2,
    )(wind_east, wind_north, geopot, *met, per_row, phase, forward, kept, slots)
    north_aheads, north_rests = (
        [x] + [shifted(x, "lon", s) for s in range(1, z.n_lon)] for x in (north_ahead, north_rest)
    )

    east_final, thick_part, east_keep, east_send = call(
        functools.partial(east_inverse, z),
        10 + z.n_lon,
        [field, (z.own, z.lon), spec, spec],
        [waves_lhs, pltpu.VMEM((z.own, z.ext), jnp.float32)],
        1,
        {0: pltpu.SMEM},
    )(
        mean_depth, wind_east, wind_north, geopot, thickness, per_row, phase, kept, chosen,
        *east_shares, inverse,
    )

    polar_bands = [i for i in range(z.n_lat) if i < z.n_lat // 4 or i >= z.n_lat - z.n_lat // 4]
    (to_helper,) = call(
        functools.partial(send_spectra, z), 1 + z.n_lon, [(2, *spec)], [], 0.1
    )(east_send, *north_aheads)
    arrived = lax.ppermute(
        to_helper, "lat", [(i, (i + z.half_axis) % z.n_lat) for i in polar_bands]
    )

    north_final, thick_new, column, north_keep = call(
        functools.partial(north_inverse, z),
        7 + 2 * z.n_lon,
        [field, field, (z.lat, z.lon), spec],
        [
            waves_lhs,
            pltpu.VMEM((places, WIDE), jnp.float32),
            pltpu.VMEM((z.rows, z.ext), jnp.float32),
        ],
        2,
        {0: pltpu.SMEM},
    )(
        mean_depth, north_new, thick_part, per_row, phase, chosen,
        *north_aheads, *north_rests, inverse,
    )

    deeper = [
        lax.ppermute(column, "lev", [(i, i - distance) for i in range(distance, z.n_lev)])
        for distance in range(1, z.n_lev)
    ]
    (spectra,) = call(functools.partial(join_spectra, z), 3, [(2, *spec)], [], 4.2)(
        east_keep, north_keep, arrived
    )
    (geo_new,) = call(functools.partial(close, z), 3 + len(deeper), [field], [], 1)(
        thick_new, surface_geopot, spectra, *deeper
    )
    return tuple(level_inside(x) for x in (east_final, north_final, thick_new, geo_new, spectra))


def solution(mesh):
    field = P(("members", "lev"), "lat", "lon")
    return jax.shard_map(
        local,
        mesh=mesh,
        in_specs=(field, field, field, field, P("lat", "lon"), P("lev"), P(), P()),
        out_specs=(field, field, field, field, P(None, ("members", "lev"), "lat", "lon")),
        check_vma=False,
    )
```

```python
import functools
import math

import jax
import jax.numpy as jnp
import numpy as np
from jax import lax
from jax.experimental import pallas as pl
from jax.experimental.pallas import tpu as pltpu
from jax.sharding import PartitionSpec as P

KMAX = 360
HALF = 384
WIDE = 2 * HALF
SPARE = HALF - 128
BLOCK = 256
INVERSE_BLOCK = 768

STEP_FACTOR = 0.15
CORIOLIS = 0.2
GRAVITY = 0.25

MIB = 1024 * 1024

EAST_COEF, SINE, COSINE, NORTH_COEF, LEVEL, POLAR, NUMBER, OWN = range(8)


def round_up(value, step):
    return -(-value // step) * step


class Sizes:
    def __init__(self, shape, counts):
        self.lev, self.lat, self.lon = shape
        self.n_lat, self.n_lon, self.n_lev = counts["lat"], counts["lon"], counts["lev"]
        self.nlat, self.nlon = self.lat * self.n_lat, self.lon * self.n_lon
        self.polar = self.nlat // 4
        self.help = self.lat // 2
        self.half_axis = self.n_lat // 2
        self.own = self.lat * self.lev
        self.rows = self.own + 2 * self.lev
        assert self.rows % 8 == 0
        self.mm_rows = round_up(self.rows, 16)
        self.ext = round_up(self.lon + 4, BLOCK)
        self.blocks = self.ext // BLOCK
        self.inverse_block = min(INVERSE_BLOCK, self.ext)
        assert self.ext % self.inverse_block == 0
        self.spec_width = 2 * KMAX // self.n_lon
        self.helped = self.help * self.lev
        self.ahead = round_up(self.helped, 16)
        self.first = min(round_up(self.own * 4 // 9, 8 * self.lev), self.own)


def high_low(x):
    x = x.astype(np.float32)
    high = x.astype(jnp.bfloat16)
    return high, (x - high.astype(np.float32)).astype(jnp.bfloat16)


def basis_tables(z):
    k = np.arange(KMAX)
    angle = (np.arange(z.inverse_block)[:, None] * k[None, :] % z.nlon) * (2.0 * np.pi / z.nlon)
    full = np.zeros((z.inverse_block, WIDE))
    full[:, :KMAX] = np.cos(angle)
    full[:, HALF : HALF + KMAX] = np.sin(angle)
    high, low = high_low(full)
    forward = np.concatenate([high[:BLOCK], high[:BLOCK], low[:BLOCK]], axis=0)
    inverse = np.concatenate([high.T, high.T, low.T], axis=0)
    return forward, inverse


def phase_table(z):
    k = np.arange(KMAX)
    table = np.zeros((z.n_lon, round_up(2 * z.blocks + 2, 8), HALF), np.float32)
    for place in range(z.n_lon):
        for n, column in enumerate([*range(0, z.ext, BLOCK), -1]):
            angle = ((place * z.lon + column) * k % z.nlon) * (2.0 * np.pi / z.nlon)
            table[place, 2 * n, :KMAX] = np.cos(angle)
            table[place, 2 * n + 1, :KMAX] = np.sin(angle)
    return table


def row_table(z):
    lam_step = np.float32(2.0 * math.pi / z.nlon)
    phi_step = np.float32(math.pi / z.nlat)
    latitude = np.float32(-0.5 * math.pi) + (
        np.arange(z.nlat, dtype=np.float32) + np.float32(0.5)
    ) * phi_step
    cosine = np.cos(latitude.astype(np.float64)).astype(np.float32)
    sine = np.sin(latitude.astype(np.float64)).astype(np.float32)
    north_coef = np.float32(STEP_FACTOR) * lam_step / phi_step
    table = np.zeros((z.n_lat, z.rows, 8), np.float32)
    for place in range(z.n_lat):
        for flat in range(z.rows):
            inner, level = flat // z.lev, flat % z.lev
            inner = -1 if inner == z.lat + 1 else inner
            row = place * z.lat + inner
            one = table[place, flat]
            one[LEVEL], one[NUMBER] = level, -1
            one[OWN] = 0 <= inner < z.lat
            if 0 <= row < z.nlat:
                one[EAST_COEF] = np.float32(STEP_FACTOR) / cosine[row]
                one[SINE], one[COSINE] = sine[row], cosine[row]
                one[NORTH_COEF] = north_coef / cosine[row]
                if row < z.polar:
                    one[POLAR], one[NUMBER] = 1, row
                elif row >= z.nlat - z.polar:
                    one[POLAR], one[NUMBER] = 1, row - (z.nlat - 2 * z.polar)
    return table


def on_polar_band(z):
    lat_index = lax.axis_index("lat")
    return (lat_index < z.n_lat // 4) | (lat_index >= z.n_lat - z.n_lat // 4)


def split(x):
    high = x.astype(jnp.bfloat16)
    return high, (x - high.astype(jnp.float32)).astype(jnp.bfloat16)


def store_split(lhs_ref, first_row, x):
    rows, width = x.shape
    high, low = split(x)
    at = slice(first_row, first_row + rows)
    lhs_ref[at, :width] = high
    lhs_ref[at, width : 2 * width] = low
    lhs_ref[at, 2 * width :] = high


def pad_rows(x, rows):
    if x.shape[0] == rows:
        return x
    return jnp.concatenate([x, jnp.zeros((rows - x.shape[0], x.shape[1]), x.dtype)], axis=0)


def phase_of(phase_ref, n):
    return phase_ref[2 * n : 2 * n + 1], phase_ref[2 * n + 1 : 2 * n + 2]


def forward_sums(
    z, x, basis_ref, phase_ref, lhs_ref, out_ref, at=slice(None), basis_here=None
):
    count = round_up(x.shape[0], 16)
    for block in range(z.blocks):
        part = pad_rows(x[:, block * BLOCK : (block + 1) * BLOCK], count)
        store_split(lhs_ref, block * count, part)
    lhs = lhs_ref[: z.blocks * count]
    if basis_here is not None:
        basis_here()
    sums = jnp.dot(lhs, basis_ref[...], preferred_element_type=jnp.float32)
    real = imag = None
    for block in range(z.blocks):
        cos, sin = phase_of(phase_ref, block)
        part = sums[block * count : block * count + x.shape[0]]
        a, b = part[:, :HALF], part[:, HALF:]
        more_real, more_imag = a * cos - b * sin, a * sin + b * cos
        real = more_real if real is None else real + more_real
        imag = more_imag if imag is None else imag + more_imag
    out_ref[at, :HALF] = real
    out_ref[at, HALF:] = imag


def inverse_rows(z, coef, basis_ref, phase_ref, lhs_ref, out_ref, at=slice(None)):
    a, b = coef[:, :HALF], coef[:, HALF:]
    count, width = round_up(coef.shape[0], 16), z.inverse_block
    blocks = range(z.ext // width)
    for block in blocks:
        cos, sin = phase_of(phase_ref, block * width // BLOCK)
        turned = jnp.concatenate([a * cos + b * sin, b * cos - a * sin], axis=1)
        store_split(lhs_ref, block * count, pad_rows(turned, count))
    lhs = lhs_ref[: len(blocks) * count]
    rows = jnp.dot(lhs, basis_ref[...], preferred_element_type=jnp.float32)
    for block in blocks:
        out_ref[at, block * width : (block + 1) * width] = rows[
            block * count : block * count + coef.shape[0]
        ]


def roll(x, shift, axis):
    return pltpu.roll(x, shift % x.shape[axis], axis)


def east_diff(x):
    return roll(x, -1, 1) - roll(x, 1, 1)


def flat_rows(z, ref):
    return ref[...].reshape(z.own, ref.shape[2])


def widen(z, x):
    return jnp.concatenate([x, jnp.zeros((x.shape[0], z.ext - x.shape[1]), x.dtype)], axis=1)


def put_lane(x, at, column):
    lane = lax.broadcasted_iota(jnp.int32, x.shape, 1)
    return jnp.where(lane == at, column, x)


def column_of(row_ref, which):
    return row_ref[:, which : which + 1]


def north_factor(z):
    return STEP_FACTOR * (2.0 * math.pi / z.nlon) / (math.pi / z.nlat)


def look_up(number, table_ref):
    table = table_ref[...].astype(jnp.float32)
    lane = lax.broadcasted_iota(jnp.int32, (number.shape[0], table.shape[1]), 1)
    return jnp.sum(jnp.where(lane == number, table, 0.0), axis=1, keepdims=True)


def coefficients(z, sums, kept):
    lane = lax.broadcasted_iota(jnp.int32, (1, WIDE), 1)
    k = jnp.where(lane < HALF, lane, lane - HALF)
    weight = jnp.where(k == 0, 1.0 / z.nlon, 2.0 / z.nlon).astype(jnp.float32)
    keep = (k.astype(jnp.float32) < kept) & (k < KMAX)
    return jnp.where(keep, sums * weight, 0.0)


def slot_order(z, number, row_ref, slot_ref):
    lat_index = lax.axis_index("lat")
    slot = look_up(number, slot_ref).astype(jnp.int32)
    theirs = slot - lax.rem(lat_index + z.half_axis, z.n_lat) * z.help
    mine = slot - lat_index * z.help
    level = column_of(row_ref, LEVEL).astype(jnp.int32)
    flat = lax.broadcasted_iota(jnp.int32, slot.shape, 0)
    place = jnp.where((mine >= 0) & (mine < z.help), z.helped + mine * z.lev + level, -1)
    place = jnp.where((theirs >= 0) & (theirs < z.help), theirs * z.lev + level, place)
    place = jnp.where(number >= 0, place, -1)
    place = jnp.where(flat < z.own, place, flat)
    lane = lax.broadcasted_iota(jnp.int32, (z.rows, round_up(z.rows, 128)), 1)
    return (lane == place).astype(jnp.float32)


def reorder(chosen, values):
    high, low = (
        lax.dot_general(
            chosen.astype(jnp.bfloat16),
            part,
            (((0,), (0,)), ((), ())),
            preferred_element_type=jnp.float32,
        )
        for part in split(values)
    )
    return high + low


def sector_part(z, coef, place):
    part = None
    for one in range(z.n_lon):
        first = one * z.spec_width
        first = first if first < KMAX else first - KMAX + HALF
        this = coef[:, first : first + z.spec_width]
        part = this if part is None else jnp.where(place == one, this, part)
    return part


def depths(z, depth_ref, row_ref):
    level = column_of(row_ref, LEVEL)[: z.own]
    depth = jnp.zeros_like(level)
    for lev in range(z.lev):
        depth = jnp.where(level == lev, depth_ref[lev], depth)
    return depth


def store_rims(z, ref, g, we, wn, last):
    edge = 2 * z.lev
    ref[:edge] = g[z.own - edge :] if last else g[:edge]
    ref[edge : edge + z.lev] = we[z.own - z.lev :] if last else we[: z.lev]
    ref[edge + z.lev :] = wn[z.own - z.lev :] if last else wn[: z.lev]


def east_shares_of(
    z, at, we_ref, wn_ref, g_ref, row_ref, phase_ref, basis_ref, share_ref, lhs_ref, basis_here=None
):
    inner = slice(at.start // z.lev, at.stop // z.lev)
    g, we, wn = (ref[inner].reshape(at.stop - at.start, z.lon) for ref in (g_ref, we_ref, wn_ref))

    @pl.when(on_polar_band(z))
    def _():
        coef, sine = column_of(row_ref, EAST_COEF)[at], column_of(row_ref, SINE)[at]
        new = widen(z, we + CORIOLIS * sine * wn) - coef * east_diff(widen(z, g))
        tail = put_lane(new[:, z.ext - 128 :], 127, 0.0)
        new = jnp.concatenate([new[:, : z.ext - 128], tail], axis=1)
        forward_sums(z, new, basis_ref, phase_ref, lhs_ref, share_ref, basis_here=basis_here)
        cos, sin = phase_of(phase_ref, z.blocks)
        before = -coef * g[:, 0:1]
        share_ref[:, :HALF] += before * cos
        share_ref[:, HALF:] += before * sin

    @pl.when(jnp.logical_not(on_polar_band(z)))
    def _():
        if basis_here is not None:
            basis_here()
        share_ref[...] = jnp.zeros_like(share_ref)

    last = z.lon - 1
    spare = share_ref[:, SPARE:HALF]
    edges = ((g, last - 1), (g, last), (we, last), (wn, last), (g, 0), (g, 1), (we, 0), (wn, 0))
    for n, (x, column) in enumerate(edges):
        spare = put_lane(spare, KMAX - SPARE + n, x[:, column : column + 1])
    share_ref[:, SPARE:HALF] = spare


def east_first(
    z, we_hbm, wn_hbm, g_hbm, row_hbm, phase_hbm, basis_hbm,
    share_ref, even_ref, odd_ref, we_ref, wn_ref, g_ref, row_ref, phase_ref, basis_ref, lhs_ref, sems,
):
    fields = ((g_hbm, g_ref), (we_hbm, we_ref), (wn_hbm, wn_ref))
    cut, rim = z.first // z.lev, z.lat - 2

    def copies(first_sem, pairs):
        return [pltpu.make_async_copy(*pair, sems.at[first_sem + n]) for n, pair in enumerate(pairs)]

    tables = copies(
        0,
        (
            (row_hbm.at[lax.axis_index("lat")], row_ref),
            (phase_hbm.at[lax.axis_index("lon")], phase_ref),
        ),
    )
    first = copies(2, [(a.at[:cut], b.at[:cut]) for a, b in fields])
    basis = copies(5, [(basis_hbm, basis_ref)])
    edge = copies(6, [(a.at[rim:], b.at[rim:]) for a, b in fields])
    between = copies(9, [(a.at[cut:rim], b.at[cut:rim]) for a, b in fields])
    for copy in first + tables + basis + edge:
        copy.start()
    for copy in first + tables:
        copy.wait()

    def basis_here():
        for copy in basis + edge:
            copy.wait()
        for copy in between:
            copy.start()

    east_shares_of(
        z, slice(0, z.first), we_ref, wn_ref, g_ref, row_ref, phase_ref, basis_ref, share_ref, lhs_ref,
        basis_here,
    )
    odd = lax.rem(lax.axis_index("lat"), 2) == 1
    last, flat = z.lat - 1, (z.lev, z.lon)
    far = (g_ref[last - 1], g_ref[last], we_ref[last], wn_ref[last])
    near = (g_ref[0], g_ref[1], we_ref[0], wn_ref[0])
    for n, (bottom, top) in enumerate(zip(far, near, strict=True)):
        at = slice(n * z.lev, (n + 1) * z.lev)
        even_ref[at] = jnp.where(odd, top, bottom).reshape(flat)
        odd_ref[at] = jnp.where(odd, bottom, top).reshape(flat)
    for copy in between:
        copy.wait()


def north_forward(
    z, we_ref, wn_ref, g_ref, even_ref, odd_ref, row_ref, phase_ref, basis_ref, kept_ref, slot_ref, *rest
):
    ahead_ref, rest_ref, north_ref, chosen_ref, g_rows, lhs_ref, share_ref = rest
    edge, lev = 2 * z.lev, z.lev
    odd = lax.rem(lax.axis_index("lat"), 2) == 1
    below = jnp.where(odd, odd_ref[...], even_ref[...])
    above = jnp.where(odd, even_ref[...], odd_ref[...])
    coef, sine = north_factor(z), CORIOLIS * column_of(row_ref, SINE)
    own = flat_rows(z, g_ref)
    g_rows[: z.own] = own
    g_rows[z.own : z.own + lev] = below[:lev]
    g_rows[z.own + lev :] = above[lev:edge]
    g = g_rows[...]
    diff = (roll(g, -lev, 0) - roll(g, lev, 0))[: z.own]
    north_ref[: z.own] = flat_rows(z, wn_ref) - coef * diff - sine[: z.own] * flat_rows(z, we_ref)
    for at, diff, rim in (
        (z.own, below[lev:edge] - own[z.own - lev :], below),
        (z.own + lev, own[:lev] - above[:lev], above),
    ):
        we, wn = rim[edge : edge + lev], rim[edge + lev :]
        north_ref[at : at + lev] = wn - coef * diff - sine[at : at + lev] * we
    number = column_of(row_ref, NUMBER).astype(jnp.int32)
    kept = look_up(number, kept_ref)

    @pl.when(on_polar_band(z))
    def _():
        forward_sums(z, widen(z, north_ref[...]), basis_ref, phase_ref, lhs_ref, share_ref)
        share_ref[:, SPARE:HALF] = put_lane(share_ref[:, SPARE:HALF], KMAX - SPARE, kept)
        chosen = slot_order(z, number, row_ref, slot_ref)
        ordered = reorder(chosen, share_ref[...])
        ahead_ref[...] = ordered[: z.ahead]
        rest_ref[...] = ordered[z.ahead : z.rows]
        chosen_ref[...] = chosen

    @pl.when(jnp.logical_not(on_polar_band(z)))
    def _():
        beyond = slice(z.own - z.ahead, z.rows - z.ahead)
        ahead_ref[...] = jnp.zeros_like(ahead_ref)
        rest_ref[...] = jnp.zeros_like(rest_ref)
        chosen_ref[...] = jnp.zeros_like(chosen_ref)
        rows = widen(z, north_ref[z.own :])
        forward_sums(z, rows, basis_ref, phase_ref, lhs_ref, rest_ref, beyond)
        rest_ref[beyond, SPARE:HALF] = put_lane(
            rest_ref[beyond, SPARE:HALF], KMAX - SPARE, kept[z.own :]
        )


def arrival(arrived_ref, out_ref):
    out_ref[...] = arrived_ref[:8, :128]


def east_inverse(
    z, depth_ref, we_ref, wn_ref, g_ref, thick_ref, row_ref, phase_ref, kept_ref, chosen_ref, first_here,
    *rest,
):
    del first_here
    firsts, seconds, rest = rest[: z.n_lon], rest[z.n_lon : 2 * z.n_lon], rest[2 * z.n_lon :]
    basis_ref, final_ref, part_ref, keep_ref, send_ref, lhs_ref, rows_ref, sums_ref = rest
    coef, sine = column_of(row_ref, EAST_COEF)[: z.own], column_of(row_ref, SINE)[: z.own]

    @pl.when(on_polar_band(z))
    def _():
        number = column_of(row_ref, NUMBER)[: z.own].astype(jnp.int32)
        sums_ref[: z.first] = sum(ref[...] for ref in firsts)
        sums_ref[z.first :] = sum(ref[...] for ref in seconds)
        waves = coefficients(z, sums_ref[...], look_up(number, kept_ref))
        part = sector_part(z, waves, lax.axis_index("lon"))
        ordered = reorder(chosen_ref[: z.own], part)
        send_ref[...] = ordered[: z.helped].reshape(send_ref.shape)
        keep_ref[...] = ordered[z.helped : 2 * z.helped].reshape(keep_ref.shape)
        inverse_rows(z, waves, basis_ref, phase_ref, lhs_ref, rows_ref)
        cos, sin = phase_of(phase_ref, z.blocks)
        before = jnp.sum(waves[:, :HALF] * cos + waves[:, HALF:] * sin, axis=1, keepdims=True)
        rows_ref[:, z.ext - 128 :] = put_lane(rows_ref[:, z.ext - 128 :], 127, before)

    @pl.when(jnp.logical_not(on_polar_band(z)))
    def _():
        send_ref[...] = jnp.zeros_like(send_ref)
        keep_ref[...] = jnp.zeros_like(keep_ref)
        first = KMAX - SPARE
        left, right = (
            jnp.concatenate([firsts[n][:, SPARE:HALF], seconds[n][:, SPARE:HALF]], axis=0)
            for n in (1, -1)
        )
        at_right = z.lon - (z.ext - 128)

        def rimmed(ref, left_of, right_of):
            x = widen(z, flat_rows(z, ref))
            tail = x[:, z.ext - 128 :]
            for n, lane in enumerate(right_of):
                tail = put_lane(tail, at_right + n, right[:, first + lane : first + lane + 1])
            for n, lane in enumerate(left_of):
                tail = put_lane(tail, 127 - n, left[:, first + lane : first + lane + 1])
            return jnp.concatenate([x[:, : z.ext - 128], tail], axis=1)

        g = rimmed(g_ref, (1, 0), (4, 5))
        we, wn = rimmed(we_ref, (2,), (6,)), rimmed(wn_ref, (3,), (7,))
        rows_ref[...] = we - coef * east_diff(g) + CORIOLIS * sine * wn

    final = rows_ref[...]
    final_ref[...] = final[:, : z.lon].reshape(final_ref.shape)
    change = depths(z, depth_ref, row_ref) * coef * east_diff(final)[:, : z.lon]
    part_ref[...] = flat_rows(z, thick_ref) - change


def send_spectra(z, east_ref, *rest):
    shares, send_ref = rest[:-1], rest[-1]
    kept = shares[0][:, KMAX : KMAX + 1]
    coef = coefficients(z, sum(ref[...] for ref in shares), kept)
    part = sector_part(z, coef, lax.axis_index("lon"))
    send_ref[0] = east_ref[...]
    send_ref[1] = part[: z.helped].reshape(east_ref.shape)


def ahead_inverse(z, phase_ref, *rest):
    shares, (basis_ref, high_ref, low_ref, lhs_ref, rows_ref) = rest[: z.n_lon], rest[z.n_lon :]

    @pl.when(on_polar_band(z))
    def _():
        kept = shares[0][:, KMAX : KMAX + 1]
        waves = coefficients(z, sum(ref[...] for ref in shares), kept)
        inverse_rows(z, waves, basis_ref, phase_ref, lhs_ref, rows_ref)
        high_ref[...], low_ref[...] = split(rows_ref[...])


def north_inverse(
    z, depth_ref, north_ref, part_ref, row_ref, phase_ref, chosen_ref, high_ahead, low_ahead, *rest
):
    ahead, shares, rest = rest[: z.n_lon], rest[z.n_lon : 2 * z.n_lon], rest[2 * z.n_lon :]
    basis_ref, final_ref, thick_ref, column_ref, keep_ref, lhs_ref, rows_ref, high_ref, low_ref = rest

    @pl.when(on_polar_band(z))
    def _():
        more = z.ahead - 8
        kept = [ahead[0][more:, KMAX : KMAX + 1], shares[0][:, KMAX : KMAX + 1]]
        sums = [sum(ref[more:] for ref in ahead), sum(ref[...] for ref in shares)]
        waves = coefficients(z, jnp.concatenate(sums, axis=0), jnp.concatenate(kept, axis=0))
        part = sector_part(z, waves, lax.axis_index("lon"))
        first = z.helped - more
        keep_ref[...] = part[first : first + z.helped].reshape(keep_ref.shape)
        inverse_rows(z, waves[8:], basis_ref, phase_ref, lhs_ref, rows_ref, slice(z.rows - z.ahead))
        count = high_ref.shape[0] - z.ahead
        rest_high, rest_low = split(pad_rows(rows_ref[: z.rows - z.ahead], count))
        high_ref[: z.ahead], low_ref[: z.ahead] = high_ahead[...], low_ahead[...]
        high_ref[z.ahead :], low_ref[z.ahead :] = rest_high, rest_low
        chosen = chosen_ref[...].astype(jnp.bfloat16)
        rows_ref[...] = jnp.dot(
            chosen, high_ref[...], preferred_element_type=jnp.float32
        ) + jnp.dot(chosen, low_ref[...], preferred_element_type=jnp.float32)
        beyond = slice(z.own, z.rows)
        polar = column_of(row_ref, POLAR)[beyond] > 0.0
        rows_ref[beyond, : z.lon] = jnp.where(polar, rows_ref[beyond, : z.lon], north_ref[beyond])

    @pl.when(jnp.logical_not(on_polar_band(z)))
    def _():
        keep_ref[...] = jnp.zeros_like(keep_ref)
        beyond = slice(z.own, z.rows)
        at = slice(z.own - z.ahead, z.rows - z.ahead)
        waves = coefficients(z, sum(ref[at] for ref in shares), shares[0][at, KMAX : KMAX + 1])
        inverse_rows(z, waves, basis_ref, phase_ref, lhs_ref, rows_ref, beyond)
        polar = column_of(row_ref, POLAR)[beyond] > 0.0
        rows_ref[beyond, : z.lon] = jnp.where(polar, rows_ref[beyond, : z.lon], north_ref[beyond])
        rows_ref[: z.own, : z.lon] = north_ref[: z.own]

    final = rows_ref[:, : z.lon]
    final_ref[...] = final[: z.own].reshape(final_ref.shape)
    scaled = final * column_of(row_ref, COSINE)
    diff = (roll(scaled, -z.lev, 0) - roll(scaled, z.lev, 0))[: z.own]
    scale = depths(z, depth_ref, row_ref) * column_of(row_ref, NORTH_COEF)[: z.own]
    thick_ref[...] = (part_ref[...] - scale * diff).reshape(thick_ref.shape)
    column_ref[...] = sum(thick_ref[:, lev, :] for lev in range(z.lev))


def store_results(z, east_keep, north_keep, arrived_ref, surface_ref, *rest):
    fields, outs = rest[:2], rest[2:4]
    spectra_ref, geo_ref, sems = rest[4:]
    copies = [
        pltpu.make_async_copy(*pair, sems.at[n])
        for n, pair in enumerate(zip(fields, outs, strict=True))
    ]
    for copy in copies:
        copy.start()
    column = None
    for lev in reversed(range(z.lev)):
        one = fields[1][:, lev, :]
        column = one if column is None else column + one
        geo_ref[:, lev, :] = surface_ref[...] + GRAVITY * column
    polar = on_polar_band(z)
    spectra_ref[0] = jnp.where(polar, east_keep[...], arrived_ref[0])
    spectra_ref[1] = jnp.where(polar, north_keep[...], arrived_ref[1])
    for copy in copies:
        copy.wait()


def add_deeper(z, own_ref, *rest):
    deeper, geo_ref = rest[:-1], rest[-1]
    deeper = GRAVITY * sum(ref[...] for ref in deeper)
    for lev in range(z.lev):
        geo_ref[:, lev, :] = own_ref[:, lev, :] + deeper


def call(kernel, n_in, out_shape, scratch, micros, spaces=None, in_hbm=0, vmem=24):
    vmem_spec = pl.BlockSpec(memory_space=pltpu.VMEM)
    spaces = spaces or {}
    return pl.pallas_call(
        kernel,
        in_specs=[
            pl.BlockSpec(memory_space=spaces[n]) if n in spaces else vmem_spec for n in range(n_in)
        ],
        out_specs=[pl.BlockSpec(memory_space=pltpu.HBM)] * in_hbm
        + [vmem_spec] * (len(out_shape) - in_hbm),
        out_shape=[
            jax.ShapeDtypeStruct(s, jnp.float32) if isinstance(s, tuple) else s for s in out_shape
        ],
        scratch_shapes=scratch,
        compiler_params=pltpu.CompilerParams(vmem_limit_bytes=vmem * MIB),
        cost_estimate=pl.CostEstimate(
            flops=int(micros * 1.15e9), bytes_accessed=0, transcendentals=0
        ),
    )


def shifted(block, axis, distance):
    count = lax.axis_size(axis)
    return lax.ppermute(block, axis, [(i, (i + distance) % count) for i in range(count)])


def level_inside(x):
    return jnp.swapaxes(x, -3, -2)


def local(
    wind_east, wind_north, thickness, geopot, surface_geopot, mean_depth, kept_modes, slot_table
):
    z = Sizes(thickness.shape, {axis: lax.axis_size(axis) for axis in ("lat", "lon", "lev")})
    wind_east, wind_north, thickness, geopot = (
        level_inside(x) for x in (wind_east, wind_north, thickness, geopot)
    )
    field = (z.lat, z.lev, z.lon)
    forward, inverse = (jnp.asarray(x) for x in basis_tables(z))
    phase = jnp.asarray(phase_table(z))
    per_row = jnp.asarray(row_table(z))
    kept = kept_modes[None, :]
    slots = slot_table[None, :]
    payload = (z.rows, WIDE)
    rims = (4 * z.lev, z.lon)
    spec = (z.help, z.lev, z.spec_width)
    waves_lhs = pltpu.VMEM((z.ext // z.inverse_block * z.mm_rows, 3 * WIDE), jnp.bfloat16)

    row_shape, phase_shape = per_row.shape[1:], phase.shape[1:]
    pinned = [
        pltpu.with_memory_space_constraint(x, pltpu.HBM)
        for x in (wind_east, wind_north, geopot, per_row, phase, forward)
    ]
    columns_lhs = pltpu.VMEM((z.blocks * z.mm_rows, 3 * BLOCK), jnp.bfloat16)
    waves_lhs = pltpu.VMEM((z.ext // z.inverse_block * z.mm_rows, 3 * WIDE), jnp.bfloat16)

    share_first, to_even, to_odd, wind_east, wind_north, geopot, per_row, phase, forward = call(
        functools.partial(east_first, z),
        6,
        [(z.first, WIDE), rims, rims]
        + [pltpu.VMEM(s, jnp.float32) for s in (field, field, field, row_shape, phase_shape)]
        + [pltpu.VMEM(forward.shape, forward.dtype)],
        [columns_lhs, pltpu.SemaphoreType.DMA((12,))],
        1,
        {n: pltpu.HBM for n in range(6)},
    )(*pinned)
    (share_second,) = call(
        functools.partial(east_shares_of, z, slice(z.first, z.own)),
        6,
        [(z.own - z.first, WIDE)],
        [columns_lhs],
        0.18,
    )(wind_east, wind_north, geopot, per_row, phase, forward)
    east_firsts, east_seconds = (
        [x] + [shifted(x, "lon", s) for s in range(1, z.n_lon)] for x in (share_first, share_second)
    )
    met = []
    for start, rim in enumerate((to_even, to_odd)):
        pairs = [(i, i + 1) for i in range(start, z.n_lat - 1, 2)]
        met.append(lax.ppermute(rim, "lat", pairs + [(b, a) for a, b in pairs]))

    places = round_up(z.rows, 128)
    north_ahead, north_rest, north_new, chosen = call(
        functools.partial(north_forward, z),
        10,
        [(z.ahead, WIDE), (z.rows - z.ahead, WIDE), (z.rows, z.lon), (z.rows, places)],
        [
            pltpu.VMEM((z.rows, z.lon), jnp.float32),
            columns_lhs,
            pltpu.VMEM((z.rows, WIDE), jnp.float32),
        ],
        0.8,
    )(
        wind_east, wind_north, geopot, *met, per_row, phase, forward, kept, slots
    )
    north_rests = [north_rest] + [shifted(north_rest, "lon", s) for s in range(1, z.n_lon)]
    polar_bands = [i for i in range(z.n_lat) if i < z.n_lat // 4 or i >= z.n_lat - z.n_lat // 4]
    north_aheads = [north_ahead]
    for distance in range(1, z.n_lon):
        route = [
            (band * z.n_lon + lon, band * z.n_lon + (lon + distance) % z.n_lon)
            for band in polar_bands
            for lon in range(z.n_lon)
        ]
        north_aheads.append(lax.ppermute(north_ahead, ("lat", "lon"), route))

    (first_here,) = call(arrival, 1, [(8, 128)], [], 0.95)(east_firsts[1])
    east_final, thick_part, east_keep, east_send = call(
        functools.partial(east_inverse, z),
        11 + 2 * z.n_lon,
        [field, (z.own, z.lon), spec, spec],
        [
            waves_lhs,
            pltpu.VMEM((z.own, z.ext), jnp.float32),
            pltpu.VMEM((z.own, WIDE), jnp.float32),
        ],
        1,
        {0: pltpu.SMEM},
    )(
        mean_depth, wind_east, wind_north, geopot, thickness, per_row, phase, kept, chosen,
        first_here, *east_firsts, *east_seconds, inverse,
    )

    (to_helper,) = call(
        functools.partial(send_spectra, z), 1 + z.n_lon, [(2, *spec)], [], 0.1
    )(east_send, *north_aheads)
    arrived = lax.ppermute(
        to_helper, "lat", [(i, (i + z.half_axis) % z.n_lat) for i in polar_bands]
    )

    ahead_rows = jax.ShapeDtypeStruct((z.ahead, z.ext), jnp.bfloat16)
    ahead_high, ahead_low = call(
        functools.partial(ahead_inverse, z),
        2 + z.n_lon,
        [ahead_rows] * 2,
        [waves_lhs, pltpu.VMEM((z.ahead, z.ext), jnp.float32)],
        0.5,
    )(phase, *north_aheads, inverse)

    north_final, thick_new, column, north_keep = call(
        functools.partial(north_inverse, z),
        9 + 2 * z.n_lon,
        [pltpu.VMEM(field, jnp.float32)] * 2 + [(z.lat, z.lon), spec],
        [waves_lhs, pltpu.VMEM((z.rows, z.ext), jnp.float32)]
        + [pltpu.VMEM((places, z.ext), jnp.bfloat16)] * 2,
        2,
        {0: pltpu.SMEM},
    )(
        mean_depth, north_new, thick_part, per_row, phase, chosen, ahead_high, ahead_low,
        *north_aheads, *north_rests, inverse,
    )

    deeper = [
        lax.ppermute(column, "lev", [(i, i - distance) for i in range(distance, z.n_lev)])
        for distance in range(1, z.n_lev)
    ]
    north_final, thick_out, spectra, geo_own = call(
        functools.partial(store_results, z),
        6,
        [pltpu.HBM(field, jnp.float32)] * 2 + [(2, *spec), pltpu.VMEM(field, jnp.float32)],
        [pltpu.SemaphoreType.DMA((2,))],
        5,
        in_hbm=2,
    )(east_keep, north_keep, arrived, surface_geopot, north_final, thick_new)
    (geo_new,) = call(functools.partial(add_deeper, z), 1 + len(deeper), [field], [], 1)(
        geo_own, *deeper
    )
    return tuple(level_inside(x) for x in (east_final, north_final, thick_out, geo_new, spectra))


def solution(mesh):
    field = P(("members", "lev"), "lat", "lon")
    return jax.shard_map(
        local,
        mesh=mesh,
        in_specs=(field, field, field, field, P("lat", "lon"), P("lev"), P(), P()),
        out_specs=(field, field, field, field, P(None, ("members", "lev"), "lat", "lon")),
        check_vma=False,
    )
```

```python
import functools
import math

import jax
import jax.numpy as jnp
import numpy as np
from jax import lax
from jax.experimental import pallas as pl
from jax.experimental.pallas import tpu as pltpu
from jax.sharding import PartitionSpec as P

KMAX = 360
HALF = 384
WIDE = 2 * HALF
SPARE = HALF - 128
BLOCK = 256
INVERSE_BLOCK = 768

STEP_FACTOR = 0.15
CORIOLIS = 0.2
GRAVITY = 0.25

MIB = 1024 * 1024

EAST_COEF, SINE, COSINE, NORTH_COEF, LEVEL, POLAR, NUMBER, OWN = range(8)


def round_up(value, step):
    return -(-value // step) * step


class Sizes:
    def __init__(self, shape, counts):
        self.lev, self.lat, self.lon = shape
        self.n_lat, self.n_lon, self.n_lev = counts["lat"], counts["lon"], counts["lev"]
        self.nlat, self.nlon = self.lat * self.n_lat, self.lon * self.n_lon
        self.polar = self.nlat // 4
        self.help = self.lat // 2
        self.half_axis = self.n_lat // 2
        self.own = self.lat * self.lev
        self.rows = self.own + 2 * self.lev
        assert self.rows % 8 == 0
        self.mm_rows = round_up(self.rows, 16)
        self.ext = round_up(self.lon + 4, BLOCK)
        self.blocks = self.ext // BLOCK
        self.inverse_block = min(INVERSE_BLOCK, self.ext)
        assert self.ext % self.inverse_block == 0
        self.spec_width = 2 * KMAX // self.n_lon
        self.helped = self.help * self.lev
        self.ahead = round_up(self.helped, 16)
        self.cuts = 2
        self.first = min(round_up(self.own * 4 // 9, 8 * self.lev), self.own)


def high_low(x):
    x = x.astype(np.float32)
    high = x.astype(jnp.bfloat16)
    return high, (x - high.astype(np.float32)).astype(jnp.bfloat16)


def basis_tables(z):
    k = np.arange(KMAX)
    angle = (np.arange(z.inverse_block)[:, None] * k[None, :] % z.nlon) * (2.0 * np.pi / z.nlon)
    full = np.zeros((z.inverse_block, WIDE))
    full[:, :KMAX] = np.cos(angle)
    full[:, HALF : HALF + KMAX] = np.sin(angle)
    high, low = high_low(full)
    forward = np.concatenate([high[:BLOCK], high[:BLOCK], low[:BLOCK]], axis=0)
    inverse = np.concatenate([high.T, high.T, low.T], axis=0)
    return forward, inverse


def phase_table(z):
    k = np.arange(KMAX)
    table = np.zeros((z.n_lon, round_up(2 * z.blocks + 2, 8), HALF), np.float32)
    for place in range(z.n_lon):
        for n, column in enumerate([*range(0, z.ext, BLOCK), -1]):
            angle = ((place * z.lon + column) * k % z.nlon) * (2.0 * np.pi / z.nlon)
            table[place, 2 * n, :KMAX] = np.cos(angle)
            table[place, 2 * n + 1, :KMAX] = np.sin(angle)
    return table


def row_table(z):
    lam_step = np.float32(2.0 * math.pi / z.nlon)
    phi_step = np.float32(math.pi / z.nlat)
    latitude = np.float32(-0.5 * math.pi) + (
        np.arange(z.nlat, dtype=np.float32) + np.float32(0.5)
    ) * phi_step
    cosine = np.cos(latitude.astype(np.float64)).astype(np.float32)
    sine = np.sin(latitude.astype(np.float64)).astype(np.float32)
    north_coef = np.float32(STEP_FACTOR) * lam_step / phi_step
    table = np.zeros((z.n_lat, z.rows, 8), np.float32)
    for place in range(z.n_lat):
        for flat in range(z.rows):
            inner, level = flat // z.lev, flat % z.lev
            inner = -1 if inner == z.lat + 1 else inner
            row = place * z.lat + inner
            one = table[place, flat]
            one[LEVEL], one[NUMBER] = level, -1
            one[OWN] = 0 <= inner < z.lat
            if 0 <= row < z.nlat:
                one[EAST_COEF] = np.float32(STEP_FACTOR) / cosine[row]
                one[SINE], one[COSINE] = sine[row], cosine[row]
                one[NORTH_COEF] = north_coef / cosine[row]
                if row < z.polar:
                    one[POLAR], one[NUMBER] = 1, row
                elif row >= z.nlat - z.polar:
                    one[POLAR], one[NUMBER] = 1, row - (z.nlat - 2 * z.polar)
    return table


def on_polar_band(z):
    lat_index = lax.axis_index("lat")
    return (lat_index < z.n_lat // 4) | (lat_index >= z.n_lat - z.n_lat // 4)


def split(x):
    high = x.astype(jnp.bfloat16)
    return high, (x - high.astype(jnp.float32)).astype(jnp.bfloat16)


def store_split(lhs_ref, first_row, x):
    rows, width = x.shape
    high, low = split(x)
    at = slice(first_row, first_row + rows)
    lhs_ref[at, :width] = high
    lhs_ref[at, width : 2 * width] = low
    lhs_ref[at, 2 * width :] = high


def pad_rows(x, rows):
    if x.shape[0] == rows:
        return x
    return jnp.concatenate([x, jnp.zeros((rows - x.shape[0], x.shape[1]), x.dtype)], axis=0)


def phase_of(phase_ref, n):
    return phase_ref[2 * n : 2 * n + 1], phase_ref[2 * n + 1 : 2 * n + 2]


def forward_sums(
    z, x, basis_ref, phase_ref, lhs_ref, out_ref, at=slice(None), basis_here=None
):
    count = round_up(x.shape[0], 16)
    for block in range(z.blocks):
        part = pad_rows(x[:, block * BLOCK : (block + 1) * BLOCK], count)
        store_split(lhs_ref, block * count, part)
    lhs = lhs_ref[: z.blocks * count]
    if basis_here is not None:
        basis_here()
    sums = jnp.dot(lhs, basis_ref[...], preferred_element_type=jnp.float32)
    real = imag = None
    for block in range(z.blocks):
        cos, sin = phase_of(phase_ref, block)
        part = sums[block * count : block * count + x.shape[0]]
        a, b = part[:, :HALF], part[:, HALF:]
        more_real, more_imag = a * cos - b * sin, a * sin + b * cos
        real = more_real if real is None else real + more_real
        imag = more_imag if imag is None else imag + more_imag
    out_ref[at, :HALF] = real
    out_ref[at, HALF:] = imag


def inverse_rows(z, coef, basis_ref, phase_ref, lhs_ref, out_ref, at=slice(None)):
    a, b = coef[:, :HALF], coef[:, HALF:]
    count, width = round_up(coef.shape[0], 16), z.inverse_block
    blocks = range(z.ext // width)
    for block in blocks:
        cos, sin = phase_of(phase_ref, block * width // BLOCK)
        turned = jnp.concatenate([a * cos + b * sin, b * cos - a * sin], axis=1)
        store_split(lhs_ref, block * count, pad_rows(turned, count))
    lhs = lhs_ref[: len(blocks) * count]
    rows = jnp.dot(lhs, basis_ref[...], preferred_element_type=jnp.float32)
    for block in blocks:
        out_ref[at, block * width : (block + 1) * width] = rows[
            block * count : block * count + coef.shape[0]
        ]


def roll(x, shift, axis):
    return pltpu.roll(x, shift % x.shape[axis], axis)


def east_diff(x):
    return roll(x, -1, 1) - roll(x, 1, 1)


def flat_rows(z, ref):
    return ref[...].reshape(z.own, ref.shape[2])


def widen(z, x):
    return jnp.concatenate([x, jnp.zeros((x.shape[0], z.ext - x.shape[1]), x.dtype)], axis=1)


def put_lane(x, at, column):
    lane = lax.broadcasted_iota(jnp.int32, x.shape, 1)
    return jnp.where(lane == at, column, x)


def column_of(row_ref, which):
    return row_ref[:, which : which + 1]


def north_factor(z):
    return STEP_FACTOR * (2.0 * math.pi / z.nlon) / (math.pi / z.nlat)


def look_up(number, table_ref):
    table = table_ref[...].astype(jnp.float32)
    lane = lax.broadcasted_iota(jnp.int32, (number.shape[0], table.shape[1]), 1)
    return jnp.sum(jnp.where(lane == number, table, 0.0), axis=1, keepdims=True)


def coefficients(z, sums, kept):
    lane = lax.broadcasted_iota(jnp.int32, (1, WIDE), 1)
    k = jnp.where(lane < HALF, lane, lane - HALF)
    weight = jnp.where(k == 0, 1.0 / z.nlon, 2.0 / z.nlon).astype(jnp.float32)
    keep = (k.astype(jnp.float32) < kept) & (k < KMAX)
    return jnp.where(keep, sums * weight, 0.0)


def slot_order(z, number, row_ref, slot_ref):
    lat_index = lax.axis_index("lat")
    slot = look_up(number, slot_ref).astype(jnp.int32)
    theirs = slot - lax.rem(lat_index + z.half_axis, z.n_lat) * z.help
    mine = slot - lat_index * z.help
    level = column_of(row_ref, LEVEL).astype(jnp.int32)
    flat = lax.broadcasted_iota(jnp.int32, slot.shape, 0)
    place = jnp.where((mine >= 0) & (mine < z.help), z.helped + mine * z.lev + level, -1)
    place = jnp.where((theirs >= 0) & (theirs < z.help), theirs * z.lev + level, place)
    place = jnp.where(number >= 0, place, -1)
    place = jnp.where(flat < z.own, place, flat)
    lane = lax.broadcasted_iota(jnp.int32, (z.rows, round_up(z.rows, 128)), 1)
    return (lane == place).astype(jnp.float32)


def reorder(chosen, values):
    high, low = (
        lax.dot_general(
            chosen.astype(jnp.bfloat16),
            part,
            (((0,), (0,)), ((), ())),
            preferred_element_type=jnp.float32,
        )
        for part in split(values)
    )
    return high + low


def sector_part(z, coef, place):
    part = None
    for one in range(z.n_lon):
        first = one * z.spec_width
        first = first if first < KMAX else first - KMAX + HALF
        this = coef[:, first : first + z.spec_width]
        part = this if part is None else jnp.where(place == one, this, part)
    return part


def depths(z, depth_ref, row_ref):
    level = column_of(row_ref, LEVEL)[: z.own]
    depth = jnp.zeros_like(level)
    for lev in range(z.lev):
        depth = jnp.where(level == lev, depth_ref[lev], depth)
    return depth


def store_rims(z, ref, g, we, wn, last):
    edge = 2 * z.lev
    ref[:edge] = g[z.own - edge :] if last else g[:edge]
    ref[edge : edge + z.lev] = we[z.own - z.lev :] if last else we[: z.lev]
    ref[edge + z.lev :] = wn[z.own - z.lev :] if last else wn[: z.lev]


def east_shares_of(
    z, at, we_ref, wn_ref, g_ref, row_ref, phase_ref, basis_ref, share_ref, lhs_ref, basis_here=None
):
    inner = slice(at.start // z.lev, at.stop // z.lev)
    g, we, wn = (ref[inner].reshape(at.stop - at.start, z.lon) for ref in (g_ref, we_ref, wn_ref))

    @pl.when(on_polar_band(z))
    def _():
        coef, sine = column_of(row_ref, EAST_COEF)[at], column_of(row_ref, SINE)[at]
        new = widen(z, we + CORIOLIS * sine * wn) - coef * east_diff(widen(z, g))
        tail = put_lane(new[:, z.ext - 128 :], 127, 0.0)
        new = jnp.concatenate([new[:, : z.ext - 128], tail], axis=1)
        forward_sums(z, new, basis_ref, phase_ref, lhs_ref, share_ref, basis_here=basis_here)
        cos, sin = phase_of(phase_ref, z.blocks)
        before = -coef * g[:, 0:1]
        share_ref[:, :HALF] += before * cos
        share_ref[:, HALF:] += before * sin

    @pl.when(jnp.logical_not(on_polar_band(z)))
    def _():
        if basis_here is not None:
            basis_here()
        share_ref[...] = jnp.zeros_like(share_ref)

    last = z.lon - 1
    spare = share_ref[:, SPARE:HALF]
    edges = ((g, last - 1), (g, last), (we, last), (wn, last), (g, 0), (g, 1), (we, 0), (wn, 0))
    for n, (x, column) in enumerate(edges):
        spare = put_lane(spare, KMAX - SPARE + n, x[:, column : column + 1])
    share_ref[:, SPARE:HALF] = spare


def east_first(
    z, we_hbm, wn_hbm, g_hbm, row_hbm, phase_hbm, basis_hbm,
    share_ref, even_ref, odd_ref, we_ref, wn_ref, g_ref, row_ref, phase_ref, basis_ref, lhs_ref, sems,
):
    fields = ((g_hbm, g_ref), (we_hbm, we_ref), (wn_hbm, wn_ref))
    cut, rim = z.first // z.lev, z.lat - 2

    def copies(first_sem, pairs):
        return [pltpu.make_async_copy(*pair, sems.at[first_sem + n]) for n, pair in enumerate(pairs)]

    tables = copies(
        0,
        (
            (row_hbm.at[lax.axis_index("lat")], row_ref),
            (phase_hbm.at[lax.axis_index("lon")], phase_ref),
        ),
    )
    first = copies(2, [(a.at[:cut], b.at[:cut]) for a, b in fields])
    basis = copies(5, [(basis_hbm, basis_ref)])
    edge = copies(6, [(a.at[rim:], b.at[rim:]) for a, b in fields])
    between = copies(9, [(a.at[cut:rim], b.at[cut:rim]) for a, b in fields])
    for copy in first + tables + basis + edge:
        copy.start()
    for copy in first + tables:
        copy.wait()

    def basis_here():
        for copy in basis + edge:
            copy.wait()
        for copy in between:
            copy.start()

    east_shares_of(
        z, slice(0, z.first), we_ref, wn_ref, g_ref, row_ref, phase_ref, basis_ref, share_ref, lhs_ref,
        basis_here,
    )
    odd = lax.rem(lax.axis_index("lat"), 2) == 1
    last, flat = z.lat - 1, (z.lev, z.lon)
    far = (g_ref[last - 1], g_ref[last], we_ref[last], wn_ref[last])
    near = (g_ref[0], g_ref[1], we_ref[0], wn_ref[0])
    for n, (bottom, top) in enumerate(zip(far, near, strict=True)):
        at = slice(n * z.lev, (n + 1) * z.lev)
        even_ref[at] = jnp.where(odd, top, bottom).reshape(flat)
        odd_ref[at] = jnp.where(odd, bottom, top).reshape(flat)
    for copy in between:
        copy.wait()


def north_forward(
    z, we_ref, wn_ref, g_ref, even_ref, odd_ref, row_ref, phase_ref, basis_ref, kept_ref, slot_ref, *rest
):
    ahead_ref, rest_ref, north_ref, chosen_ref, g_rows, lhs_ref, share_ref = rest
    edge, lev = 2 * z.lev, z.lev
    odd = lax.rem(lax.axis_index("lat"), 2) == 1
    below = jnp.where(odd, odd_ref[...], even_ref[...])
    above = jnp.where(odd, even_ref[...], odd_ref[...])
    coef, sine = north_factor(z), CORIOLIS * column_of(row_ref, SINE)
    own = flat_rows(z, g_ref)
    g_rows[: z.own] = own
    g_rows[z.own : z.own + lev] = below[:lev]
    g_rows[z.own + lev :] = above[lev:edge]
    g = g_rows[...]
    diff = (roll(g, -lev, 0) - roll(g, lev, 0))[: z.own]
    north_ref[: z.own] = flat_rows(z, wn_ref) - coef * diff - sine[: z.own] * flat_rows(z, we_ref)
    for at, diff, rim in (
        (z.own, below[lev:edge] - own[z.own - lev :], below),
        (z.own + lev, own[:lev] - above[:lev], above),
    ):
        we, wn = rim[edge : edge + lev], rim[edge + lev :]
        north_ref[at : at + lev] = wn - coef * diff - sine[at : at + lev] * we
    number = column_of(row_ref, NUMBER).astype(jnp.int32)
    kept = look_up(number, kept_ref)

    @pl.when(on_polar_band(z))
    def _():
        forward_sums(z, widen(z, north_ref[...]), basis_ref, phase_ref, lhs_ref, share_ref)
        share_ref[:, SPARE:HALF] = put_lane(share_ref[:, SPARE:HALF], KMAX - SPARE, kept)
        chosen = slot_order(z, number, row_ref, slot_ref)
        ordered = reorder(chosen, share_ref[...])
        ahead_ref[...] = ordered[: z.ahead]
        rest_ref[...] = ordered[z.ahead : z.rows]
        chosen_ref[...] = chosen

    @pl.when(jnp.logical_not(on_polar_band(z)))
    def _():
        beyond = slice(z.own - z.ahead, z.rows - z.ahead)
        ahead_ref[...] = jnp.zeros_like(ahead_ref)
        rest_ref[...] = jnp.zeros_like(rest_ref)
        chosen_ref[...] = jnp.zeros_like(chosen_ref)
        rows = widen(z, north_ref[z.own :])
        forward_sums(z, rows, basis_ref, phase_ref, lhs_ref, rest_ref, beyond)
        rest_ref[beyond, SPARE:HALF] = put_lane(
            rest_ref[beyond, SPARE:HALF], KMAX - SPARE, kept[z.own :]
        )


def arrival(arrived_ref, out_ref):
    out_ref[...] = arrived_ref[:8, :128]


def east_inverse(
    z, depth_ref, we_ref, wn_ref, g_ref, thick_ref, row_ref, phase_ref, kept_ref, chosen_ref, first_here,
    *rest,
):
    del first_here
    firsts, seconds, rest = rest[: z.n_lon], rest[z.n_lon : 2 * z.n_lon], rest[2 * z.n_lon :]
    basis_ref, final_ref, part_ref, keep_ref, send_ref, lhs_ref, rows_ref, sums_ref = rest
    coef, sine = column_of(row_ref, EAST_COEF)[: z.own], column_of(row_ref, SINE)[: z.own]

    @pl.when(on_polar_band(z))
    def _():
        number = column_of(row_ref, NUMBER)[: z.own].astype(jnp.int32)
        sums_ref[: z.first] = sum(ref[...] for ref in firsts)
        sums_ref[z.first :] = sum(ref[...] for ref in seconds)
        waves = coefficients(z, sums_ref[...], look_up(number, kept_ref))
        part = sector_part(z, waves, lax.axis_index("lon"))
        ordered = reorder(chosen_ref[: z.own], part)
        send_ref[...] = ordered[: z.helped].reshape(send_ref.shape)
        keep_ref[...] = ordered[z.helped : 2 * z.helped].reshape(keep_ref.shape)
        inverse_rows(z, waves, basis_ref, phase_ref, lhs_ref, rows_ref)
        cos, sin = phase_of(phase_ref, z.blocks)
        before = jnp.sum(waves[:, :HALF] * cos + waves[:, HALF:] * sin, axis=1, keepdims=True)
        rows_ref[:, z.ext - 128 :] = put_lane(rows_ref[:, z.ext - 128 :], 127, before)

    @pl.when(jnp.logical_not(on_polar_band(z)))
    def _():
        send_ref[...] = jnp.zeros_like(send_ref)
        keep_ref[...] = jnp.zeros_like(keep_ref)
        first = KMAX - SPARE
        left, right = (
            jnp.concatenate([firsts[n][:, SPARE:HALF], seconds[n][:, SPARE:HALF]], axis=0)
            for n in (1, -1)
        )
        at_right = z.lon - (z.ext - 128)

        def rimmed(ref, left_of, right_of):
            x = widen(z, flat_rows(z, ref))
            tail = x[:, z.ext - 128 :]
            for n, lane in enumerate(right_of):
                tail = put_lane(tail, at_right + n, right[:, first + lane : first + lane + 1])
            for n, lane in enumerate(left_of):
                tail = put_lane(tail, 127 - n, left[:, first + lane : first + lane + 1])
            return jnp.concatenate([x[:, : z.ext - 128], tail], axis=1)

        g = rimmed(g_ref, (1, 0), (4, 5))
        we, wn = rimmed(we_ref, (2,), (6,)), rimmed(wn_ref, (3,), (7,))
        rows_ref[...] = we - coef * east_diff(g) + CORIOLIS * sine * wn

    final = rows_ref[...]
    final_ref[...] = final[:, : z.lon].reshape(final_ref.shape)
    change = depths(z, depth_ref, row_ref) * coef * east_diff(final)[:, : z.lon]
    part_ref[...] = flat_rows(z, thick_ref) - change


def send_spectra(z, east_ref, *rest):
    shares, send_ref = rest[:-1], rest[-1]
    kept = shares[0][:, KMAX : KMAX + 1]
    coef = coefficients(z, sum(ref[...] for ref in shares), kept)
    part = sector_part(z, coef, lax.axis_index("lon"))
    send_ref[0] = east_ref[...]
    send_ref[1] = part[: z.helped].reshape(east_ref.shape)


def ahead_inverse(z, phase_ref, *rest):
    shares, (basis_ref, high_ref, low_ref, lhs_ref, rows_ref) = rest[: z.n_lon], rest[z.n_lon :]

    @pl.when(on_polar_band(z))
    def _():
        kept = shares[0][:, KMAX : KMAX + 1]
        waves = coefficients(z, sum(ref[...] for ref in shares), kept)
        inverse_rows(z, waves, basis_ref, phase_ref, lhs_ref, rows_ref)
        high_ref[...], low_ref[...] = split(rows_ref[...])


def north_inverse(
    z, active, depth_ref, north_ref, part_ref, row_ref, phase_ref, chosen_ref, high_ahead, low_ahead,
    *rest,
):
    ahead, shares, rest = rest[: z.n_lon], rest[z.n_lon : 2 * z.n_lon], rest[2 * z.n_lon :]
    basis_ref, final_ref, thick_ref, column_ref, keep_ref, lhs_ref, rows_ref, high_ref, low_ref = rest

    @pl.when(active & on_polar_band(z))
    def _():
        more = z.ahead - 8
        kept = [ahead[0][more:, KMAX : KMAX + 1], shares[0][:, KMAX : KMAX + 1]]
        sums = [sum(ref[more:] for ref in ahead), sum(ref[...] for ref in shares)]
        waves = coefficients(z, jnp.concatenate(sums, axis=0), jnp.concatenate(kept, axis=0))
        part = sector_part(z, waves, lax.axis_index("lon"))
        first = z.helped - more
        keep_ref[...] = part[first : first + z.helped].reshape(keep_ref.shape)
        inverse_rows(z, waves[8:], basis_ref, phase_ref, lhs_ref, rows_ref, slice(z.rows - z.ahead))
        count = high_ref.shape[0] - z.ahead
        rest_high, rest_low = split(pad_rows(rows_ref[: z.rows - z.ahead], count))
        high_ref[: z.ahead], low_ref[: z.ahead] = high_ahead[...], low_ahead[...]
        high_ref[z.ahead :], low_ref[z.ahead :] = rest_high, rest_low
        chosen = chosen_ref[...].astype(jnp.bfloat16)
        rows_ref[...] = jnp.dot(
            chosen, high_ref[...], preferred_element_type=jnp.float32
        ) + jnp.dot(chosen, low_ref[...], preferred_element_type=jnp.float32)
        beyond = slice(z.own, z.rows)
        polar = column_of(row_ref, POLAR)[beyond] > 0.0
        rows_ref[beyond, : z.lon] = jnp.where(polar, rows_ref[beyond, : z.lon], north_ref[beyond])

    @pl.when(active & jnp.logical_not(on_polar_band(z)))
    def _():
        keep_ref[...] = jnp.zeros_like(keep_ref)
        beyond = slice(z.own, z.rows)
        at = slice(z.own - z.ahead, z.rows - z.ahead)
        waves = coefficients(z, sum(ref[at] for ref in shares), shares[0][at, KMAX : KMAX + 1])
        inverse_rows(z, waves, basis_ref, phase_ref, lhs_ref, rows_ref, beyond)
        polar = column_of(row_ref, POLAR)[beyond] > 0.0
        rows_ref[beyond, : z.lon] = jnp.where(polar, rows_ref[beyond, : z.lon], north_ref[beyond])
        rows_ref[: z.own, : z.lon] = north_ref[: z.own]

    @pl.when(active)
    def _():
        final = rows_ref[:, : z.lon]
        final_ref[...] = final[: z.own].reshape(final_ref.shape)
        scaled = final * column_of(row_ref, COSINE)
        diff = (roll(scaled, -z.lev, 0) - roll(scaled, z.lev, 0))[: z.own]
        scale = depths(z, depth_ref, row_ref) * column_of(row_ref, NORTH_COEF)[: z.own]
        thick_ref[...] = (part_ref[...] - scale * diff).reshape(thick_ref.shape)
        column_ref[...] = sum(thick_ref[:, lev, :] for lev in range(z.lev))


def sends_column():
    return lax.axis_index("lev") > 0


def north_deeper(z, *refs):
    north_inverse(z, sends_column(), *refs)


def north_shallowest(z, east_keep, north_keep, arrived_ref, *rest):
    *refs, spectra_ref, column_ref, keep_ref, lhs_ref, rows_ref, high_ref, low_ref = rest
    active = jnp.logical_not(sends_column())
    north_inverse(z, active, *refs, column_ref, keep_ref, lhs_ref, rows_ref, high_ref, low_ref)

    @pl.when(sends_column())
    def _():
        keep_ref[...] = north_keep[...]

    polar = on_polar_band(z)
    spectra_ref[0] = jnp.where(polar, east_keep[...], arrived_ref[0])
    spectra_ref[1] = jnp.where(polar, keep_ref[...], arrived_ref[1])


def finish(z, surface_ref, *rest):
    deeper_fields, own_fields, deeper, outs = rest[:2], rest[2:4], rest[4 : 3 + z.n_lev], rest[3 + z.n_lev :]
    final_out, thick_out, geo_out, geo_ref, sems = outs

    def store(fields):
        copies = [
            pltpu.make_async_copy(*pair, sems.at[n])
            for n, pair in enumerate(zip(fields, (final_out, thick_out), strict=True))
        ]
        for copy in copies:
            copy.start()
        for n in range(z.cuts):
            at = slice(n * z.lat // z.cuts, (n + 1) * z.lat // z.cuts)
            column = sum(ref[at] for ref in deeper)
            for lev in reversed(range(z.lev)):
                column = column + fields[1][at, lev, :]
                geo_ref[at, lev, :] = surface_ref[at] + GRAVITY * column
            copies.append(pltpu.make_async_copy(geo_ref.at[at], geo_out.at[at], sems.at[2 + n]))
            copies[-1].start()
        for copy in copies:
            copy.wait()

    @pl.when(sends_column())
    def _():
        store(deeper_fields)

    @pl.when(jnp.logical_not(sends_column()))
    def _():
        store(own_fields)


def call(kernel, n_in, out_shape, scratch, micros, spaces=None, in_hbm=0, vmem=24):
    vmem_spec = pl.BlockSpec(memory_space=pltpu.VMEM)
    spaces = spaces or {}
    return pl.pallas_call(
        kernel,
        in_specs=[
            pl.BlockSpec(memory_space=spaces[n]) if n in spaces else vmem_spec for n in range(n_in)
        ],
        out_specs=[pl.BlockSpec(memory_space=pltpu.HBM)] * in_hbm
        + [vmem_spec] * (len(out_shape) - in_hbm),
        out_shape=[
            jax.ShapeDtypeStruct(s, jnp.float32) if isinstance(s, tuple) else s for s in out_shape
        ],
        scratch_shapes=scratch,
        compiler_params=pltpu.CompilerParams(vmem_limit_bytes=vmem * MIB),
        cost_estimate=pl.CostEstimate(
            flops=int(micros * 1.15e9), bytes_accessed=0, transcendentals=0
        ),
    )


def shifted(block, axis, distance):
    count = lax.axis_size(axis)
    return lax.ppermute(block, axis, [(i, (i + distance) % count) for i in range(count)])


def level_inside(x):
    return jnp.swapaxes(x, -3, -2)


def local(
    wind_east, wind_north, thickness, geopot, surface_geopot, mean_depth, kept_modes, slot_table
):
    z = Sizes(thickness.shape, {axis: lax.axis_size(axis) for axis in ("lat", "lon", "lev")})
    wind_east, wind_north, thickness, geopot = (
        level_inside(x) for x in (wind_east, wind_north, thickness, geopot)
    )
    field = (z.lat, z.lev, z.lon)
    forward, inverse = (jnp.asarray(x) for x in basis_tables(z))
    phase = jnp.asarray(phase_table(z))
    per_row = jnp.asarray(row_table(z))
    kept = kept_modes[None, :]
    slots = slot_table[None, :]
    payload = (z.rows, WIDE)
    rims = (4 * z.lev, z.lon)
    spec = (z.help, z.lev, z.spec_width)
    waves_lhs = pltpu.VMEM((z.ext // z.inverse_block * z.mm_rows, 3 * WIDE), jnp.bfloat16)

    row_shape, phase_shape = per_row.shape[1:], phase.shape[1:]
    pinned = [
        pltpu.with_memory_space_constraint(x, pltpu.HBM)
        for x in (wind_east, wind_north, geopot, per_row, phase, forward)
    ]
    columns_lhs = pltpu.VMEM((z.blocks * z.mm_rows, 3 * BLOCK), jnp.bfloat16)
    waves_lhs = pltpu.VMEM((z.ext // z.inverse_block * z.mm_rows, 3 * WIDE), jnp.bfloat16)

    share_first, to_even, to_odd, wind_east, wind_north, geopot, per_row, phase, forward = call(
        functools.partial(east_first, z),
        6,
        [(z.first, WIDE), rims, rims]
        + [pltpu.VMEM(s, jnp.float32) for s in (field, field, field, row_shape, phase_shape)]
        + [pltpu.VMEM(forward.shape, forward.dtype)],
        [columns_lhs, pltpu.SemaphoreType.DMA((12,))],
        1,
        {n: pltpu.HBM for n in range(6)},
    )(*pinned)
    (share_second,) = call(
        functools.partial(east_shares_of, z, slice(z.first, z.own)),
        6,
        [(z.own - z.first, WIDE)],
        [columns_lhs],
        0.18,
    )(wind_east, wind_north, geopot, per_row, phase, forward)
    east_firsts, east_seconds = (
        [x] + [shifted(x, "lon", s) for s in range(1, z.n_lon)] for x in (share_first, share_second)
    )
    met = []
    for start, rim in enumerate((to_even, to_odd)):
        pairs = [(i, i + 1) for i in range(start, z.n_lat - 1, 2)]
        met.append(lax.ppermute(rim, "lat", pairs + [(b, a) for a, b in pairs]))

    places = round_up(z.rows, 128)
    north_ahead, north_rest, north_new, chosen = call(
        functools.partial(north_forward, z),
        10,
        [(z.ahead, WIDE), (z.rows - z.ahead, WIDE), (z.rows, z.lon), (z.rows, places)],
        [
            pltpu.VMEM((z.rows, z.lon), jnp.float32),
            columns_lhs,
            pltpu.VMEM((z.rows, WIDE), jnp.float32),
        ],
        0.8,
    )(
        wind_east, wind_north, geopot, *met, per_row, phase, forward, kept, slots
    )
    north_rests = [north_rest] + [shifted(north_rest, "lon", s) for s in range(1, z.n_lon)]
    polar_bands = [i for i in range(z.n_lat) if i < z.n_lat // 4 or i >= z.n_lat - z.n_lat // 4]
    north_aheads = [north_ahead]
    for distance in range(1, z.n_lon):
        route = [
            (band * z.n_lon + lon, band * z.n_lon + (lon + distance) % z.n_lon)
            for band in polar_bands
            for lon in range(z.n_lon)
        ]
        north_aheads.append(lax.ppermute(north_ahead, ("lat", "lon"), route))

    (first_here,) = call(arrival, 1, [(8, 128)], [], 0.95)(east_firsts[1])
    east_final, thick_part, east_keep, east_send = call(
        functools.partial(east_inverse, z),
        11 + 2 * z.n_lon,
        [field, (z.own, z.lon), spec, spec],
        [
            waves_lhs,
            pltpu.VMEM((z.own, z.ext), jnp.float32),
            pltpu.VMEM((z.own, WIDE), jnp.float32),
        ],
        1,
        {0: pltpu.SMEM},
    )(
        mean_depth, wind_east, wind_north, geopot, thickness, per_row, phase, kept, chosen,
        first_here, *east_firsts, *east_seconds, inverse,
    )

    (to_helper,) = call(
        functools.partial(send_spectra, z), 1 + z.n_lon, [(2, *spec)], [], 0.1
    )(east_send, *north_aheads)
    arrived = lax.ppermute(
        to_helper, "lat", [(i, (i + z.half_axis) % z.n_lat) for i in polar_bands]
    )

    ahead_rows = jax.ShapeDtypeStruct((z.ahead, z.ext), jnp.bfloat16)
    ahead_high, ahead_low = call(
        functools.partial(ahead_inverse, z),
        2 + z.n_lon,
        [ahead_rows] * 2,
        [waves_lhs, pltpu.VMEM((z.ahead, z.ext), jnp.float32)],
        0.5,
    )(phase, *north_aheads, inverse)

    operands = (
        mean_depth, north_new, thick_part, per_row, phase, chosen, ahead_high, ahead_low,
        *north_aheads, *north_rests, inverse,
    )
    in_vmem = pltpu.VMEM(field, jnp.float32)
    scratch = [waves_lhs, pltpu.VMEM((z.rows, z.ext), jnp.float32)]
    scratch += [pltpu.VMEM((places, z.ext), jnp.bfloat16)] * 2
    final_deeper, thick_deeper, column, north_keep = call(
        functools.partial(north_deeper, z),
        len(operands),
        [in_vmem, in_vmem, (z.lat, z.lon), spec],
        scratch,
        2,
        {0: pltpu.SMEM},
    )(*operands)
    deeper = [
        lax.ppermute(column, "lev", [(i, i - distance) for i in range(distance, z.n_lev)])
        for distance in range(1, z.n_lev)
    ]
    final_own, thick_own, spectra = call(
        functools.partial(north_shallowest, z),
        3 + len(operands),
        [in_vmem, in_vmem, (2, *spec)],
        [pltpu.VMEM((z.lat, z.lon), jnp.float32), pltpu.VMEM(spec, jnp.float32)] + scratch,
        3.2,
        {3: pltpu.SMEM},
    )(east_keep, north_keep, arrived, *operands)
    north_final, thick_new, geo_new = call(
        functools.partial(finish, z),
        5 + len(deeper),
        [pltpu.HBM(field, jnp.float32)] * 3,
        [pltpu.VMEM(field, jnp.float32), pltpu.SemaphoreType.DMA((2 + z.cuts,))],
        1,
        in_hbm=3,
    )(surface_geopot, final_deeper, thick_deeper, final_own, thick_own, *deeper)
    return tuple(level_inside(x) for x in (east_final, north_final, thick_new, geo_new, spectra))


def solution(mesh):
    field = P(("members", "lev"), "lat", "lon")
    return jax.shard_map(
        local,
        mesh=mesh,
        in_specs=(field, field, field, field, P("lat", "lon"), P("lev"), P(), P()),
        out_specs=(field, field, field, field, P(None, ("members", "lev"), "lat", "lon")),
        check_vma=False,
    )
```

```python
import functools
import math

import jax
import jax.numpy as jnp
import numpy as np
from jax import lax
from jax.experimental import pallas as pl
from jax.experimental.pallas import tpu as pltpu
from jax.sharding import PartitionSpec as P

KMAX = 360
HALF = 384
WIDE = 2 * HALF
SPARE = HALF - 128
MORE = KMAX - SPARE
MOVED = 128 - MORE
LEFT = MORE - MOVED
BLOCK = 256
INVERSE_BLOCK = 768

STEP_FACTOR = 0.15
CORIOLIS = 0.2
GRAVITY = 0.25

MIB = 1024 * 1024

EAST_COEF, SINE, COSINE, NORTH_COEF, LEVEL, POLAR, NUMBER, OWN = range(8)


def round_up(value, step):
    return -(-value // step) * step


class Sizes:
    def __init__(self, shape, counts):
        self.lev, self.lat, self.lon = shape
        self.n_lat, self.n_lon, self.n_lev = counts["lat"], counts["lon"], counts["lev"]
        self.nlat, self.nlon = self.lat * self.n_lat, self.lon * self.n_lon
        self.polar = self.nlat // 4
        self.help = self.lat // 2
        self.half_axis = self.n_lat // 2
        self.own = self.lat * self.lev
        self.rows = self.own + 2 * self.lev
        assert self.rows % 8 == 0
        self.mm_rows = round_up(self.rows, 16)
        self.ext = round_up(self.lon + 4, BLOCK)
        self.blocks = self.ext // BLOCK
        self.inverse_block = min(INVERSE_BLOCK, self.ext)
        assert self.ext % self.inverse_block == 0
        self.spec_width = 2 * KMAX // self.n_lon
        self.helped = self.help * self.lev
        self.ahead = round_up(self.helped, 16)
        self.cuts = 2
        self.first = min(round_up(self.own * 4 // 9, 8 * self.lev), self.own)


def high_low(x):
    x = x.astype(np.float32)
    high = x.astype(jnp.bfloat16)
    return high, (x - high.astype(np.float32)).astype(jnp.bfloat16)


def basis_tables(z):
    k = np.arange(KMAX)
    angle = (np.arange(z.inverse_block)[:, None] * k[None, :] % z.nlon) * (2.0 * np.pi / z.nlon)
    full = np.zeros((z.inverse_block, WIDE))
    full[:, :KMAX] = np.cos(angle)
    full[:, HALF : HALF + KMAX] = np.sin(angle)
    high, low = high_low(full)
    forward = np.concatenate([high[:BLOCK], high[:BLOCK], low[:BLOCK]], axis=0)
    inverse = np.concatenate([high.T, high.T, low.T], axis=0)
    return forward, inverse


def phase_table(z):
    k = np.arange(KMAX)
    table = np.zeros((z.n_lon, round_up(2 * z.blocks + 2, 8), HALF), np.float32)
    for place in range(z.n_lon):
        for n, column in enumerate([*range(0, z.ext, BLOCK), -1]):
            angle = ((place * z.lon + column) * k % z.nlon) * (2.0 * np.pi / z.nlon)
            table[place, 2 * n, :KMAX] = np.cos(angle)
            table[place, 2 * n + 1, :KMAX] = np.sin(angle)
    return table


def row_table(z):
    lam_step = np.float32(2.0 * math.pi / z.nlon)
    phi_step = np.float32(math.pi / z.nlat)
    latitude = np.float32(-0.5 * math.pi) + (
        np.arange(z.nlat, dtype=np.float32) + np.float32(0.5)
    ) * phi_step
    cosine = np.cos(latitude.astype(np.float64)).astype(np.float32)
    sine = np.sin(latitude.astype(np.float64)).astype(np.float32)
    north_coef = np.float32(STEP_FACTOR) * lam_step / phi_step
    table = np.zeros((z.n_lat, z.rows, 8), np.float32)
    for place in range(z.n_lat):
        for flat in range(z.rows):
            inner, level = flat // z.lev, flat % z.lev
            inner = -1 if inner == z.lat + 1 else inner
            row = place * z.lat + inner
            one = table[place, flat]
            one[LEVEL], one[NUMBER] = level, -1
            one[OWN] = 0 <= inner < z.lat
            if 0 <= row < z.nlat:
                one[EAST_COEF] = np.float32(STEP_FACTOR) / cosine[row]
                one[SINE], one[COSINE] = sine[row], cosine[row]
                one[NORTH_COEF] = north_coef / cosine[row]
                if row < z.polar:
                    one[POLAR], one[NUMBER] = 1, row
                elif row >= z.nlat - z.polar:
                    one[POLAR], one[NUMBER] = 1, row - (z.nlat - 2 * z.polar)
    return table


def on_polar_band(z):
    lat_index = lax.axis_index("lat")
    return (lat_index < z.n_lat // 4) | (lat_index >= z.n_lat - z.n_lat // 4)


def split(x):
    high = x.astype(jnp.bfloat16)
    return high, (x - high.astype(jnp.float32)).astype(jnp.bfloat16)


def store_split(lhs_ref, first_row, x):
    rows, width = x.shape
    high, low = split(x)
    at = slice(first_row, first_row + rows)
    lhs_ref[at, :width] = high
    lhs_ref[at, width : 2 * width] = low
    lhs_ref[at, 2 * width :] = high


def pad_rows(x, rows):
    if x.shape[0] == rows:
        return x
    return jnp.concatenate([x, jnp.zeros((rows - x.shape[0], x.shape[1]), x.dtype)], axis=0)


def phase_of(phase_ref, n):
    return phase_ref[2 * n : 2 * n + 1], phase_ref[2 * n + 1 : 2 * n + 2]


def packed_rows(rows):
    return 5 * rows + round_up(-(-rows // 2), 8) + 16


def lanes_of(x):
    return lax.broadcasted_iota(jnp.int32, x.shape, 1)


def pack(x, out_ref):
    rows = x.shape[0]
    half = round_up(-(-rows // 2), 8)
    tiles = [x[:, n : n + 128] for n in range(0, WIDE, 128)]
    left = tiles[5]
    lane = lanes_of(left)
    tiles[2] = jnp.where(lane < MORE, tiles[2], roll(left, MOVED, 1))
    for n in range(5):
        out_ref[n * rows : (n + 1) * rows] = tiles[n]
    lower = pad_rows(left[half:], half)
    out_ref[5 * rows : 5 * rows + half] = jnp.where(lane[:half] < 64, left[:half], roll(lower, 64, 1))
    out_ref[5 * rows + half :] = pad_rows(roll(left, -64, 1), 128).T[:16]


def unpack(x, rows):
    half = round_up(-(-rows // 2), 8)
    tiles = [x[n * rows : (n + 1) * rows] for n in range(5)]
    pairs = x[5 * rows : 5 * rows + half]
    ends = pad_rows(x[5 * rows + half :], 128).T[:rows]
    left = jnp.concatenate([pairs, roll(pairs, 64, 1)[: rows - half]], axis=0)
    lane = lanes_of(left)
    left = jnp.where(lane < 64, left, jnp.where(lane < LEFT, roll(ends, 64, 1), roll(tiles[2], -MOVED, 1)))
    return jnp.concatenate([*tiles, left], axis=1)


def forward_sums(
    z, x, basis_ref, phase_ref, lhs_ref, out_ref, at=slice(None), basis_here=None
):
    count = round_up(x.shape[0], 16)
    for block in range(z.blocks):
        part = pad_rows(x[:, block * BLOCK : (block + 1) * BLOCK], count)
        store_split(lhs_ref, block * count, part)
    lhs = lhs_ref[: z.blocks * count]
    if basis_here is not None:
        basis_here()
    sums = jnp.dot(lhs, basis_ref[...], preferred_element_type=jnp.float32)
    real = imag = None
    for block in range(z.blocks):
        cos, sin = phase_of(phase_ref, block)
        part = sums[block * count : block * count + x.shape[0]]
        a, b = part[:, :HALF], part[:, HALF:]
        more_real, more_imag = a * cos - b * sin, a * sin + b * cos
        real = more_real if real is None else real + more_real
        imag = more_imag if imag is None else imag + more_imag
    out_ref[at, :HALF] = real
    out_ref[at, HALF:] = imag


def inverse_rows(z, coef, basis_ref, phase_ref, lhs_ref, out_ref, at=slice(None)):
    a, b = coef[:, :HALF], coef[:, HALF:]
    count, width = round_up(coef.shape[0], 16), z.inverse_block
    blocks = range(z.ext // width)
    for block in blocks:
        cos, sin = phase_of(phase_ref, block * width // BLOCK)
        turned = jnp.concatenate([a * cos + b * sin, b * cos - a * sin], axis=1)
        store_split(lhs_ref, block * count, pad_rows(turned, count))
    lhs = lhs_ref[: len(blocks) * count]
    rows = jnp.dot(lhs, basis_ref[...], preferred_element_type=jnp.float32)
    for block in blocks:
        out_ref[at, block * width : (block + 1) * width] = rows[
            block * count : block * count + coef.shape[0]
        ]


def roll(x, shift, axis):
    return pltpu.roll(x, shift % x.shape[axis], axis)


def east_diff(x):
    return roll(x, -1, 1) - roll(x, 1, 1)


def flat_rows(z, ref):
    return ref[...].reshape(z.own, ref.shape[2])


def widen(z, x):
    return jnp.concatenate([x, jnp.zeros((x.shape[0], z.ext - x.shape[1]), x.dtype)], axis=1)


def put_lane(x, at, column):
    lane = lax.broadcasted_iota(jnp.int32, x.shape, 1)
    return jnp.where(lane == at, column, x)


def column_of(row_ref, which):
    return row_ref[:, which : which + 1]


def north_factor(z):
    return STEP_FACTOR * (2.0 * math.pi / z.nlon) / (math.pi / z.nlat)


def look_up(number, table_ref):
    table = table_ref[...].astype(jnp.float32)
    lane = lax.broadcasted_iota(jnp.int32, (number.shape[0], table.shape[1]), 1)
    return jnp.sum(jnp.where(lane == number, table, 0.0), axis=1, keepdims=True)


def coefficients(z, sums, kept):
    lane = lax.broadcasted_iota(jnp.int32, (1, WIDE), 1)
    k = jnp.where(lane < HALF, lane, lane - HALF)
    weight = jnp.where(k == 0, 1.0 / z.nlon, 2.0 / z.nlon).astype(jnp.float32)
    keep = (k.astype(jnp.float32) < kept) & (k < KMAX)
    return jnp.where(keep, sums * weight, 0.0)


def slot_order(z, number, row_ref, slot_ref):
    lat_index = lax.axis_index("lat")
    slot = look_up(number, slot_ref).astype(jnp.int32)
    theirs = slot - lax.rem(lat_index + z.half_axis, z.n_lat) * z.help
    mine = slot - lat_index * z.help
    level = column_of(row_ref, LEVEL).astype(jnp.int32)
    flat = lax.broadcasted_iota(jnp.int32, slot.shape, 0)
    place = jnp.where((mine >= 0) & (mine < z.help), z.helped + mine * z.lev + level, -1)
    place = jnp.where((theirs >= 0) & (theirs < z.help), theirs * z.lev + level, place)
    place = jnp.where(number >= 0, place, -1)
    place = jnp.where(flat < z.own, place, flat)
    lane = lax.broadcasted_iota(jnp.int32, (z.rows, round_up(z.rows, 128)), 1)
    return (lane == place).astype(jnp.float32)


def reorder(chosen, values):
    high, low = (
        lax.dot_general(
            chosen.astype(jnp.bfloat16),
            part,
            (((0,), (0,)), ((), ())),
            preferred_element_type=jnp.float32,
        )
        for part in split(values)
    )
    return high + low


def sector_part(z, coef, place):
    part = None
    for one in range(z.n_lon):
        first = one * z.spec_width
        first = first if first < KMAX else first - KMAX + HALF
        this = coef[:, first : first + z.spec_width]
        part = this if part is None else jnp.where(place == one, this, part)
    return part


def depths(z, depth_ref, row_ref):
    level = column_of(row_ref, LEVEL)[: z.own]
    depth = jnp.zeros_like(level)
    for lev in range(z.lev):
        depth = jnp.where(level == lev, depth_ref[lev], depth)
    return depth


def store_rims(z, ref, g, we, wn, last):
    edge = 2 * z.lev
    ref[:edge] = g[z.own - edge :] if last else g[:edge]
    ref[edge : edge + z.lev] = we[z.own - z.lev :] if last else we[: z.lev]
    ref[edge + z.lev :] = wn[z.own - z.lev :] if last else wn[: z.lev]


def east_shares_of(
    z, at, we_ref, wn_ref, g_ref, row_ref, phase_ref, basis_ref, out_ref, lhs_ref, share_ref,
    basis_here=None,
):
    inner, rows = slice(at.start // z.lev, at.stop // z.lev), at.stop - at.start
    g, we, wn = (ref[inner].reshape(rows, z.lon) for ref in (g_ref, we_ref, wn_ref))

    @pl.when(on_polar_band(z))
    def _():
        coef, sine = column_of(row_ref, EAST_COEF)[at], column_of(row_ref, SINE)[at]
        new = widen(z, we + CORIOLIS * sine * wn) - coef * east_diff(widen(z, g))
        tail = put_lane(new[:, z.ext - 128 :], 127, 0.0)
        new = jnp.concatenate([new[:, : z.ext - 128], tail], axis=1)
        forward_sums(
            z, new, basis_ref, phase_ref, lhs_ref, share_ref, slice(rows), basis_here=basis_here
        )
        cos, sin = phase_of(phase_ref, z.blocks)
        before = -coef * g[:, 0:1]
        share_ref[:rows, :HALF] += before * cos
        share_ref[:rows, HALF:] += before * sin
        pack(share_ref[...], out_ref)

    @pl.when(jnp.logical_not(on_polar_band(z)))
    def _():
        if basis_here is not None:
            basis_here()
        last = z.lon - 1
        columns = jnp.zeros((rows, 128), jnp.float32)
        edges = ((g, last - 1), (g, last), (we, last), (wn, last), (g, 0), (g, 1), (we, 0), (wn, 0))
        for n, (x, column) in enumerate(edges):
            columns = put_lane(columns, n, x[:, column : column + 1])
        out_ref[...] = jnp.zeros_like(out_ref)
        out_ref[:rows] = columns


def east_first(
    z, we_hbm, wn_hbm, g_hbm, row_hbm, phase_hbm, basis_hbm,
    share_ref, even_ref, odd_ref, we_ref, wn_ref, g_ref, row_ref, phase_ref, basis_ref, lhs_ref, sums_ref, sems,
):
    fields = ((g_hbm, g_ref), (we_hbm, we_ref), (wn_hbm, wn_ref))
    cut, rim = z.first // z.lev, z.lat - 2

    def copies(first_sem, pairs):
        return [pltpu.make_async_copy(*pair, sems.at[first_sem + n]) for n, pair in enumerate(pairs)]

    tables = copies(
        0,
        (
            (row_hbm.at[lax.axis_index("lat")], row_ref),
            (phase_hbm.at[lax.axis_index("lon")], phase_ref),
        ),
    )
    first = copies(2, [(a.at[:cut], b.at[:cut]) for a, b in fields])
    basis = copies(5, [(basis_hbm, basis_ref)])
    edge = copies(6, [(a.at[rim:], b.at[rim:]) for a, b in fields])
    between = copies(9, [(a.at[cut:rim], b.at[cut:rim]) for a, b in fields])
    for copy in first + tables + basis + edge:
        copy.start()
    for copy in first + tables:
        copy.wait()

    def basis_here():
        for copy in basis + edge:
            copy.wait()
        for copy in between:
            copy.start()

    east_shares_of(
        z, slice(0, z.first), we_ref, wn_ref, g_ref, row_ref, phase_ref, basis_ref, share_ref, lhs_ref,
        sums_ref, basis_here,
    )
    odd = lax.rem(lax.axis_index("lat"), 2) == 1
    last, flat = z.lat - 1, (z.lev, z.lon)
    far = (g_ref[last - 1], g_ref[last], we_ref[last], wn_ref[last])
    near = (g_ref[0], g_ref[1], we_ref[0], wn_ref[0])
    for n, (bottom, top) in enumerate(zip(far, near, strict=True)):
        at = slice(n * z.lev, (n + 1) * z.lev)
        even_ref[at] = jnp.where(odd, top, bottom).reshape(flat)
        odd_ref[at] = jnp.where(odd, bottom, top).reshape(flat)
    for copy in between:
        copy.wait()


def north_forward(
    z, we_ref, wn_ref, g_ref, even_ref, odd_ref, row_ref, phase_ref, basis_ref, kept_ref, slot_ref, *rest
):
    ahead_ref, rest_ref, north_ref, chosen_ref, sorted_ref, g_rows, lhs_ref, share_ref = rest
    edge, lev = 2 * z.lev, z.lev
    odd = lax.rem(lax.axis_index("lat"), 2) == 1
    below = jnp.where(odd, odd_ref[...], even_ref[...])
    above = jnp.where(odd, even_ref[...], odd_ref[...])
    coef, sine = north_factor(z), CORIOLIS * column_of(row_ref, SINE)
    own = flat_rows(z, g_ref)
    g_rows[: z.own] = own
    g_rows[z.own : z.own + lev] = below[:lev]
    g_rows[z.own + lev :] = above[lev:edge]
    g = g_rows[...]
    diff = (roll(g, -lev, 0) - roll(g, lev, 0))[: z.own]
    north_ref[: z.own] = flat_rows(z, wn_ref) - coef * diff - sine[: z.own] * flat_rows(z, we_ref)
    for at, diff, rim in (
        (z.own, below[lev:edge] - own[z.own - lev :], below),
        (z.own + lev, own[:lev] - above[:lev], above),
    ):
        we, wn = rim[edge : edge + lev], rim[edge + lev :]
        north_ref[at : at + lev] = wn - coef * diff - sine[at : at + lev] * we
    number = column_of(row_ref, NUMBER).astype(jnp.int32)
    kept = look_up(number, kept_ref)

    @pl.when(on_polar_band(z))
    def _():
        forward_sums(z, widen(z, north_ref[...]), basis_ref, phase_ref, lhs_ref, share_ref)
        share_ref[:, SPARE:HALF] = put_lane(share_ref[:, SPARE:HALF], KMAX - SPARE, kept)
        chosen = slot_order(z, number, row_ref, slot_ref)
        ordered = reorder(chosen, share_ref[...])
        pack(ordered[: z.ahead], ahead_ref)
        pack(ordered[z.ahead : z.rows], rest_ref)
        sorted_ref[...] = ordered[: z.rows, SPARE:HALF]
        chosen_ref[...] = chosen

    @pl.when(jnp.logical_not(on_polar_band(z)))
    def _():
        ahead_ref[...] = jnp.zeros_like(ahead_ref)
        chosen_ref[...] = jnp.zeros_like(chosen_ref)
        share_ref[...] = jnp.zeros_like(share_ref)
        rows = widen(z, north_ref[z.own :])
        forward_sums(z, rows, basis_ref, phase_ref, lhs_ref, share_ref, slice(z.own, z.rows))
        pack(share_ref[z.ahead :], rest_ref)
        sorted_ref[...] = jnp.broadcast_to(kept, sorted_ref.shape)


def arrival(arrived_ref, out_ref):
    out_ref[...] = arrived_ref[:8, :128]


def east_inverse(
    z, depth_ref, we_ref, wn_ref, g_ref, thick_ref, row_ref, phase_ref, kept_ref, chosen_ref, first_here,
    *rest,
):
    del first_here
    firsts, seconds, rest = rest[: z.n_lon], rest[z.n_lon : 2 * z.n_lon], rest[2 * z.n_lon :]
    basis_ref, final_ref, part_ref, keep_ref, send_ref, lhs_ref, rows_ref, sums_ref = rest
    coef, sine = column_of(row_ref, EAST_COEF)[: z.own], column_of(row_ref, SINE)[: z.own]

    @pl.when(on_polar_band(z))
    def _():
        number = column_of(row_ref, NUMBER)[: z.own].astype(jnp.int32)
        second = round_up(z.own - z.first, 8)
        sums_ref[: z.first] = unpack(sum(ref[...] for ref in firsts), z.first)
        sums_ref[z.first :] = unpack(sum(ref[...] for ref in seconds), second)[: z.own - z.first]
        waves = coefficients(z, sums_ref[...], look_up(number, kept_ref))
        part = sector_part(z, waves, lax.axis_index("lon"))
        ordered = reorder(chosen_ref[: z.own], part)
        send_ref[...] = ordered[: z.helped].reshape(send_ref.shape)
        keep_ref[...] = ordered[z.helped : 2 * z.helped].reshape(keep_ref.shape)
        inverse_rows(z, waves, basis_ref, phase_ref, lhs_ref, rows_ref)
        cos, sin = phase_of(phase_ref, z.blocks)
        before = jnp.sum(waves[:, :HALF] * cos + waves[:, HALF:] * sin, axis=1, keepdims=True)
        rows_ref[:, z.ext - 128 :] = put_lane(rows_ref[:, z.ext - 128 :], 127, before)

    @pl.when(jnp.logical_not(on_polar_band(z)))
    def _():
        send_ref[...] = jnp.zeros_like(send_ref)
        keep_ref[...] = jnp.zeros_like(keep_ref)
        left, right = (
            jnp.concatenate([firsts[n][: z.first], seconds[n][: z.own - z.first]], axis=0)
            for n in (1, -1)
        )
        at_right = z.lon - (z.ext - 128)

        def rimmed(ref, left_of, right_of):
            x = widen(z, flat_rows(z, ref))
            tail = x[:, z.ext - 128 :]
            for n, lane in enumerate(right_of):
                tail = put_lane(tail, at_right + n, right[:, lane : lane + 1])
            for n, lane in enumerate(left_of):
                tail = put_lane(tail, 127 - n, left[:, lane : lane + 1])
            return jnp.concatenate([x[:, : z.ext - 128], tail], axis=1)

        g = rimmed(g_ref, (1, 0), (4, 5))
        we, wn = rimmed(we_ref, (2,), (6,)), rimmed(wn_ref, (3,), (7,))
        rows_ref[...] = we - coef * east_diff(g) + CORIOLIS * sine * wn

    final = rows_ref[...]
    final_ref[...] = final[:, : z.lon].reshape(final_ref.shape)
    change = depths(z, depth_ref, row_ref) * coef * east_diff(final)[:, : z.lon]
    part_ref[...] = flat_rows(z, thick_ref) - change


def ahead_waves(z, shares, sorted_ref):
    sums = unpack(sum(ref[...] for ref in shares), z.ahead)
    return coefficients(z, sums, sorted_ref[: z.ahead, MORE : MORE + 1])


def send_spectra(z, east_ref, sorted_ref, *rest):
    shares, send_ref, waves_ref = rest[:-2], rest[-2], rest[-1]
    waves = ahead_waves(z, shares, sorted_ref)
    waves_ref[...] = waves
    part = sector_part(z, waves, lax.axis_index("lon"))
    send_ref[0] = east_ref[...]
    send_ref[1] = part[: z.helped].reshape(east_ref.shape)


def ahead_inverse(z, phase_ref, waves_ref, basis_ref, high_ref, low_ref, lhs_ref, rows_ref):
    @pl.when(on_polar_band(z))
    def _():
        inverse_rows(z, waves_ref[...], basis_ref, phase_ref, lhs_ref, rows_ref)
        high_ref[...], low_ref[...] = split(rows_ref[...])


def north_inverse(
    z, active, depth_ref, north_ref, part_ref, row_ref, phase_ref, chosen_ref, sorted_ref, waves_ahead,
    high_ahead, low_ahead, *rest,
):
    shares, rest = rest[: z.n_lon], rest[z.n_lon :]
    basis_ref, final_ref, thick_ref, column_ref, keep_ref, lhs_ref, rows_ref, high_ref, low_ref = rest

    @pl.when(active & on_polar_band(z))
    def _():
        more = z.ahead - 8
        sums = unpack(sum(ref[...] for ref in shares), z.rows - z.ahead)
        waves = coefficients(z, sums, sorted_ref[z.ahead :, MORE : MORE + 1])
        both = jnp.concatenate([waves_ahead[more:], waves], axis=0)
        part = sector_part(z, both, lax.axis_index("lon"))
        first = z.helped - more
        keep_ref[...] = part[first : first + z.helped].reshape(keep_ref.shape)
        inverse_rows(z, waves, basis_ref, phase_ref, lhs_ref, rows_ref, slice(z.rows - z.ahead))
        count = high_ref.shape[0] - z.ahead
        rest_high, rest_low = split(pad_rows(rows_ref[: z.rows - z.ahead], count))
        high_ref[: z.ahead], low_ref[: z.ahead] = high_ahead[...], low_ahead[...]
        high_ref[z.ahead :], low_ref[z.ahead :] = rest_high, rest_low
        chosen = chosen_ref[...].astype(jnp.bfloat16)
        rows_ref[...] = jnp.dot(
            chosen, high_ref[...], preferred_element_type=jnp.float32
        ) + jnp.dot(chosen, low_ref[...], preferred_element_type=jnp.float32)
        beyond = slice(z.own, z.rows)
        polar = column_of(row_ref, POLAR)[beyond] > 0.0
        rows_ref[beyond, : z.lon] = jnp.where(polar, rows_ref[beyond, : z.lon], north_ref[beyond])

    @pl.when(active & jnp.logical_not(on_polar_band(z)))
    def _():
        keep_ref[...] = jnp.zeros_like(keep_ref)
        beyond = slice(z.own, z.rows)
        at = slice(z.own - z.ahead, z.rows - z.ahead)
        sums = unpack(sum(ref[...] for ref in shares), z.rows - z.ahead)
        waves = coefficients(z, sums[at], sorted_ref[beyond, MORE : MORE + 1])
        inverse_rows(z, waves, basis_ref, phase_ref, lhs_ref, rows_ref, beyond)
        polar = column_of(row_ref, POLAR)[beyond] > 0.0
        rows_ref[beyond, : z.lon] = jnp.where(polar, rows_ref[beyond, : z.lon], north_ref[beyond])
        rows_ref[: z.own, : z.lon] = north_ref[: z.own]

    @pl.when(active)
    def _():
        final = rows_ref[:, : z.lon]
        final_ref[...] = final[: z.own].reshape(final_ref.shape)
        scaled = final * column_of(row_ref, COSINE)
        diff = (roll(scaled, -z.lev, 0) - roll(scaled, z.lev, 0))[: z.own]
        scale = depths(z, depth_ref, row_ref) * column_of(row_ref, NORTH_COEF)[: z.own]
        thick_ref[...] = (part_ref[...] - scale * diff).reshape(thick_ref.shape)
        column_ref[...] = sum(thick_ref[:, lev, :] for lev in range(z.lev))


def sends_column():
    return lax.axis_index("lev") > 0


def north_deeper(z, *refs):
    north_inverse(z, sends_column(), *refs)


def north_shallowest(z, east_keep, north_keep, arrived_ref, *rest):
    *refs, spectra_ref, column_ref, keep_ref, lhs_ref, rows_ref, high_ref, low_ref = rest
    active = jnp.logical_not(sends_column())
    north_inverse(z, active, *refs, column_ref, keep_ref, lhs_ref, rows_ref, high_ref, low_ref)

    @pl.when(sends_column())
    def _():
        keep_ref[...] = north_keep[...]

    polar = on_polar_band(z)
    spectra_ref[0] = jnp.where(polar, east_keep[...], arrived_ref[0])
    spectra_ref[1] = jnp.where(polar, keep_ref[...], arrived_ref[1])


def finish(z, surface_ref, *rest):
    deeper_fields, own_fields, deeper, outs = rest[:2], rest[2:4], rest[4 : 3 + z.n_lev], rest[3 + z.n_lev :]
    final_out, thick_out, geo_out, geo_ref, sems = outs

    def store(fields):
        copies = [
            pltpu.make_async_copy(*pair, sems.at[n])
            for n, pair in enumerate(zip(fields, (final_out, thick_out), strict=True))
        ]
        for copy in copies:
            copy.start()
        for n in range(z.cuts):
            at = slice(n * z.lat // z.cuts, (n + 1) * z.lat // z.cuts)
            column = sum(ref[at] for ref in deeper)
            for lev in reversed(range(z.lev)):
                column = column + fields[1][at, lev, :]
                geo_ref[at, lev, :] = surface_ref[at] + GRAVITY * column
            copies.append(pltpu.make_async_copy(geo_ref.at[at], geo_out.at[at], sems.at[2 + n]))
            copies[-1].start()
        for copy in copies:
            copy.wait()

    @pl.when(sends_column())
    def _():
        store(deeper_fields)

    @pl.when(jnp.logical_not(sends_column()))
    def _():
        store(own_fields)


def call(kernel, n_in, out_shape, scratch, micros, spaces=None, in_hbm=0, vmem=24):
    vmem_spec = pl.BlockSpec(memory_space=pltpu.VMEM)
    spaces = spaces or {}
    return pl.pallas_call(
        kernel,
        in_specs=[
            pl.BlockSpec(memory_space=spaces[n]) if n in spaces else vmem_spec for n in range(n_in)
        ],
        out_specs=[pl.BlockSpec(memory_space=pltpu.HBM)] * in_hbm
        + [vmem_spec] * (len(out_shape) - in_hbm),
        out_shape=[
            jax.ShapeDtypeStruct(s, jnp.float32) if isinstance(s, tuple) else s for s in out_shape
        ],
        scratch_shapes=scratch,
        compiler_params=pltpu.CompilerParams(vmem_limit_bytes=vmem * MIB),
        cost_estimate=pl.CostEstimate(
            flops=int(micros * 1.15e9), bytes_accessed=0, transcendentals=0
        ),
    )


def shifted(block, axis, distance):
    count = lax.axis_size(axis)
    return lax.ppermute(block, axis, [(i, (i + distance) % count) for i in range(count)])


def level_inside(x):
    return jnp.swapaxes(x, -3, -2)


def local(
    wind_east, wind_north, thickness, geopot, surface_geopot, mean_depth, kept_modes, slot_table
):
    z = Sizes(thickness.shape, {axis: lax.axis_size(axis) for axis in ("lat", "lon", "lev")})
    wind_east, wind_north, thickness, geopot = (
        level_inside(x) for x in (wind_east, wind_north, thickness, geopot)
    )
    field = (z.lat, z.lev, z.lon)
    forward, inverse = (jnp.asarray(x) for x in basis_tables(z))
    phase = jnp.asarray(phase_table(z))
    per_row = jnp.asarray(row_table(z))
    kept = kept_modes[None, :]
    slots = slot_table[None, :]
    payload = (z.rows, WIDE)
    rims = (4 * z.lev, z.lon)
    spec = (z.help, z.lev, z.spec_width)
    waves_lhs = pltpu.VMEM((z.ext // z.inverse_block * z.mm_rows, 3 * WIDE), jnp.bfloat16)

    row_shape, phase_shape = per_row.shape[1:], phase.shape[1:]
    pinned = [
        pltpu.with_memory_space_constraint(x, pltpu.HBM)
        for x in (wind_east, wind_north, geopot, per_row, phase, forward)
    ]
    columns_lhs = pltpu.VMEM((z.blocks * z.mm_rows, 3 * BLOCK), jnp.bfloat16)
    waves_lhs = pltpu.VMEM((z.ext // z.inverse_block * z.mm_rows, 3 * WIDE), jnp.bfloat16)

    share_first, to_even, to_odd, wind_east, wind_north, geopot, per_row, phase, forward = call(
        functools.partial(east_first, z),
        6,
        [(packed_rows(z.first), 128), rims, rims]
        + [pltpu.VMEM(s, jnp.float32) for s in (field, field, field, row_shape, phase_shape)]
        + [pltpu.VMEM(forward.shape, forward.dtype)],
        [
            columns_lhs,
            pltpu.VMEM((z.first, WIDE), jnp.float32),
            pltpu.SemaphoreType.DMA((12,)),
        ],
        1,
        {n: pltpu.HBM for n in range(6)},
    )(*pinned)
    second = round_up(z.own - z.first, 8)
    (share_second,) = call(
        functools.partial(east_shares_of, z, slice(z.first, z.own)),
        6,
        [(packed_rows(second), 128)],
        [columns_lhs, pltpu.VMEM((second, WIDE), jnp.float32)],
        0.18,
    )(wind_east, wind_north, geopot, per_row, phase, forward)
    east_firsts, east_seconds = (
        [x] + [shifted(x, "lon", s) for s in range(1, z.n_lon)] for x in (share_first, share_second)
    )
    met = []
    for start, rim in enumerate((to_even, to_odd)):
        pairs = [(i, i + 1) for i in range(start, z.n_lat - 1, 2)]
        met.append(lax.ppermute(rim, "lat", pairs + [(b, a) for a, b in pairs]))

    places = round_up(z.rows, 128)
    north_ahead, north_rest, north_new, chosen, kept_sorted = call(
        functools.partial(north_forward, z),
        10,
        [
            (packed_rows(z.ahead), 128),
            (packed_rows(z.rows - z.ahead), 128),
            (z.rows, z.lon),
            (z.rows, places),
            (z.rows, 128),
        ],
        [
            pltpu.VMEM((z.rows, z.lon), jnp.float32),
            columns_lhs,
            pltpu.VMEM((z.rows, WIDE), jnp.float32),
        ],
        0.8,
    )(
        wind_east, wind_north, geopot, *met, per_row, phase, forward, kept, slots
    )
    north_rests = [north_rest] + [shifted(north_rest, "lon", s) for s in range(1, z.n_lon)]
    polar_bands = [i for i in range(z.n_lat) if i < z.n_lat // 4 or i >= z.n_lat - z.n_lat // 4]
    north_aheads = [north_ahead]
    for distance in range(1, z.n_lon):
        route = [
            (band * z.n_lon + lon, band * z.n_lon + (lon + distance) % z.n_lon)
            for band in polar_bands
            for lon in range(z.n_lon)
        ]
        north_aheads.append(lax.ppermute(north_ahead, ("lat", "lon"), route))

    (first_here,) = call(arrival, 1, [(8, 128)], [], 0.95)(east_firsts[1])
    east_final, thick_part, east_keep, east_send = call(
        functools.partial(east_inverse, z),
        11 + 2 * z.n_lon,
        [field, (z.own, z.lon), spec, spec],
        [
            waves_lhs,
            pltpu.VMEM((z.own, z.ext), jnp.float32),
            pltpu.VMEM((z.own, WIDE), jnp.float32),
        ],
        1,
        {0: pltpu.SMEM},
    )(
        mean_depth, wind_east, wind_north, geopot, thickness, per_row, phase, kept, chosen,
        first_here, *east_firsts, *east_seconds, inverse,
    )

    to_helper, waves_ahead = call(
        functools.partial(send_spectra, z), 2 + z.n_lon, [(2, *spec), (z.ahead, WIDE)], [], 0.1
    )(east_send, kept_sorted, *north_aheads)
    arrived = lax.ppermute(
        to_helper, "lat", [(i, (i + z.half_axis) % z.n_lat) for i in polar_bands]
    )

    ahead_rows = jax.ShapeDtypeStruct((z.ahead, z.ext), jnp.bfloat16)
    ahead_high, ahead_low = call(
        functools.partial(ahead_inverse, z),
        3,
        [ahead_rows] * 2,
        [waves_lhs, pltpu.VMEM((z.ahead, z.ext), jnp.float32)],
        0.5,
    )(phase, waves_ahead, inverse)

    operands = (
        mean_depth, north_new, thick_part, per_row, phase, chosen, kept_sorted, waves_ahead,
        ahead_high, ahead_low, *north_rests, inverse,
    )
    in_vmem = pltpu.VMEM(field, jnp.float32)
    scratch = [waves_lhs, pltpu.VMEM((z.rows, z.ext), jnp.float32)]
    scratch += [pltpu.VMEM((places, z.ext), jnp.bfloat16)] * 2
    final_deeper, thick_deeper, column, north_keep = call(
        functools.partial(north_deeper, z),
        len(operands),
        [in_vmem, in_vmem, (z.lat, z.lon), spec],
        scratch,
        2,
        {0: pltpu.SMEM},
    )(*operands)
    deeper = [
        lax.ppermute(column, "lev", [(i, i - distance) for i in range(distance, z.n_lev)])
        for distance in range(1, z.n_lev)
    ]
    final_own, thick_own, spectra = call(
        functools.partial(north_shallowest, z),
        3 + len(operands),
        [in_vmem, in_vmem, (2, *spec)],
        [pltpu.VMEM((z.lat, z.lon), jnp.float32), pltpu.VMEM(spec, jnp.float32)] + scratch,
        3.2,
        {3: pltpu.SMEM},
    )(east_keep, north_keep, arrived, *operands)
    north_final, thick_new, geo_new = call(
        functools.partial(finish, z),
        5 + len(deeper),
        [pltpu.HBM(field, jnp.float32)] * 3,
        [pltpu.VMEM(field, jnp.float32), pltpu.SemaphoreType.DMA((2 + z.cuts,))],
        1,
        in_hbm=3,
    )(surface_geopot, final_deeper, thick_deeper, final_own, thick_own, *deeper)
    return tuple(level_inside(x) for x in (east_final, north_final, thick_new, geo_new, spectra))


def solution(mesh):
    field = P(("members", "lev"), "lat", "lon")
    return jax.shard_map(
        local,
        mesh=mesh,
        in_specs=(field, field, field, field, P("lat", "lon"), P("lev"), P(), P()),
        out_specs=(field, field, field, field, P(None, ("members", "lev"), "lat", "lon")),
        check_vma=False,
    )
```

```python
import functools
import math

import jax
import jax.numpy as jnp
import numpy as np
from jax import lax
from jax.experimental import pallas as pl
from jax.experimental.pallas import tpu as pltpu
from jax.sharding import PartitionSpec as P

KMAX = 360
HALF = 384
WIDE = 2 * HALF
SPARE = HALF - 128
MORE = KMAX - SPARE
MOVED = 128 - MORE
LEFT = MORE - MOVED
BLOCK = 256
INVERSE_BLOCK = 768

STEP_FACTOR = 0.15
CORIOLIS = 0.2
GRAVITY = 0.25

MIB = 1024 * 1024

EAST_COEF, SINE, COSINE, NORTH_COEF, LEVEL, POLAR, NUMBER, OWN = range(8)


def round_up(value, step):
    return -(-value // step) * step


class Sizes:
    def __init__(self, shape, counts):
        self.lev, self.lat, self.lon = shape
        self.n_lat, self.n_lon, self.n_lev = counts["lat"], counts["lon"], counts["lev"]
        self.nlat, self.nlon = self.lat * self.n_lat, self.lon * self.n_lon
        self.polar = self.nlat // 4
        self.help = self.lat // 2
        self.half_axis = self.n_lat // 2
        self.own = self.lat * self.lev
        self.rows = self.own + 2 * self.lev
        assert self.rows % 8 == 0
        self.mm_rows = round_up(self.rows, 16)
        self.ext = round_up(self.lon + 4, BLOCK)
        self.blocks = self.ext // BLOCK
        self.inverse_block = min(INVERSE_BLOCK, self.ext)
        assert self.ext % self.inverse_block == 0
        self.spec_width = 2 * KMAX // self.n_lon
        self.helped = self.help * self.lev
        self.ahead = round_up(self.helped, 16)
        self.cuts = 2
        self.first = min(round_up(self.own * 4 // 9, 8 * self.lev), self.own)


def high_low(x):
    x = x.astype(np.float32)
    high = x.astype(jnp.bfloat16)
    return high, (x - high.astype(np.float32)).astype(jnp.bfloat16)


def basis_tables(z):
    k = np.arange(KMAX)
    angle = (np.arange(z.inverse_block)[:, None] * k[None, :] % z.nlon) * (2.0 * np.pi / z.nlon)
    full = np.zeros((z.inverse_block, WIDE))
    full[:, :KMAX] = np.cos(angle)
    full[:, HALF : HALF + KMAX] = np.sin(angle)
    high, low = high_low(full)
    forward = np.concatenate([high[:BLOCK], high[:BLOCK], low[:BLOCK]], axis=0)
    inverse = np.concatenate([high.T, high.T, low.T], axis=0)
    return forward, inverse


def phase_table(z):
    k = np.arange(KMAX)
    table = np.zeros((z.n_lon, round_up(2 * z.blocks + 2, 8), HALF), np.float32)
    for place in range(z.n_lon):
        for n, column in enumerate([*range(0, z.ext, BLOCK), -1]):
            angle = ((place * z.lon + column) * k % z.nlon) * (2.0 * np.pi / z.nlon)
            table[place, 2 * n, :KMAX] = np.cos(angle)
            table[place, 2 * n + 1, :KMAX] = np.sin(angle)
    return table


def row_table(z):
    lam_step = np.float32(2.0 * math.pi / z.nlon)
    phi_step = np.float32(math.pi / z.nlat)
    latitude = np.float32(-0.5 * math.pi) + (
        np.arange(z.nlat, dtype=np.float32) + np.float32(0.5)
    ) * phi_step
    cosine = np.cos(latitude.astype(np.float64)).astype(np.float32)
    sine = np.sin(latitude.astype(np.float64)).astype(np.float32)
    north_coef = np.float32(STEP_FACTOR) * lam_step / phi_step
    table = np.zeros((z.n_lat, z.rows, 8), np.float32)
    for place in range(z.n_lat):
        for flat in range(z.rows):
            inner, level = flat // z.lev, flat % z.lev
            inner = -1 if inner == z.lat + 1 else inner
            row = place * z.lat + inner
            one = table[place, flat]
            one[LEVEL], one[NUMBER] = level, -1
            one[OWN] = 0 <= inner < z.lat
            if 0 <= row < z.nlat:
                one[EAST_COEF] = np.float32(STEP_FACTOR) / cosine[row]
                one[SINE], one[COSINE] = sine[row], cosine[row]
                one[NORTH_COEF] = north_coef / cosine[row]
                if row < z.polar:
                    one[POLAR], one[NUMBER] = 1, row
                elif row >= z.nlat - z.polar:
                    one[POLAR], one[NUMBER] = 1, row - (z.nlat - 2 * z.polar)
    return table


def on_polar_band(z):
    lat_index = lax.axis_index("lat")
    return (lat_index < z.n_lat // 4) | (lat_index >= z.n_lat - z.n_lat // 4)


def split(x):
    high = x.astype(jnp.bfloat16)
    return high, (x - high.astype(jnp.float32)).astype(jnp.bfloat16)


def store_split(lhs_ref, first_row, x):
    rows, width = x.shape
    high, low = split(x)
    at = slice(first_row, first_row + rows)
    lhs_ref[at, :width] = high
    lhs_ref[at, width : 2 * width] = low
    lhs_ref[at, 2 * width :] = high


def pad_rows(x, rows):
    if x.shape[0] == rows:
        return x
    return jnp.concatenate([x, jnp.zeros((rows - x.shape[0], x.shape[1]), x.dtype)], axis=0)


def phase_of(phase_ref, n):
    return phase_ref[2 * n : 2 * n + 1], phase_ref[2 * n + 1 : 2 * n + 2]


def packed_rows(rows):
    return 5 * rows + round_up(-(-rows // 2), 8) + 16


def lanes_of(x):
    return lax.broadcasted_iota(jnp.int32, x.shape, 1)


def pack(x, out_ref):
    rows = x.shape[0]
    half = round_up(-(-rows // 2), 8)
    tiles = [x[:, n : n + 128] for n in range(0, WIDE, 128)]
    left = tiles[5]
    lane = lanes_of(left)
    tiles[2] = jnp.where(lane < MORE, tiles[2], roll(left, MOVED, 1))
    for n in range(5):
        out_ref[n * rows : (n + 1) * rows] = tiles[n]
    lower = pad_rows(left[half:], half)
    out_ref[5 * rows : 5 * rows + half] = jnp.where(lane[:half] < 64, left[:half], roll(lower, 64, 1))
    out_ref[5 * rows + half :] = pad_rows(roll(left, -64, 1), 128).T[:16]


def unpack(x, rows):
    half = round_up(-(-rows // 2), 8)
    tiles = [x[n * rows : (n + 1) * rows] for n in range(5)]
    pairs = x[5 * rows : 5 * rows + half]
    ends = pad_rows(x[5 * rows + half :], 128).T[:rows]
    left = jnp.concatenate([pairs, roll(pairs, 64, 1)[: rows - half]], axis=0)
    lane = lanes_of(left)
    left = jnp.where(lane < 64, left, jnp.where(lane < LEFT, roll(ends, 64, 1), roll(tiles[2], -MOVED, 1)))
    return jnp.concatenate([*tiles, left], axis=1)


def forward_sums(
    z, x, basis_ref, phase_ref, lhs_ref, out_ref, at=slice(None), basis_here=None
):
    count = round_up(x.shape[0], 16)
    for block in range(z.blocks):
        part = pad_rows(x[:, block * BLOCK : (block + 1) * BLOCK], count)
        store_split(lhs_ref, block * count, part)
    lhs = lhs_ref[: z.blocks * count]
    if basis_here is not None:
        basis_here()
    sums = jnp.dot(lhs, basis_ref[...], preferred_element_type=jnp.float32)
    real = imag = None
    for block in range(z.blocks):
        cos, sin = phase_of(phase_ref, block)
        part = sums[block * count : block * count + x.shape[0]]
        a, b = part[:, :HALF], part[:, HALF:]
        more_real, more_imag = a * cos - b * sin, a * sin + b * cos
        real = more_real if real is None else real + more_real
        imag = more_imag if imag is None else imag + more_imag
    out_ref[at, :HALF] = real
    out_ref[at, HALF:] = imag


def inverse_rows(z, coef, basis_ref, phase_ref, lhs_ref, out_ref, at=slice(None)):
    a, b = coef[:, :HALF], coef[:, HALF:]
    count, width = round_up(coef.shape[0], 16), z.inverse_block
    blocks = range(z.ext // width)
    for block in blocks:
        cos, sin = phase_of(phase_ref, block * width // BLOCK)
        turned = jnp.concatenate([a * cos + b * sin, b * cos - a * sin], axis=1)
        store_split(lhs_ref, block * count, pad_rows(turned, count))
    lhs = lhs_ref[: len(blocks) * count]
    rows = jnp.dot(lhs, basis_ref[...], preferred_element_type=jnp.float32)
    for block in blocks:
        out_ref[at, block * width : (block + 1) * width] = rows[
            block * count : block * count + coef.shape[0]
        ]


def roll(x, shift, axis):
    return pltpu.roll(x, shift % x.shape[axis], axis)


def east_diff(x):
    return roll(x, -1, 1) - roll(x, 1, 1)


def flat_rows(z, ref):
    return ref[...].reshape(z.own, ref.shape[2])


def widen(z, x):
    return jnp.concatenate([x, jnp.zeros((x.shape[0], z.ext - x.shape[1]), x.dtype)], axis=1)


def put_lane(x, at, column):
    lane = lax.broadcasted_iota(jnp.int32, x.shape, 1)
    return jnp.where(lane == at, column, x)


def column_of(row_ref, which):
    return row_ref[:, which : which + 1]


def north_factor(z):
    return STEP_FACTOR * (2.0 * math.pi / z.nlon) / (math.pi / z.nlat)


def look_up(number, table_ref):
    table = table_ref[...].astype(jnp.float32)
    lane = lax.broadcasted_iota(jnp.int32, (number.shape[0], table.shape[1]), 1)
    return jnp.sum(jnp.where(lane == number, table, 0.0), axis=1, keepdims=True)


def coefficients(z, sums, kept):
    lane = lax.broadcasted_iota(jnp.int32, (1, WIDE), 1)
    k = jnp.where(lane < HALF, lane, lane - HALF)
    weight = jnp.where(k == 0, 1.0 / z.nlon, 2.0 / z.nlon).astype(jnp.float32)
    keep = (k.astype(jnp.float32) < kept) & (k < KMAX)
    return jnp.where(keep, sums * weight, 0.0)


def slot_order(z, number, row_ref, slot_ref):
    lat_index = lax.axis_index("lat")
    slot = look_up(number, slot_ref).astype(jnp.int32)
    theirs = slot - lax.rem(lat_index + z.half_axis, z.n_lat) * z.help
    mine = slot - lat_index * z.help
    level = column_of(row_ref, LEVEL).astype(jnp.int32)
    flat = lax.broadcasted_iota(jnp.int32, slot.shape, 0)
    place = jnp.where((mine >= 0) & (mine < z.help), z.helped + mine * z.lev + level, -1)
    place = jnp.where((theirs >= 0) & (theirs < z.help), theirs * z.lev + level, place)
    place = jnp.where(number >= 0, place, -1)
    place = jnp.where(flat < z.own, place, flat)
    lane = lax.broadcasted_iota(jnp.int32, (z.rows, round_up(z.rows, 128)), 1)
    return (lane == place).astype(jnp.float32)


def reorder(chosen, values):
    high, low = (
        lax.dot_general(
            chosen.astype(jnp.bfloat16),
            part,
            (((0,), (0,)), ((), ())),
            preferred_element_type=jnp.float32,
        )
        for part in split(values)
    )
    return high + low


def sector_part(z, coef, place):
    part = None
    for one in range(z.n_lon):
        first = one * z.spec_width
        first = first if first < KMAX else first - KMAX + HALF
        this = coef[:, first : first + z.spec_width]
        part = this if part is None else jnp.where(place == one, this, part)
    return part


def depths(z, depth_ref, row_ref):
    level = column_of(row_ref, LEVEL)[: z.own]
    depth = jnp.zeros_like(level)
    for lev in range(z.lev):
        depth = jnp.where(level == lev, depth_ref[lev], depth)
    return depth


def store_rims(z, ref, g, we, wn, last):
    edge = 2 * z.lev
    ref[:edge] = g[z.own - edge :] if last else g[:edge]
    ref[edge : edge + z.lev] = we[z.own - z.lev :] if last else we[: z.lev]
    ref[edge + z.lev :] = wn[z.own - z.lev :] if last else wn[: z.lev]


def east_shares_of(
    z, at, we_ref, wn_ref, g_ref, row_ref, phase_ref, basis_ref, out_ref, lhs_ref, share_ref,
    basis_here=None,
):
    inner, rows = slice(at.start // z.lev, at.stop // z.lev), at.stop - at.start
    g, we, wn = (ref[inner].reshape(rows, z.lon) for ref in (g_ref, we_ref, wn_ref))

    @pl.when(on_polar_band(z))
    def _():
        coef, sine = column_of(row_ref, EAST_COEF)[at], column_of(row_ref, SINE)[at]
        new = widen(z, we + CORIOLIS * sine * wn) - coef * east_diff(widen(z, g))
        tail = put_lane(new[:, z.ext - 128 :], 127, 0.0)
        new = jnp.concatenate([new[:, : z.ext - 128], tail], axis=1)
        forward_sums(
            z, new, basis_ref, phase_ref, lhs_ref, share_ref, slice(rows), basis_here=basis_here
        )
        cos, sin = phase_of(phase_ref, z.blocks)
        before = -coef * g[:, 0:1]
        share_ref[:rows, :HALF] += before * cos
        share_ref[:rows, HALF:] += before * sin
        pack(share_ref[...], out_ref)

    @pl.when(jnp.logical_not(on_polar_band(z)))
    def _():
        if basis_here is not None:
            basis_here()
        last = z.lon - 1
        columns = jnp.zeros((rows, 128), jnp.float32)
        edges = ((g, last - 1), (g, last), (we, last), (wn, last), (g, 0), (g, 1), (we, 0), (wn, 0))
        for n, (x, column) in enumerate(edges):
            columns = put_lane(columns, n, x[:, column : column + 1])
        out_ref[...] = jnp.zeros_like(out_ref)
        out_ref[:rows] = columns


def east_first(
    z, we_hbm, wn_hbm, g_hbm, row_hbm, phase_hbm, basis_hbm,
    share_ref, even_ref, odd_ref, we_ref, wn_ref, g_ref, row_ref, phase_ref, basis_ref, lhs_ref, sums_ref, sems,
):
    fields = ((g_hbm, g_ref), (we_hbm, we_ref), (wn_hbm, wn_ref))
    cut, rim = z.first // z.lev, z.lat - 2

    def copies(first_sem, pairs):
        return [pltpu.make_async_copy(*pair, sems.at[first_sem + n]) for n, pair in enumerate(pairs)]

    tables = copies(
        0,
        (
            (row_hbm.at[lax.axis_index("lat")], row_ref),
            (phase_hbm.at[lax.axis_index("lon")], phase_ref),
        ),
    )
    first = copies(2, [(a.at[:cut], b.at[:cut]) for a, b in fields])
    basis = copies(5, [(basis_hbm, basis_ref)])
    edge = copies(6, [(a.at[rim:], b.at[rim:]) for a, b in fields])
    between = copies(9, [(a.at[cut:rim], b.at[cut:rim]) for a, b in fields])
    for copy in first + tables + basis + edge:
        copy.start()
    for copy in first + tables:
        copy.wait()
    for copy in between:
        copy.start()

    def basis_here():
        for copy in basis + edge:
            copy.wait()

    east_shares_of(
        z, slice(0, z.first), we_ref, wn_ref, g_ref, row_ref, phase_ref, basis_ref, share_ref, lhs_ref,
        sums_ref, basis_here,
    )
    odd = lax.rem(lax.axis_index("lat"), 2) == 1
    last, flat = z.lat - 1, (z.lev, z.lon)
    far = (g_ref[last - 1], g_ref[last], we_ref[last], wn_ref[last])
    near = (g_ref[0], g_ref[1], we_ref[0], wn_ref[0])
    for n, (bottom, top) in enumerate(zip(far, near, strict=True)):
        at = slice(n * z.lev, (n + 1) * z.lev)
        even_ref[at] = jnp.where(odd, top, bottom).reshape(flat)
        odd_ref[at] = jnp.where(odd, bottom, top).reshape(flat)
    for copy in between:
        copy.wait()


def north_forward(
    z, we_ref, wn_ref, g_ref, even_ref, odd_ref, row_ref, phase_ref, basis_ref, kept_ref, slot_ref, *rest
):
    ahead_ref, rest_ref, north_ref, chosen_ref, sorted_ref, g_rows, lhs_ref, share_ref = rest
    edge, lev = 2 * z.lev, z.lev
    odd = lax.rem(lax.axis_index("lat"), 2) == 1
    below = jnp.where(odd, odd_ref[...], even_ref[...])
    above = jnp.where(odd, even_ref[...], odd_ref[...])
    coef, sine = north_factor(z), CORIOLIS * column_of(row_ref, SINE)
    own = flat_rows(z, g_ref)
    g_rows[: z.own] = own
    g_rows[z.own : z.own + lev] = below[:lev]
    g_rows[z.own + lev :] = above[lev:edge]
    g = g_rows[...]
    diff = (roll(g, -lev, 0) - roll(g, lev, 0))[: z.own]
    north_ref[: z.own] = flat_rows(z, wn_ref) - coef * diff - sine[: z.own] * flat_rows(z, we_ref)
    for at, diff, rim in (
        (z.own, below[lev:edge] - own[z.own - lev :], below),
        (z.own + lev, own[:lev] - above[:lev], above),
    ):
        we, wn = rim[edge : edge + lev], rim[edge + lev :]
        north_ref[at : at + lev] = wn - coef * diff - sine[at : at + lev] * we
    number = column_of(row_ref, NUMBER).astype(jnp.int32)
    kept = look_up(number, kept_ref)

    @pl.when(on_polar_band(z))
    def _():
        forward_sums(z, widen(z, north_ref[...]), basis_ref, phase_ref, lhs_ref, share_ref)
        share_ref[:, SPARE:HALF] = put_lane(share_ref[:, SPARE:HALF], KMAX - SPARE, kept)
        chosen = slot_order(z, number, row_ref, slot_ref)
        ordered = reorder(chosen, share_ref[...])
        pack(ordered[: z.ahead], ahead_ref)
        pack(ordered[z.ahead : z.rows], rest_ref)
        sorted_ref[...] = ordered[: z.rows, SPARE:HALF]
        chosen_ref[...] = chosen

    @pl.when(jnp.logical_not(on_polar_band(z)))
    def _():
        ahead_ref[...] = jnp.zeros_like(ahead_ref)
        chosen_ref[...] = jnp.zeros_like(chosen_ref)
        share_ref[...] = jnp.zeros_like(share_ref)
        rows = widen(z, north_ref[z.own :])
        forward_sums(z, rows, basis_ref, phase_ref, lhs_ref, share_ref, slice(z.own, z.rows))
        pack(share_ref[z.ahead :], rest_ref)
        sorted_ref[...] = jnp.broadcast_to(kept, sorted_ref.shape)


def arrival(arrived_ref, out_ref):
    out_ref[...] = arrived_ref[:8, :128]


def east_inverse(
    z, depth_ref, we_ref, wn_ref, g_ref, thick_ref, row_ref, phase_ref, kept_ref, chosen_ref, first_here,
    *rest,
):
    del first_here
    firsts, seconds, rest = rest[: z.n_lon], rest[z.n_lon : 2 * z.n_lon], rest[2 * z.n_lon :]
    basis_ref, final_ref, part_ref, keep_ref, send_ref, lhs_ref, rows_ref, sums_ref = rest
    coef, sine = column_of(row_ref, EAST_COEF)[: z.own], column_of(row_ref, SINE)[: z.own]

    @pl.when(on_polar_band(z))
    def _():
        number = column_of(row_ref, NUMBER)[: z.own].astype(jnp.int32)
        second = round_up(z.own - z.first, 8)
        sums_ref[: z.first] = unpack(sum(ref[...] for ref in firsts), z.first)
        sums_ref[z.first :] = unpack(sum(ref[...] for ref in seconds), second)[: z.own - z.first]
        waves = coefficients(z, sums_ref[...], look_up(number, kept_ref))
        part = sector_part(z, waves, lax.axis_index("lon"))
        ordered = reorder(chosen_ref[: z.own], part)
        send_ref[...] = ordered[: z.helped].reshape(send_ref.shape)
        keep_ref[...] = ordered[z.helped : 2 * z.helped].reshape(keep_ref.shape)
        inverse_rows(z, waves, basis_ref, phase_ref, lhs_ref, rows_ref)
        cos, sin = phase_of(phase_ref, z.blocks)
        before = jnp.sum(waves[:, :HALF] * cos + waves[:, HALF:] * sin, axis=1, keepdims=True)
        rows_ref[:, z.ext - 128 :] = put_lane(rows_ref[:, z.ext - 128 :], 127, before)

    @pl.when(jnp.logical_not(on_polar_band(z)))
    def _():
        send_ref[...] = jnp.zeros_like(send_ref)
        keep_ref[...] = jnp.zeros_like(keep_ref)
        left, right = (
            jnp.concatenate([firsts[n][: z.first], seconds[n][: z.own - z.first]], axis=0)
            for n in (1, -1)
        )
        at_right = z.lon - (z.ext - 128)

        def rimmed(ref, left_of, right_of):
            x = widen(z, flat_rows(z, ref))
            tail = x[:, z.ext - 128 :]
            for n, lane in enumerate(right_of):
                tail = put_lane(tail, at_right + n, right[:, lane : lane + 1])
            for n, lane in enumerate(left_of):
                tail = put_lane(tail, 127 - n, left[:, lane : lane + 1])
            return jnp.concatenate([x[:, : z.ext - 128], tail], axis=1)

        g = rimmed(g_ref, (1, 0), (4, 5))
        we, wn = rimmed(we_ref, (2,), (6,)), rimmed(wn_ref, (3,), (7,))
        rows_ref[...] = we - coef * east_diff(g) + CORIOLIS * sine * wn

    final = rows_ref[...]
    final_ref[...] = final[:, : z.lon].reshape(final_ref.shape)
    change = depths(z, depth_ref, row_ref) * coef * east_diff(final)[:, : z.lon]
    part_ref[...] = flat_rows(z, thick_ref) - change


def ahead_waves(z, shares, sorted_ref):
    sums = unpack(sum(ref[...] for ref in shares), z.ahead)
    return coefficients(z, sums, sorted_ref[: z.ahead, MORE : MORE + 1])


def send_spectra(z, east_ref, sorted_ref, *rest):
    shares, send_ref, waves_ref = rest[:-2], rest[-2], rest[-1]
    waves = ahead_waves(z, shares, sorted_ref)
    waves_ref[...] = waves
    part = sector_part(z, waves, lax.axis_index("lon"))
    send_ref[0] = east_ref[...]
    send_ref[1] = part[: z.helped].reshape(east_ref.shape)


def ahead_inverse(z, phase_ref, waves_ref, basis_ref, high_ref, low_ref, lhs_ref, rows_ref):
    @pl.when(on_polar_band(z))
    def _():
        inverse_rows(z, waves_ref[...], basis_ref, phase_ref, lhs_ref, rows_ref)
        high_ref[...], low_ref[...] = split(rows_ref[...])


def north_inverse(
    z, active, depth_ref, north_ref, part_ref, row_ref, phase_ref, chosen_ref, sorted_ref, waves_ahead,
    high_ahead, low_ahead, *rest,
):
    shares, rest = rest[: z.n_lon], rest[z.n_lon :]
    basis_ref, final_ref, thick_ref, column_ref, keep_ref, lhs_ref, rows_ref, high_ref, low_ref = rest

    @pl.when(active & on_polar_band(z))
    def _():
        more = z.ahead - 8
        sums = unpack(sum(ref[...] for ref in shares), z.rows - z.ahead)
        waves = coefficients(z, sums, sorted_ref[z.ahead :, MORE : MORE + 1])
        both = jnp.concatenate([waves_ahead[more:], waves], axis=0)
        part = sector_part(z, both, lax.axis_index("lon"))
        first = z.helped - more
        keep_ref[...] = part[first : first + z.helped].reshape(keep_ref.shape)
        inverse_rows(z, waves, basis_ref, phase_ref, lhs_ref, rows_ref, slice(z.rows - z.ahead))
        count = high_ref.shape[0] - z.ahead
        rest_high, rest_low = split(pad_rows(rows_ref[: z.rows - z.ahead], count))
        high_ref[: z.ahead], low_ref[: z.ahead] = high_ahead[...], low_ahead[...]
        high_ref[z.ahead :], low_ref[z.ahead :] = rest_high, rest_low
        chosen = chosen_ref[:, : z.mm_rows].astype(jnp.bfloat16)
        rows_ref[...] = jnp.dot(
            chosen, high_ref[...], preferred_element_type=jnp.float32
        ) + jnp.dot(chosen, low_ref[...], preferred_element_type=jnp.float32)
        beyond = slice(z.own, z.rows)
        polar = column_of(row_ref, POLAR)[beyond] > 0.0
        rows_ref[beyond, : z.lon] = jnp.where(polar, rows_ref[beyond, : z.lon], north_ref[beyond])

    @pl.when(active & jnp.logical_not(on_polar_band(z)))
    def _():
        keep_ref[...] = jnp.zeros_like(keep_ref)
        beyond = slice(z.own, z.rows)
        at = slice(z.own - z.ahead, z.rows - z.ahead)
        sums = unpack(sum(ref[...] for ref in shares), z.rows - z.ahead)
        waves = coefficients(z, sums[at], sorted_ref[beyond, MORE : MORE + 1])
        inverse_rows(z, waves, basis_ref, phase_ref, lhs_ref, rows_ref, beyond)
        polar = column_of(row_ref, POLAR)[beyond] > 0.0
        rows_ref[beyond, : z.lon] = jnp.where(polar, rows_ref[beyond, : z.lon], north_ref[beyond])
        rows_ref[: z.own, : z.lon] = north_ref[: z.own]

    @pl.when(active)
    def _():
        final = rows_ref[:, : z.lon]
        final_ref[...] = final[: z.own].reshape(final_ref.shape)
        scaled = final * column_of(row_ref, COSINE)
        diff = (roll(scaled, -z.lev, 0) - roll(scaled, z.lev, 0))[: z.own]
        scale = depths(z, depth_ref, row_ref) * column_of(row_ref, NORTH_COEF)[: z.own]
        thick_ref[...] = (part_ref[...] - scale * diff).reshape(thick_ref.shape)
        column_ref[...] = sum(thick_ref[:, lev, :] for lev in range(z.lev))


def sends_column():
    return lax.axis_index("lev") > 0


def north_deeper(z, *refs):
    north_inverse(z, sends_column(), *refs)


def north_shallowest(z, east_keep, north_keep, arrived_ref, *rest):
    *refs, spectra_ref, column_ref, keep_ref, lhs_ref, rows_ref, high_ref, low_ref = rest
    active = jnp.logical_not(sends_column())
    north_inverse(z, active, *refs, column_ref, keep_ref, lhs_ref, rows_ref, high_ref, low_ref)

    @pl.when(sends_column())
    def _():
        keep_ref[...] = north_keep[...]

    polar = on_polar_band(z)
    spectra_ref[0] = jnp.where(polar, east_keep[...], arrived_ref[0])
    spectra_ref[1] = jnp.where(polar, keep_ref[...], arrived_ref[1])


def finish(z, surface_ref, *rest):
    deeper_fields, own_fields, deeper, outs = rest[:2], rest[2:4], rest[4 : 3 + z.n_lev], rest[3 + z.n_lev :]
    final_out, thick_out, geo_out, geo_ref, sems = outs

    def store(fields):
        copies = [
            pltpu.make_async_copy(*pair, sems.at[n])
            for n, pair in enumerate(zip(fields, (final_out, thick_out), strict=True))
        ]
        for copy in copies:
            copy.start()
        for n in range(z.cuts):
            at = slice(n * z.lat // z.cuts, (n + 1) * z.lat // z.cuts)
            column = sum(ref[at] for ref in deeper)
            for lev in reversed(range(z.lev)):
                column = column + fields[1][at, lev, :]
                geo_ref[at, lev, :] = surface_ref[at] + GRAVITY * column
            copies.append(pltpu.make_async_copy(geo_ref.at[at], geo_out.at[at], sems.at[2 + n]))
            copies[-1].start()
        for copy in copies:
            copy.wait()

    @pl.when(sends_column())
    def _():
        store(deeper_fields)

    @pl.when(jnp.logical_not(sends_column()))
    def _():
        store(own_fields)


def call(kernel, n_in, out_shape, scratch, micros, spaces=None, in_hbm=0, vmem=24):
    vmem_spec = pl.BlockSpec(memory_space=pltpu.VMEM)
    spaces = spaces or {}
    return pl.pallas_call(
        kernel,
        in_specs=[
            pl.BlockSpec(memory_space=spaces[n]) if n in spaces else vmem_spec for n in range(n_in)
        ],
        out_specs=[pl.BlockSpec(memory_space=pltpu.HBM)] * in_hbm
        + [vmem_spec] * (len(out_shape) - in_hbm),
        out_shape=[
            jax.ShapeDtypeStruct(s, jnp.float32) if isinstance(s, tuple) else s for s in out_shape
        ],
        scratch_shapes=scratch,
        compiler_params=pltpu.CompilerParams(vmem_limit_bytes=vmem * MIB),
        cost_estimate=pl.CostEstimate(
            flops=int(micros * 1.15e9), bytes_accessed=0, transcendentals=0
        ),
    )


def shifted(block, axis, distance):
    count = lax.axis_size(axis)
    return lax.ppermute(block, axis, [(i, (i + distance) % count) for i in range(count)])


def level_inside(x):
    return jnp.swapaxes(x, -3, -2)


def local(
    wind_east, wind_north, thickness, geopot, surface_geopot, mean_depth, kept_modes, slot_table
):
    z = Sizes(thickness.shape, {axis: lax.axis_size(axis) for axis in ("lat", "lon", "lev")})
    wind_east, wind_north, thickness, geopot = (
        level_inside(x) for x in (wind_east, wind_north, thickness, geopot)
    )
    field = (z.lat, z.lev, z.lon)
    forward, inverse = (jnp.asarray(x) for x in basis_tables(z))
    phase = jnp.asarray(phase_table(z))
    per_row = jnp.asarray(row_table(z))
    kept = kept_modes[None, :]
    slots = slot_table[None, :]
    payload = (z.rows, WIDE)
    rims = (4 * z.lev, z.lon)
    spec = (z.help, z.lev, z.spec_width)
    waves_lhs = pltpu.VMEM((z.ext // z.inverse_block * z.mm_rows, 3 * WIDE), jnp.bfloat16)

    row_shape, phase_shape = per_row.shape[1:], phase.shape[1:]
    pinned = [
        pltpu.with_memory_space_constraint(x, pltpu.HBM)
        for x in (wind_east, wind_north, geopot, per_row, phase, forward)
    ]
    columns_lhs = pltpu.VMEM((z.blocks * z.mm_rows, 3 * BLOCK), jnp.bfloat16)
    waves_lhs = pltpu.VMEM((z.ext // z.inverse_block * z.mm_rows, 3 * WIDE), jnp.bfloat16)

    share_first, to_even, to_odd, wind_east, wind_north, geopot, per_row, phase, forward = call(
        functools.partial(east_first, z),
        6,
        [(packed_rows(z.first), 128), rims, rims]
        + [pltpu.VMEM(s, jnp.float32) for s in (field, field, field, row_shape, phase_shape)]
        + [pltpu.VMEM(forward.shape, forward.dtype)],
        [
            columns_lhs,
            pltpu.VMEM((z.first, WIDE), jnp.float32),
            pltpu.SemaphoreType.DMA((12,)),
        ],
        1,
        {n: pltpu.HBM for n in range(6)},
    )(*pinned)
    second = round_up(z.own - z.first, 8)
    (share_second,) = call(
        functools.partial(east_shares_of, z, slice(z.first, z.own)),
        6,
        [(packed_rows(second), 128)],
        [columns_lhs, pltpu.VMEM((second, WIDE), jnp.float32)],
        0.18,
    )(wind_east, wind_north, geopot, per_row, phase, forward)
    east_firsts, east_seconds = (
        [x] + [shifted(x, "lon", s) for s in range(1, z.n_lon)] for x in (share_first, share_second)
    )
    met = []
    for start, rim in enumerate((to_even, to_odd)):
        pairs = [(i, i + 1) for i in range(start, z.n_lat - 1, 2)]
        met.append(lax.ppermute(rim, "lat", pairs + [(b, a) for a, b in pairs]))

    places = round_up(z.rows, 128)
    north_ahead, north_rest, north_new, chosen, kept_sorted = call(
        functools.partial(north_forward, z),
        10,
        [
            (packed_rows(z.ahead), 128),
            (packed_rows(z.rows - z.ahead), 128),
            (z.rows, z.lon),
            (z.rows, places),
            (z.rows, 128),
        ],
        [
            pltpu.VMEM((z.rows, z.lon), jnp.float32),
            columns_lhs,
            pltpu.VMEM((z.rows, WIDE), jnp.float32),
        ],
        0.8,
    )(
        wind_east, wind_north, geopot, *met, per_row, phase, forward, kept, slots
    )
    north_rests = [north_rest] + [shifted(north_rest, "lon", s) for s in range(1, z.n_lon)]
    polar_bands = [i for i in range(z.n_lat) if i < z.n_lat // 4 or i >= z.n_lat - z.n_lat // 4]
    north_aheads = [north_ahead]
    for distance in range(1, z.n_lon):
        route = [
            (band * z.n_lon + lon, band * z.n_lon + (lon + distance) % z.n_lon)
            for band in polar_bands
            for lon in range(z.n_lon)
        ]
        north_aheads.append(lax.ppermute(north_ahead, ("lat", "lon"), route))

    (first_here,) = call(arrival, 1, [(8, 128)], [], 0.95)(east_firsts[1])
    east_final, thick_part, east_keep, east_send = call(
        functools.partial(east_inverse, z),
        11 + 2 * z.n_lon,
        [field, (z.own, z.lon), spec, spec],
        [
            waves_lhs,
            pltpu.VMEM((z.own, z.ext), jnp.float32),
            pltpu.VMEM((z.own, WIDE), jnp.float32),
        ],
        1,
        {0: pltpu.SMEM},
    )(
        mean_depth, wind_east, wind_north, geopot, thickness, per_row, phase, kept, chosen,
        first_here, *east_firsts, *east_seconds, inverse,
    )

    to_helper, waves_ahead = call(
        functools.partial(send_spectra, z), 2 + z.n_lon, [(2, *spec), (z.ahead, WIDE)], [], 0.1
    )(east_send, kept_sorted, *north_aheads)
    arrived = lax.ppermute(
        to_helper, "lat", [(i, (i + z.half_axis) % z.n_lat) for i in polar_bands]
    )

    ahead_rows = jax.ShapeDtypeStruct((z.ahead, z.ext), jnp.bfloat16)
    ahead_high, ahead_low = call(
        functools.partial(ahead_inverse, z),
        3,
        [ahead_rows] * 2,
        [waves_lhs, pltpu.VMEM((z.ahead, z.ext), jnp.float32)],
        0.5,
    )(phase, waves_ahead, inverse)

    operands = (
        mean_depth, north_new, thick_part, per_row, phase, chosen, kept_sorted, waves_ahead,
        ahead_high, ahead_low, *north_rests, inverse,
    )
    in_vmem = pltpu.VMEM(field, jnp.float32)
    scratch = [waves_lhs, pltpu.VMEM((z.rows, z.ext), jnp.float32)]
    scratch += [pltpu.VMEM((z.mm_rows, z.ext), jnp.bfloat16)] * 2
    final_deeper, thick_deeper, column, north_keep = call(
        functools.partial(north_deeper, z),
        len(operands),
        [in_vmem, in_vmem, (z.lat, z.lon), spec],
        scratch,
        2,
        {0: pltpu.SMEM},
    )(*operands)
    deeper = [
        lax.ppermute(column, "lev", [(i, i - distance) for i in range(distance, z.n_lev)])
        for distance in range(1, z.n_lev)
    ]
    final_own, thick_own, spectra = call(
        functools.partial(north_shallowest, z),
        3 + len(operands),
        [in_vmem, in_vmem, (2, *spec)],
        [pltpu.VMEM((z.lat, z.lon), jnp.float32), pltpu.VMEM(spec, jnp.float32)] + scratch,
        3.2,
        {3: pltpu.SMEM},
    )(east_keep, north_keep, arrived, *operands)
    north_final, thick_new, geo_new = call(
        functools.partial(finish, z),
        5 + len(deeper),
        [pltpu.HBM(field, jnp.float32)] * 3,
        [pltpu.VMEM(field, jnp.float32), pltpu.SemaphoreType.DMA((2 + z.cuts,))],
        1,
        in_hbm=3,
    )(surface_geopot, final_deeper, thick_deeper, final_own, thick_own, *deeper)
    return tuple(level_inside(x) for x in (east_final, north_final, thick_new, geo_new, spectra))


def solution(mesh):
    field = P(("members", "lev"), "lat", "lon")
    return jax.shard_map(
        local,
        mesh=mesh,
        in_specs=(field, field, field, field, P("lat", "lon"), P("lev"), P(), P()),
        out_specs=(field, field, field, field, P(None, ("members", "lev"), "lat", "lon")),
        check_vma=False,
    )
```

```python
import functools
import math

import jax
import jax.numpy as jnp
import numpy as np
from jax import lax
from jax.experimental import pallas as pl
from jax.experimental.pallas import tpu as pltpu
from jax.sharding import PartitionSpec as P

KMAX = 360
HALF = 384
WIDE = 2 * HALF
SPARE = HALF - 128
MORE = KMAX - SPARE
MOVED = 128 - MORE
LEFT = MORE - MOVED
BLOCK = 256
INVERSE_BLOCK = 768

STEP_FACTOR = 0.15
CORIOLIS = 0.2
GRAVITY = 0.25

MIB = 1024 * 1024

EAST_COEF, SINE, COSINE, NORTH_COEF, LEVEL, POLAR, NUMBER, OWN = range(8)


def round_up(value, step):
    return -(-value // step) * step


class Sizes:
    def __init__(self, shape, counts):
        self.lev, self.lat, self.lon = shape
        self.n_lat, self.n_lon, self.n_lev = counts["lat"], counts["lon"], counts["lev"]
        self.nlat, self.nlon = self.lat * self.n_lat, self.lon * self.n_lon
        self.polar = self.nlat // 4
        self.help = self.lat // 2
        self.half_axis = self.n_lat // 2
        self.own = self.lat * self.lev
        self.rows = self.own + 2 * self.lev
        assert self.rows % 8 == 0
        self.mm_rows = round_up(self.rows, 16)
        self.ext = round_up(self.lon + 4, BLOCK)
        self.blocks = self.ext // BLOCK
        self.inverse_block = min(INVERSE_BLOCK, self.ext)
        assert self.ext % self.inverse_block == 0
        self.spec_width = 2 * KMAX // self.n_lon
        self.helped = self.help * self.lev
        self.ahead = round_up(self.helped, 16)
        self.cuts = 2
        self.first = min(round_up(self.own * 4 // 9, 8 * self.lev), self.own)


def high_low(x):
    x = x.astype(np.float32)
    high = x.astype(jnp.bfloat16)
    return high, (x - high.astype(np.float32)).astype(jnp.bfloat16)


def basis_tables(z):
    k = np.arange(KMAX)
    angle = (np.arange(z.inverse_block)[:, None] * k[None, :] % z.nlon) * (2.0 * np.pi / z.nlon)
    full = np.zeros((z.inverse_block, WIDE))
    full[:, :KMAX] = np.cos(angle)
    full[:, HALF : HALF + KMAX] = np.sin(angle)
    high, low = high_low(full)
    forward = np.concatenate([high[:BLOCK], high[:BLOCK], low[:BLOCK]], axis=0)
    inverse = np.concatenate([high.T, high.T, low.T], axis=0)
    return forward, inverse


def phase_table(z):
    k = np.arange(KMAX)
    table = np.zeros((z.n_lon, round_up(2 * z.blocks + 2, 8), HALF), np.float32)
    for place in range(z.n_lon):
        for n, column in enumerate([*range(0, z.ext, BLOCK), -1]):
            angle = ((place * z.lon + column) * k % z.nlon) * (2.0 * np.pi / z.nlon)
            table[place, 2 * n, :KMAX] = np.cos(angle)
            table[place, 2 * n + 1, :KMAX] = np.sin(angle)
    return table


def row_table(z):
    lam_step = np.float32(2.0 * math.pi / z.nlon)
    phi_step = np.float32(math.pi / z.nlat)
    latitude = np.float32(-0.5 * math.pi) + (
        np.arange(z.nlat, dtype=np.float32) + np.float32(0.5)
    ) * phi_step
    cosine = np.cos(latitude.astype(np.float64)).astype(np.float32)
    sine = np.sin(latitude.astype(np.float64)).astype(np.float32)
    north_coef = np.float32(STEP_FACTOR) * lam_step / phi_step
    table = np.zeros((z.n_lat, z.rows, 8), np.float32)
    for place in range(z.n_lat):
        for flat in range(z.rows):
            inner, level = flat // z.lev, flat % z.lev
            inner = -1 if inner == z.lat + 1 else inner
            row = place * z.lat + inner
            one = table[place, flat]
            one[LEVEL], one[NUMBER] = level, -1
            one[OWN] = 0 <= inner < z.lat
            if 0 <= row < z.nlat:
                one[EAST_COEF] = np.float32(STEP_FACTOR) / cosine[row]
                one[SINE], one[COSINE] = sine[row], cosine[row]
                one[NORTH_COEF] = north_coef / cosine[row]
                if row < z.polar:
                    one[POLAR], one[NUMBER] = 1, row
                elif row >= z.nlat - z.polar:
                    one[POLAR], one[NUMBER] = 1, row - (z.nlat - 2 * z.polar)
    return table


def on_polar_band(z):
    lat_index = lax.axis_index("lat")
    return (lat_index < z.n_lat // 4) | (lat_index >= z.n_lat - z.n_lat // 4)


def split(x):
    high = x.astype(jnp.bfloat16)
    return high, (x - high.astype(jnp.float32)).astype(jnp.bfloat16)


def store_split(lhs_ref, first_row, x):
    rows, width = x.shape
    high, low = split(x)
    at = slice(first_row, first_row + rows)
    lhs_ref[at, :width] = high
    lhs_ref[at, width : 2 * width] = low
    lhs_ref[at, 2 * width :] = high


def pad_rows(x, rows):
    if x.shape[0] == rows:
        return x
    return jnp.concatenate([x, jnp.zeros((rows - x.shape[0], x.shape[1]), x.dtype)], axis=0)


def phase_of(phase_ref, n):
    return phase_ref[2 * n : 2 * n + 1], phase_ref[2 * n + 1 : 2 * n + 2]


def packed_rows(rows):
    return 5 * rows + round_up(-(-rows // 2), 8) + 16


def lanes_of(x):
    return lax.broadcasted_iota(jnp.int32, x.shape, 1)


def pack(x, out_ref):
    rows = x.shape[0]
    half = round_up(-(-rows // 2), 8)
    tiles = [x[:, n : n + 128] for n in range(0, WIDE, 128)]
    left = tiles[5]
    lane = lanes_of(left)
    tiles[2] = jnp.where(lane < MORE, tiles[2], roll(left, MOVED, 1))
    for n in range(5):
        out_ref[n * rows : (n + 1) * rows] = tiles[n]
    lower = pad_rows(left[half:], half)
    out_ref[5 * rows : 5 * rows + half] = jnp.where(lane[:half] < 64, left[:half], roll(lower, 64, 1))
    out_ref[5 * rows + half :] = pad_rows(roll(left, -64, 1), 128).T[:16]


def unpack(x, rows):
    half = round_up(-(-rows // 2), 8)
    tiles = [x[n * rows : (n + 1) * rows] for n in range(5)]
    pairs = x[5 * rows : 5 * rows + half]
    ends = pad_rows(x[5 * rows + half :], 128).T[:rows]
    left = jnp.concatenate([pairs, roll(pairs, 64, 1)[: rows - half]], axis=0)
    lane = lanes_of(left)
    left = jnp.where(lane < 64, left, jnp.where(lane < LEFT, roll(ends, 64, 1), roll(tiles[2], -MOVED, 1)))
    return jnp.concatenate([*tiles, left], axis=1)


def forward_sums(
    z, x, basis_ref, phase_ref, lhs_ref, out_ref, at=slice(None), basis_here=None
):
    count = round_up(x.shape[0], 16)
    for block in range(z.blocks):
        part = pad_rows(x[:, block * BLOCK : (block + 1) * BLOCK], count)
        store_split(lhs_ref, block * count, part)
    lhs = lhs_ref[: z.blocks * count]
    if basis_here is not None:
        basis_here()
    sums = jnp.dot(lhs, basis_ref[...], preferred_element_type=jnp.float32)
    real = imag = None
    for block in range(z.blocks):
        cos, sin = phase_of(phase_ref, block)
        part = sums[block * count : block * count + x.shape[0]]
        a, b = part[:, :HALF], part[:, HALF:]
        more_real, more_imag = a * cos - b * sin, a * sin + b * cos
        real = more_real if real is None else real + more_real
        imag = more_imag if imag is None else imag + more_imag
    out_ref[at, :HALF] = real
    out_ref[at, HALF:] = imag


def inverse_rows(z, coef, basis_ref, phase_ref, lhs_ref, out_ref, at=slice(None)):
    a, b = coef[:, :HALF], coef[:, HALF:]
    count, width = round_up(coef.shape[0], 16), z.inverse_block
    blocks = range(z.ext // width)
    for block in blocks:
        cos, sin = phase_of(phase_ref, block * width // BLOCK)
        turned = jnp.concatenate([a * cos + b * sin, b * cos - a * sin], axis=1)
        store_split(lhs_ref, block * count, pad_rows(turned, count))
    lhs = lhs_ref[: len(blocks) * count]
    rows = jnp.dot(lhs, basis_ref[...], preferred_element_type=jnp.float32)
    for block in blocks:
        out_ref[at, block * width : (block + 1) * width] = rows[
            block * count : block * count + coef.shape[0]
        ]


def roll(x, shift, axis):
    return pltpu.roll(x, shift % x.shape[axis], axis)


def east_diff(x):
    return roll(x, -1, 1) - roll(x, 1, 1)


def flat_rows(z, ref):
    return ref[...].reshape(z.own, ref.shape[2])


def widen(z, x):
    return jnp.concatenate([x, jnp.zeros((x.shape[0], z.ext - x.shape[1]), x.dtype)], axis=1)


def put_lane(x, at, column):
    lane = lax.broadcasted_iota(jnp.int32, x.shape, 1)
    return jnp.where(lane == at, column, x)


def column_of(row_ref, which):
    return row_ref[:, which : which + 1]


def north_factor(z):
    return STEP_FACTOR * (2.0 * math.pi / z.nlon) / (math.pi / z.nlat)


def look_up(number, table_ref):
    table = table_ref[...].astype(jnp.float32)
    lane = lax.broadcasted_iota(jnp.int32, (number.shape[0], table.shape[1]), 1)
    return jnp.sum(jnp.where(lane == number, table, 0.0), axis=1, keepdims=True)


def coefficients(z, sums, kept):
    lane = lax.broadcasted_iota(jnp.int32, (1, WIDE), 1)
    k = jnp.where(lane < HALF, lane, lane - HALF)
    weight = jnp.where(k == 0, 1.0 / z.nlon, 2.0 / z.nlon).astype(jnp.float32)
    keep = (k.astype(jnp.float32) < kept) & (k < KMAX)
    return jnp.where(keep, sums * weight, 0.0)


def slot_order(z, number, row_ref, slot_ref):
    lat_index = lax.axis_index("lat")
    slot = look_up(number, slot_ref).astype(jnp.int32)
    theirs = slot - lax.rem(lat_index + z.half_axis, z.n_lat) * z.help
    mine = slot - lat_index * z.help
    level = column_of(row_ref, LEVEL).astype(jnp.int32)
    flat = lax.broadcasted_iota(jnp.int32, slot.shape, 0)
    place = jnp.where((mine >= 0) & (mine < z.help), z.helped + mine * z.lev + level, -1)
    place = jnp.where((theirs >= 0) & (theirs < z.help), theirs * z.lev + level, place)
    place = jnp.where(number >= 0, place, -1)
    place = jnp.where(flat < z.own, place, flat)
    lane = lax.broadcasted_iota(jnp.int32, (z.rows, round_up(z.rows, 128)), 1)
    return (lane == place).astype(jnp.float32)


def reorder(chosen, values):
    high, low = (
        lax.dot_general(
            chosen.astype(jnp.bfloat16),
            part,
            (((0,), (0,)), ((), ())),
            preferred_element_type=jnp.float32,
        )
        for part in split(values)
    )
    return high + low


def sector_part(z, coef, place):
    part = None
    for one in range(z.n_lon):
        first = one * z.spec_width
        first = first if first < KMAX else first - KMAX + HALF
        this = coef[:, first : first + z.spec_width]
        part = this if part is None else jnp.where(place == one, this, part)
    return part


def depths(z, depth_ref, row_ref):
    level = column_of(row_ref, LEVEL)[: z.own]
    depth = jnp.zeros_like(level)
    for lev in range(z.lev):
        depth = jnp.where(level == lev, depth_ref[lev], depth)
    return depth


def store_rims(z, ref, g, we, wn, last):
    edge = 2 * z.lev
    ref[:edge] = g[z.own - edge :] if last else g[:edge]
    ref[edge : edge + z.lev] = we[z.own - z.lev :] if last else we[: z.lev]
    ref[edge + z.lev :] = wn[z.own - z.lev :] if last else wn[: z.lev]


def east_shares_of(
    z, at, we_ref, wn_ref, g_ref, row_ref, phase_ref, basis_ref, out_ref, lhs_ref, share_ref,
    basis_here=None,
):
    inner, rows = slice(at.start // z.lev, at.stop // z.lev), at.stop - at.start
    g, we, wn = (ref[inner].reshape(rows, z.lon) for ref in (g_ref, we_ref, wn_ref))

    @pl.when(on_polar_band(z))
    def _():
        coef, sine = column_of(row_ref, EAST_COEF)[at], column_of(row_ref, SINE)[at]
        new = widen(z, we + CORIOLIS * sine * wn) - coef * east_diff(widen(z, g))
        tail = put_lane(new[:, z.ext - 128 :], 127, 0.0)
        new = jnp.concatenate([new[:, : z.ext - 128], tail], axis=1)
        forward_sums(
            z, new, basis_ref, phase_ref, lhs_ref, share_ref, slice(rows), basis_here=basis_here
        )
        cos, sin = phase_of(phase_ref, z.blocks)
        before = -coef * g[:, 0:1]
        share_ref[:rows, :HALF] += before * cos
        share_ref[:rows, HALF:] += before * sin
        pack(share_ref[...], out_ref)

    @pl.when(jnp.logical_not(on_polar_band(z)))
    def _():
        if basis_here is not None:
            basis_here()
        last = z.lon - 1
        columns = jnp.zeros((rows, 128), jnp.float32)
        edges = ((g, last - 1), (g, last), (we, last), (wn, last), (g, 0), (g, 1), (we, 0), (wn, 0))
        for n, (x, column) in enumerate(edges):
            columns = put_lane(columns, n, x[:, column : column + 1])
        out_ref[...] = jnp.zeros_like(out_ref)
        out_ref[:rows] = columns


def east_first(
    z, we_hbm, wn_hbm, g_hbm, row_hbm, phase_hbm, basis_hbm,
    share_ref, even_ref, odd_ref, we_ref, wn_ref, g_ref, row_ref, phase_ref, basis_ref, lhs_ref, sums_ref, sems,
):
    fields = ((g_hbm, g_ref), (we_hbm, we_ref), (wn_hbm, wn_ref))
    cut, rim = z.first // z.lev, z.lat - 2

    def copies(first_sem, pairs):
        return [pltpu.make_async_copy(*pair, sems.at[first_sem + n]) for n, pair in enumerate(pairs)]

    tables = copies(
        0,
        (
            (row_hbm.at[lax.axis_index("lat")], row_ref),
            (phase_hbm.at[lax.axis_index("lon")], phase_ref),
        ),
    )
    first = copies(2, [(a.at[:cut], b.at[:cut]) for a, b in fields])
    basis = copies(5, [(basis_hbm, basis_ref)])
    edge = copies(6, [(a.at[rim:], b.at[rim:]) for a, b in fields])
    between = copies(9, [(a.at[cut:rim], b.at[cut:rim]) for a, b in fields])
    for copy in first + tables + basis + edge:
        copy.start()
    for copy in first + tables:
        copy.wait()
    for copy in between:
        copy.start()

    def basis_here():
        for copy in basis + edge:
            copy.wait()

    east_shares_of(
        z, slice(0, z.first), we_ref, wn_ref, g_ref, row_ref, phase_ref, basis_ref, share_ref, lhs_ref,
        sums_ref, basis_here,
    )
    odd = lax.rem(lax.axis_index("lat"), 2) == 1
    last, flat = z.lat - 1, (z.lev, z.lon)
    far = (g_ref[last - 1], g_ref[last], we_ref[last], wn_ref[last])
    near = (g_ref[0], g_ref[1], we_ref[0], wn_ref[0])
    for n, (bottom, top) in enumerate(zip(far, near, strict=True)):
        at = slice(n * z.lev, (n + 1) * z.lev)
        even_ref[at] = jnp.where(odd, top, bottom).reshape(flat)
        odd_ref[at] = jnp.where(odd, bottom, top).reshape(flat)
    for copy in between:
        copy.wait()


def north_forward(
    z, we_ref, wn_ref, g_ref, even_ref, odd_ref, row_ref, phase_ref, basis_ref, kept_ref, slot_ref, *rest
):
    ahead_ref, rest_ref, north_ref, chosen_ref, sorted_ref, g_rows, lhs_ref, share_ref = rest
    edge, lev = 2 * z.lev, z.lev
    odd = lax.rem(lax.axis_index("lat"), 2) == 1
    below = jnp.where(odd, odd_ref[...], even_ref[...])
    above = jnp.where(odd, even_ref[...], odd_ref[...])
    coef, sine = north_factor(z), CORIOLIS * column_of(row_ref, SINE)
    own = flat_rows(z, g_ref)
    g_rows[: z.own] = own
    g_rows[z.own : z.own + lev] = below[:lev]
    g_rows[z.own + lev :] = above[lev:edge]
    g = g_rows[...]
    diff = (roll(g, -lev, 0) - roll(g, lev, 0))[: z.own]
    north_ref[: z.own] = flat_rows(z, wn_ref) - coef * diff - sine[: z.own] * flat_rows(z, we_ref)
    for at, diff, rim in (
        (z.own, below[lev:edge] - own[z.own - lev :], below),
        (z.own + lev, own[:lev] - above[:lev], above),
    ):
        we, wn = rim[edge : edge + lev], rim[edge + lev :]
        north_ref[at : at + lev] = wn - coef * diff - sine[at : at + lev] * we
    number = column_of(row_ref, NUMBER).astype(jnp.int32)
    kept = look_up(number, kept_ref)

    @pl.when(on_polar_band(z))
    def _():
        forward_sums(z, widen(z, north_ref[...]), basis_ref, phase_ref, lhs_ref, share_ref)
        share_ref[:, SPARE:HALF] = put_lane(share_ref[:, SPARE:HALF], KMAX - SPARE, kept)
        chosen = slot_order(z, number, row_ref, slot_ref)
        ordered = reorder(chosen, share_ref[...])
        pack(ordered[: z.ahead], ahead_ref)
        pack(ordered[z.ahead : z.rows], rest_ref)
        sorted_ref[...] = ordered[: z.rows, SPARE:HALF]
        chosen_ref[...] = chosen

    @pl.when(jnp.logical_not(on_polar_band(z)))
    def _():
        ahead_ref[...] = jnp.zeros_like(ahead_ref)
        chosen_ref[...] = jnp.zeros_like(chosen_ref)
        share_ref[...] = jnp.zeros_like(share_ref)
        rows = widen(z, north_ref[z.own :])
        forward_sums(z, rows, basis_ref, phase_ref, lhs_ref, share_ref, slice(z.own, z.rows))
        pack(share_ref[z.ahead :], rest_ref)
        sorted_ref[...] = jnp.broadcast_to(kept, sorted_ref.shape)


def arrival(arrived_ref, out_ref):
    out_ref[...] = arrived_ref[:8, :128]


def east_inverse(
    z, depth_ref, we_ref, wn_ref, g_ref, thick_ref, row_ref, phase_ref, kept_ref, chosen_ref, first_here,
    *rest,
):
    del first_here
    firsts, seconds, rest = rest[: z.n_lon], rest[z.n_lon : 2 * z.n_lon], rest[2 * z.n_lon :]
    basis_ref, final_ref, part_ref, keep_ref, send_ref, lhs_ref, rows_ref, sums_ref = rest
    coef, sine = column_of(row_ref, EAST_COEF)[: z.own], column_of(row_ref, SINE)[: z.own]

    @pl.when(on_polar_band(z))
    def _():
        number = column_of(row_ref, NUMBER)[: z.own].astype(jnp.int32)
        second = round_up(z.own - z.first, 8)
        sums_ref[: z.first] = unpack(sum(ref[...] for ref in firsts), z.first)
        sums_ref[z.first :] = unpack(sum(ref[...] for ref in seconds), second)[: z.own - z.first]
        waves = coefficients(z, sums_ref[...], look_up(number, kept_ref))
        part = sector_part(z, waves, lax.axis_index("lon"))
        ordered = reorder(chosen_ref[: z.own], part)
        send_ref[...] = ordered[: z.helped].reshape(send_ref.shape)
        keep_ref[...] = ordered[z.helped : 2 * z.helped].reshape(keep_ref.shape)
        inverse_rows(z, waves, basis_ref, phase_ref, lhs_ref, rows_ref)
        cos, sin = phase_of(phase_ref, z.blocks)
        before = jnp.sum(waves[:, :HALF] * cos + waves[:, HALF:] * sin, axis=1, keepdims=True)
        rows_ref[:, z.ext - 128 :] = put_lane(rows_ref[:, z.ext - 128 :], 127, before)

    @pl.when(jnp.logical_not(on_polar_band(z)))
    def _():
        send_ref[...] = jnp.zeros_like(send_ref)
        keep_ref[...] = jnp.zeros_like(keep_ref)
        left, right = (
            jnp.concatenate([firsts[n][: z.first], seconds[n][: z.own - z.first]], axis=0)
            for n in (1, -1)
        )
        at_right = z.lon - (z.ext - 128)

        def rimmed(ref, left_of, right_of):
            x = widen(z, flat_rows(z, ref))
            tail = x[:, z.ext - 128 :]
            for n, lane in enumerate(right_of):
                tail = put_lane(tail, at_right + n, right[:, lane : lane + 1])
            for n, lane in enumerate(left_of):
                tail = put_lane(tail, 127 - n, left[:, lane : lane + 1])
            return jnp.concatenate([x[:, : z.ext - 128], tail], axis=1)

        g = rimmed(g_ref, (1, 0), (4, 5))
        we, wn = rimmed(we_ref, (2,), (6,)), rimmed(wn_ref, (3,), (7,))
        rows_ref[...] = we - coef * east_diff(g) + CORIOLIS * sine * wn

    final = rows_ref[...]
    final_ref[...] = final[:, : z.lon].reshape(final_ref.shape)
    change = depths(z, depth_ref, row_ref) * coef * east_diff(final)[:, : z.lon]
    part_ref[...] = flat_rows(z, thick_ref) - change


def ahead_waves(z, shares, sorted_ref):
    sums = unpack(sum(ref[...] for ref in shares), z.ahead)
    return coefficients(z, sums, sorted_ref[: z.ahead, MORE : MORE + 1])


def send_spectra(z, east_ref, sorted_ref, *rest):
    shares, send_ref, waves_ref = rest[:-2], rest[-2], rest[-1]
    waves = ahead_waves(z, shares, sorted_ref)
    waves_ref[...] = waves
    part = sector_part(z, waves, lax.axis_index("lon"))
    send_ref[0] = east_ref[...]
    send_ref[1] = part[: z.helped].reshape(east_ref.shape)


def ahead_inverse(z, phase_ref, waves_ref, basis_ref, high_ref, low_ref, lhs_ref, rows_ref):
    @pl.when(on_polar_band(z))
    def _():
        inverse_rows(z, waves_ref[...], basis_ref, phase_ref, lhs_ref, rows_ref)
        high_ref[...], low_ref[...] = split(rows_ref[...])


def north_inverse(
    z, active, depth_ref, north_ref, part_ref, row_ref, phase_ref, chosen_ref, sorted_ref, waves_ahead,
    high_ahead, low_ahead, *rest,
):
    shares, rest = rest[: z.n_lon], rest[z.n_lon :]
    basis_ref, final_ref, thick_ref, column_ref, keep_ref, lhs_ref, rows_ref, high_ref, low_ref = rest

    @pl.when(active & on_polar_band(z))
    def _():
        more = z.ahead - 8
        sums = unpack(sum(ref[...] for ref in shares), z.rows - z.ahead)
        waves = coefficients(z, sums, sorted_ref[z.ahead :, MORE : MORE + 1])
        both = jnp.concatenate([waves_ahead[more:], waves], axis=0)
        part = sector_part(z, both, lax.axis_index("lon"))
        first = z.helped - more
        keep_ref[...] = part[first : first + z.helped].reshape(keep_ref.shape)
        inverse_rows(z, waves, basis_ref, phase_ref, lhs_ref, rows_ref, slice(z.rows - z.ahead))
        count = high_ref.shape[0] - z.ahead
        rest_high, rest_low = split(pad_rows(rows_ref[: z.rows - z.ahead], count))
        high_ref[: z.ahead], low_ref[: z.ahead] = high_ahead[...], low_ahead[...]
        high_ref[z.ahead :], low_ref[z.ahead :] = rest_high, rest_low
        chosen = chosen_ref[:, : z.mm_rows].astype(jnp.bfloat16)
        rows_ref[...] = jnp.dot(
            chosen, high_ref[...], preferred_element_type=jnp.float32
        ) + jnp.dot(chosen, low_ref[...], preferred_element_type=jnp.float32)
        beyond = slice(z.own, z.rows)
        polar = column_of(row_ref, POLAR)[beyond] > 0.0
        rows_ref[beyond, : z.lon] = jnp.where(polar, rows_ref[beyond, : z.lon], north_ref[beyond])

    @pl.when(active & jnp.logical_not(on_polar_band(z)))
    def _():
        keep_ref[...] = jnp.zeros_like(keep_ref)
        beyond = slice(z.own, z.rows)
        at = slice(z.own - z.ahead, z.rows - z.ahead)
        sums = unpack(sum(ref[...] for ref in shares), z.rows - z.ahead)
        waves = coefficients(z, sums[at], sorted_ref[beyond, MORE : MORE + 1])
        inverse_rows(z, waves, basis_ref, phase_ref, lhs_ref, rows_ref, beyond)
        polar = column_of(row_ref, POLAR)[beyond] > 0.0
        rows_ref[beyond, : z.lon] = jnp.where(polar, rows_ref[beyond, : z.lon], north_ref[beyond])
        rows_ref[: z.own, : z.lon] = north_ref[: z.own]

    @pl.when(active)
    def _():
        final = rows_ref[:, : z.lon]
        final_ref[...] = final[: z.own].reshape(final_ref.shape)
        scaled = final * column_of(row_ref, COSINE)
        diff = (roll(scaled, -z.lev, 0) - roll(scaled, z.lev, 0))[: z.own]
        scale = depths(z, depth_ref, row_ref) * column_of(row_ref, NORTH_COEF)[: z.own]
        thick_ref[...] = (part_ref[...] - scale * diff).reshape(thick_ref.shape)
        column_ref[...] = sum(thick_ref[:, lev, :] for lev in range(z.lev))


def sends_column():
    return lax.axis_index("lev") > 0


def north_deeper(z, *refs):
    north_inverse(z, sends_column(), *refs)


def north_shallowest(z, east_keep, north_keep, arrived_ref, *rest):
    *refs, spectra_ref, column_ref, keep_ref, lhs_ref, rows_ref, high_ref, low_ref = rest
    active = jnp.logical_not(sends_column())
    north_inverse(z, active, *refs, column_ref, keep_ref, lhs_ref, rows_ref, high_ref, low_ref)

    @pl.when(sends_column())
    def _():
        keep_ref[...] = north_keep[...]

    polar = on_polar_band(z)
    spectra_ref[0] = jnp.where(polar, east_keep[...], arrived_ref[0])
    spectra_ref[1] = jnp.where(polar, keep_ref[...], arrived_ref[1])


def finish(z, surface_ref, *rest):
    deeper_fields, own_fields, deeper, outs = rest[:2], rest[2:4], rest[4 : 3 + z.n_lev], rest[3 + z.n_lev :]
    spectra, (final_out, thick_out, geo_out, spectra_out, geo_ref, sems) = outs[0], outs[1:]

    def store(fields):
        copies = [
            pltpu.make_async_copy(*pair, sems.at[n])
            for n, pair in enumerate(
                ((fields[0], final_out), (fields[1], thick_out), (spectra, spectra_out))
            )
        ]
        for copy in copies:
            copy.start()
        for n in range(z.cuts):
            at = slice(n * z.lat // z.cuts, (n + 1) * z.lat // z.cuts)
            column = sum(ref[at] for ref in deeper)
            for lev in reversed(range(z.lev)):
                column = column + fields[1][at, lev, :]
                geo_ref[at, lev, :] = surface_ref[at] + GRAVITY * column
            copies.append(pltpu.make_async_copy(geo_ref.at[at], geo_out.at[at], sems.at[3 + n]))
            copies[-1].start()
        for copy in copies:
            copy.wait()

    @pl.when(sends_column())
    def _():
        store(deeper_fields)

    @pl.when(jnp.logical_not(sends_column()))
    def _():
        store(own_fields)


def call(kernel, n_in, out_shape, scratch, micros, spaces=None, in_hbm=0, vmem=24):
    vmem_spec = pl.BlockSpec(memory_space=pltpu.VMEM)
    spaces = spaces or {}
    return pl.pallas_call(
        kernel,
        in_specs=[
            pl.BlockSpec(memory_space=spaces[n]) if n in spaces else vmem_spec for n in range(n_in)
        ],
        out_specs=[pl.BlockSpec(memory_space=pltpu.HBM)] * in_hbm
        + [vmem_spec] * (len(out_shape) - in_hbm),
        out_shape=[
            jax.ShapeDtypeStruct(s, jnp.float32) if isinstance(s, tuple) else s for s in out_shape
        ],
        scratch_shapes=scratch,
        compiler_params=pltpu.CompilerParams(vmem_limit_bytes=vmem * MIB),
        cost_estimate=pl.CostEstimate(
            flops=int(micros * 1.15e9), bytes_accessed=0, transcendentals=0
        ),
    )


def shifted(block, axis, distance):
    count = lax.axis_size(axis)
    return lax.ppermute(block, axis, [(i, (i + distance) % count) for i in range(count)])


def level_inside(x):
    return jnp.swapaxes(x, -3, -2)


def local(
    wind_east, wind_north, thickness, geopot, surface_geopot, mean_depth, kept_modes, slot_table
):
    z = Sizes(thickness.shape, {axis: lax.axis_size(axis) for axis in ("lat", "lon", "lev")})
    wind_east, wind_north, thickness, geopot = (
        level_inside(x) for x in (wind_east, wind_north, thickness, geopot)
    )
    field = (z.lat, z.lev, z.lon)
    forward, inverse = (jnp.asarray(x) for x in basis_tables(z))
    phase = jnp.asarray(phase_table(z))
    per_row = jnp.asarray(row_table(z))
    kept = kept_modes[None, :]
    slots = slot_table[None, :]
    payload = (z.rows, WIDE)
    rims = (4 * z.lev, z.lon)
    spec = (z.help, z.lev, z.spec_width)
    waves_lhs = pltpu.VMEM((z.ext // z.inverse_block * z.mm_rows, 3 * WIDE), jnp.bfloat16)

    row_shape, phase_shape = per_row.shape[1:], phase.shape[1:]
    pinned = [
        pltpu.with_memory_space_constraint(x, pltpu.HBM)
        for x in (wind_east, wind_north, geopot, per_row, phase, forward)
    ]
    columns_lhs = pltpu.VMEM((z.blocks * z.mm_rows, 3 * BLOCK), jnp.bfloat16)
    waves_lhs = pltpu.VMEM((z.ext // z.inverse_block * z.mm_rows, 3 * WIDE), jnp.bfloat16)

    share_first, to_even, to_odd, wind_east, wind_north, geopot, per_row, phase, forward = call(
        functools.partial(east_first, z),
        6,
        [(packed_rows(z.first), 128), rims, rims]
        + [pltpu.VMEM(s, jnp.float32) for s in (field, field, field, row_shape, phase_shape)]
        + [pltpu.VMEM(forward.shape, forward.dtype)],
        [
            columns_lhs,
            pltpu.VMEM((z.first, WIDE), jnp.float32),
            pltpu.SemaphoreType.DMA((12,)),
        ],
        1,
        {n: pltpu.HBM for n in range(6)},
    )(*pinned)
    second = round_up(z.own - z.first, 8)
    (share_second,) = call(
        functools.partial(east_shares_of, z, slice(z.first, z.own)),
        6,
        [(packed_rows(second), 128)],
        [columns_lhs, pltpu.VMEM((second, WIDE), jnp.float32)],
        0.18,
    )(wind_east, wind_north, geopot, per_row, phase, forward)
    east_firsts, east_seconds = (
        [x] + [shifted(x, "lon", s) for s in range(1, z.n_lon)] for x in (share_first, share_second)
    )
    met = []
    for start, rim in enumerate((to_even, to_odd)):
        pairs = [(i, i + 1) for i in range(start, z.n_lat - 1, 2)]
        met.append(lax.ppermute(rim, "lat", pairs + [(b, a) for a, b in pairs]))

    places = round_up(z.rows, 128)
    north_ahead, north_rest, north_new, chosen, kept_sorted = call(
        functools.partial(north_forward, z),
        10,
        [
            (packed_rows(z.ahead), 128),
            (packed_rows(z.rows - z.ahead), 128),
            (z.rows, z.lon),
            (z.rows, places),
            (z.rows, 128),
        ],
        [
            pltpu.VMEM((z.rows, z.lon), jnp.float32),
            columns_lhs,
            pltpu.VMEM((z.rows, WIDE), jnp.float32),
        ],
        0.8,
    )(
        wind_east, wind_north, geopot, *met, per_row, phase, forward, kept, slots
    )
    north_rests = [north_rest] + [shifted(north_rest, "lon", s) for s in range(1, z.n_lon)]
    polar_bands = [i for i in range(z.n_lat) if i < z.n_lat // 4 or i >= z.n_lat - z.n_lat // 4]
    north_aheads = [north_ahead]
    for distance in range(1, z.n_lon):
        route = [
            (band * z.n_lon + lon, band * z.n_lon + (lon + distance) % z.n_lon)
            for band in polar_bands
            for lon in range(z.n_lon)
        ]
        north_aheads.append(lax.ppermute(north_ahead, ("lat", "lon"), route))

    (first_here,) = call(arrival, 1, [(8, 128)], [], 0.95)(east_firsts[1])
    east_final, thick_part, east_keep, east_send = call(
        functools.partial(east_inverse, z),
        11 + 2 * z.n_lon,
        [field, (z.own, z.lon), spec, spec],
        [
            waves_lhs,
            pltpu.VMEM((z.own, z.ext), jnp.float32),
            pltpu.VMEM((z.own, WIDE), jnp.float32),
        ],
        1,
        {0: pltpu.SMEM},
    )(
        mean_depth, wind_east, wind_north, geopot, thickness, per_row, phase, kept, chosen,
        first_here, *east_firsts, *east_seconds, inverse,
    )

    to_helper, waves_ahead = call(
        functools.partial(send_spectra, z), 2 + z.n_lon, [(2, *spec), (z.ahead, WIDE)], [], 0.1
    )(east_send, kept_sorted, *north_aheads)
    arrived = lax.ppermute(
        to_helper, "lat", [(i, (i + z.half_axis) % z.n_lat) for i in polar_bands]
    )

    ahead_rows = jax.ShapeDtypeStruct((z.ahead, z.ext), jnp.bfloat16)
    ahead_high, ahead_low = call(
        functools.partial(ahead_inverse, z),
        3,
        [ahead_rows] * 2,
        [waves_lhs, pltpu.VMEM((z.ahead, z.ext), jnp.float32)],
        0.5,
    )(phase, waves_ahead, inverse)

    operands = (
        mean_depth, north_new, thick_part, per_row, phase, chosen, kept_sorted, waves_ahead,
        ahead_high, ahead_low, *north_rests, inverse,
    )
    in_vmem = pltpu.VMEM(field, jnp.float32)
    scratch = [waves_lhs, pltpu.VMEM((z.rows, z.ext), jnp.float32)]
    scratch += [pltpu.VMEM((z.mm_rows, z.ext), jnp.bfloat16)] * 2
    final_deeper, thick_deeper, column, north_keep = call(
        functools.partial(north_deeper, z),
        len(operands),
        [in_vmem, in_vmem, (z.lat, z.lon), spec],
        scratch,
        2,
        {0: pltpu.SMEM},
    )(*operands)
    deeper = [
        lax.ppermute(column, "lev", [(i, i - distance) for i in range(distance, z.n_lev)])
        for distance in range(1, z.n_lev)
    ]
    final_own, thick_own, joined = call(
        functools.partial(north_shallowest, z),
        3 + len(operands),
        [in_vmem, in_vmem, pltpu.VMEM((2, *spec), jnp.float32)],
        [pltpu.VMEM((z.lat, z.lon), jnp.float32), pltpu.VMEM(spec, jnp.float32)] + scratch,
        3.2,
        {3: pltpu.SMEM},
    )(east_keep, north_keep, arrived, *operands)
    north_final, thick_new, geo_new, spectra = call(
        functools.partial(finish, z),
        6 + len(deeper),
        [pltpu.HBM(field, jnp.float32)] * 3 + [pltpu.HBM((2, *spec), jnp.float32)],
        [pltpu.VMEM(field, jnp.float32), pltpu.SemaphoreType.DMA((3 + z.cuts,))],
        1,
        in_hbm=4,
    )(surface_geopot, final_deeper, thick_deeper, final_own, thick_own, *deeper, joined)
    return tuple(level_inside(x) for x in (east_final, north_final, thick_new, geo_new, spectra))


def solution(mesh):
    field = P(("members", "lev"), "lat", "lon")
    return jax.shard_map(
        local,
        mesh=mesh,
        in_specs=(field, field, field, field, P("lat", "lon"), P("lev"), P(), P()),
        out_specs=(field, field, field, field, P(None, ("members", "lev"), "lat", "lon")),
        check_vma=False,
    )
```

```python
import functools
import math

import jax
import jax.numpy as jnp
import numpy as np
from jax import lax
from jax.experimental import pallas as pl
from jax.experimental.pallas import tpu as pltpu
from jax.sharding import PartitionSpec as P

KMAX = 360
HALF = 384
WIDE = 2 * HALF
SPARE = HALF - 128
MORE = KMAX - SPARE
MOVED = 128 - MORE
LEFT = MORE - MOVED
BLOCK = 256
INVERSE_BLOCK = 512

STEP_FACTOR = 0.15
CORIOLIS = 0.2
GRAVITY = 0.25

MIB = 1024 * 1024

EAST_COEF, SINE, COSINE, NORTH_COEF, LEVEL, POLAR, NUMBER, OWN = range(8)


def round_up(value, step):
    return -(-value // step) * step


class Sizes:
    def __init__(self, shape, counts):
        self.lev, self.lat, self.lon = shape
        self.n_lat, self.n_lon, self.n_lev = counts["lat"], counts["lon"], counts["lev"]
        self.nlat, self.nlon = self.lat * self.n_lat, self.lon * self.n_lon
        self.polar = self.nlat // 4
        self.help = self.lat // 2
        self.half_axis = self.n_lat // 2
        self.own = self.lat * self.lev
        self.rows = self.own + 2 * self.lev
        assert self.rows % 8 == 0
        self.mm_rows = round_up(self.rows, 16)
        self.ext = round_up(self.lon + 4, BLOCK)
        self.blocks = self.ext // BLOCK
        self.inverse_block = min(INVERSE_BLOCK, self.ext)
        assert self.ext % self.inverse_block == 0
        self.spec_width = 2 * KMAX // self.n_lon
        self.helped = self.help * self.lev
        self.ahead = round_up(self.helped, 16)
        self.cuts = 2
        self.first = min(round_up(self.own * 4 // 9, 8 * self.lev), self.own)


def high_low(x):
    x = x.astype(np.float32)
    high = x.astype(jnp.bfloat16)
    return high, (x - high.astype(np.float32)).astype(jnp.bfloat16)


def basis_tables(z):
    k = np.arange(KMAX)
    angle = (np.arange(z.inverse_block)[:, None] * k[None, :] % z.nlon) * (2.0 * np.pi / z.nlon)
    full = np.zeros((z.inverse_block, WIDE))
    full[:, :KMAX] = np.cos(angle)
    full[:, HALF : HALF + KMAX] = np.sin(angle)
    high, low = high_low(full)
    forward = np.concatenate([high[:BLOCK], high[:BLOCK], low[:BLOCK]], axis=0)
    inverse = np.concatenate([high.T, high.T, low.T], axis=0)
    return forward, inverse


def phase_table(z):
    k = np.arange(KMAX)
    table = np.zeros((z.n_lon, round_up(2 * z.blocks + 2, 8), HALF), np.float32)
    for place in range(z.n_lon):
        for n, column in enumerate([*range(0, z.ext, BLOCK), -1]):
            angle = ((place * z.lon + column) * k % z.nlon) * (2.0 * np.pi / z.nlon)
            table[place, 2 * n, :KMAX] = np.cos(angle)
            table[place, 2 * n + 1, :KMAX] = np.sin(angle)
    return table


def row_table(z):
    lam_step = np.float32(2.0 * math.pi / z.nlon)
    phi_step = np.float32(math.pi / z.nlat)
    latitude = np.float32(-0.5 * math.pi) + (
        np.arange(z.nlat, dtype=np.float32) + np.float32(0.5)
    ) * phi_step
    cosine = np.cos(latitude.astype(np.float64)).astype(np.float32)
    sine = np.sin(latitude.astype(np.float64)).astype(np.float32)
    north_coef = np.float32(STEP_FACTOR) * lam_step / phi_step
    table = np.zeros((z.n_lat, z.rows, 8), np.float32)
    for place in range(z.n_lat):
        for flat in range(z.rows):
            inner, level = flat // z.lev, flat % z.lev
            inner = -1 if inner == z.lat + 1 else inner
            row = place * z.lat + inner
            one = table[place, flat]
            one[LEVEL], one[NUMBER] = level, -1
            one[OWN] = 0 <= inner < z.lat
            if 0 <= row < z.nlat:
                one[EAST_COEF] = np.float32(STEP_FACTOR) / cosine[row]
                one[SINE], one[COSINE] = sine[row], cosine[row]
                one[NORTH_COEF] = north_coef / cosine[row]
                if row < z.polar:
                    one[POLAR], one[NUMBER] = 1, row
                elif row >= z.nlat - z.polar:
                    one[POLAR], one[NUMBER] = 1, row - (z.nlat - 2 * z.polar)
    return table


def on_polar_band(z):
    lat_index = lax.axis_index("lat")
    return (lat_index < z.n_lat // 4) | (lat_index >= z.n_lat - z.n_lat // 4)


def split(x):
    high = x.astype(jnp.bfloat16)
    return high, (x - high.astype(jnp.float32)).astype(jnp.bfloat16)


def store_split(lhs_ref, first_row, x):
    rows, width = x.shape
    high, low = split(x)
    at = slice(first_row, first_row + rows)
    lhs_ref[at, :width] = high
    lhs_ref[at, width : 2 * width] = low
    lhs_ref[at, 2 * width :] = high


def pad_rows(x, rows):
    if x.shape[0] == rows:
        return x
    return jnp.concatenate([x, jnp.zeros((rows - x.shape[0], x.shape[1]), x.dtype)], axis=0)


def phase_of(phase_ref, n):
    return phase_ref[2 * n : 2 * n + 1], phase_ref[2 * n + 1 : 2 * n + 2]


def packed_rows(rows):
    return 5 * rows + round_up(-(-rows // 2), 8) + 16


def lanes_of(x):
    return lax.broadcasted_iota(jnp.int32, x.shape, 1)


def pack(x, out_ref):
    rows = x.shape[0]
    half = round_up(-(-rows // 2), 8)
    tiles = [x[:, n : n + 128] for n in range(0, WIDE, 128)]
    left = tiles[5]
    lane = lanes_of(left)
    tiles[2] = jnp.where(lane < MORE, tiles[2], roll(left, MOVED, 1))
    for n in range(5):
        out_ref[n * rows : (n + 1) * rows] = tiles[n]
    lower = pad_rows(left[half:], half)
    out_ref[5 * rows : 5 * rows + half] = jnp.where(lane[:half] < 64, left[:half], roll(lower, 64, 1))
    out_ref[5 * rows + half :] = pad_rows(roll(left, -64, 1), 128).T[:16]


def unpack(x, rows):
    half = round_up(-(-rows // 2), 8)
    tiles = [x[n * rows : (n + 1) * rows] for n in range(5)]
    pairs = x[5 * rows : 5 * rows + half]
    ends = pad_rows(x[5 * rows + half :], 128).T[:rows]
    left = jnp.concatenate([pairs, roll(pairs, 64, 1)[: rows - half]], axis=0)
    lane = lanes_of(left)
    left = jnp.where(lane < 64, left, jnp.where(lane < LEFT, roll(ends, 64, 1), roll(tiles[2], -MOVED, 1)))
    return jnp.concatenate([*tiles, left], axis=1)


def forward_sums(
    z, x, basis_ref, phase_ref, lhs_ref, out_ref, at=slice(None), basis_here=None
):
    count = round_up(x.shape[0], 16)
    for block in range(z.blocks):
        part = pad_rows(x[:, block * BLOCK : (block + 1) * BLOCK], count)
        store_split(lhs_ref, block * count, part)
    lhs = lhs_ref[: z.blocks * count]
    if basis_here is not None:
        basis_here()
    sums = jnp.dot(lhs, basis_ref[...], preferred_element_type=jnp.float32)
    real = imag = None
    for block in range(z.blocks):
        cos, sin = phase_of(phase_ref, block)
        part = sums[block * count : block * count + x.shape[0]]
        a, b = part[:, :HALF], part[:, HALF:]
        more_real, more_imag = a * cos - b * sin, a * sin + b * cos
        real = more_real if real is None else real + more_real
        imag = more_imag if imag is None else imag + more_imag
    out_ref[at, :HALF] = real
    out_ref[at, HALF:] = imag


def inverse_rows(z, coef, basis_ref, phase_ref, lhs_ref, out_ref, at=slice(None)):
    a, b = coef[:, :HALF], coef[:, HALF:]
    count, width = round_up(coef.shape[0], 16), z.inverse_block
    blocks = range(z.ext // width)
    for block in blocks:
        cos, sin = phase_of(phase_ref, block * width // BLOCK)
        turned = jnp.concatenate([a * cos + b * sin, b * cos - a * sin], axis=1)
        store_split(lhs_ref, block * count, pad_rows(turned, count))
    lhs = lhs_ref[: len(blocks) * count]
    rows = jnp.dot(lhs, basis_ref[...], preferred_element_type=jnp.float32)
    for block in blocks:
        out_ref[at, block * width : (block + 1) * width] = rows[
            block * count : block * count + coef.shape[0]
        ]


def roll(x, shift, axis):
    return pltpu.roll(x, shift % x.shape[axis], axis)


def east_diff(x):
    return roll(x, -1, 1) - roll(x, 1, 1)


def flat_rows(z, ref):
    return ref[...].reshape(z.own, ref.shape[2])


def widen(z, x):
    return jnp.concatenate([x, jnp.zeros((x.shape[0], z.ext - x.shape[1]), x.dtype)], axis=1)


def put_lane(x, at, column):
    lane = lax.broadcasted_iota(jnp.int32, x.shape, 1)
    return jnp.where(lane == at, column, x)


def column_of(row_ref, which):
    return row_ref[:, which : which + 1]


def north_factor(z):
    return STEP_FACTOR * (2.0 * math.pi / z.nlon) / (math.pi / z.nlat)


def look_up(number, table_ref):
    table = table_ref[...].astype(jnp.float32)
    lane = lax.broadcasted_iota(jnp.int32, (number.shape[0], table.shape[1]), 1)
    return jnp.sum(jnp.where(lane == number, table, 0.0), axis=1, keepdims=True)


def coefficients(z, sums, kept):
    lane = lax.broadcasted_iota(jnp.int32, (1, WIDE), 1)
    k = jnp.where(lane < HALF, lane, lane - HALF)
    weight = jnp.where(k == 0, 1.0 / z.nlon, 2.0 / z.nlon).astype(jnp.float32)
    keep = (k.astype(jnp.float32) < kept) & (k < KMAX)
    return jnp.where(keep, sums * weight, 0.0)


def slot_order(z, number, row_ref, slot_ref):
    lat_index = lax.axis_index("lat")
    slot = look_up(number, slot_ref).astype(jnp.int32)
    theirs = slot - lax.rem(lat_index + z.half_axis, z.n_lat) * z.help
    mine = slot - lat_index * z.help
    level = column_of(row_ref, LEVEL).astype(jnp.int32)
    flat = lax.broadcasted_iota(jnp.int32, slot.shape, 0)
    place = jnp.where((mine >= 0) & (mine < z.help), z.helped + mine * z.lev + level, -1)
    place = jnp.where((theirs >= 0) & (theirs < z.help), theirs * z.lev + level, place)
    place = jnp.where(number >= 0, place, -1)
    place = jnp.where(flat < z.own, place, flat)
    lane = lax.broadcasted_iota(jnp.int32, (z.rows, round_up(z.rows, 128)), 1)
    return (lane == place).astype(jnp.float32)


def reorder(chosen, values):
    high, low = (
        lax.dot_general(
            chosen.astype(jnp.bfloat16),
            part,
            (((0,), (0,)), ((), ())),
            preferred_element_type=jnp.float32,
        )
        for part in split(values)
    )
    return high + low


def sector_part(z, coef, place):
    part = None
    for one in range(z.n_lon):
        first = one * z.spec_width
        first = first if first < KMAX else first - KMAX + HALF
        this = coef[:, first : first + z.spec_width]
        part = this if part is None else jnp.where(place == one, this, part)
    return part


def depths(z, depth_ref, row_ref):
    level = column_of(row_ref, LEVEL)[: z.own]
    depth = jnp.zeros_like(level)
    for lev in range(z.lev):
        depth = jnp.where(level == lev, depth_ref[lev], depth)
    return depth


def store_rims(z, ref, g, we, wn, last):
    edge = 2 * z.lev
    ref[:edge] = g[z.own - edge :] if last else g[:edge]
    ref[edge : edge + z.lev] = we[z.own - z.lev :] if last else we[: z.lev]
    ref[edge + z.lev :] = wn[z.own - z.lev :] if last else wn[: z.lev]


def east_shares_of(
    z, at, we_ref, wn_ref, g_ref, row_ref, phase_ref, basis_ref, out_ref, lhs_ref, share_ref,
    basis_here=None,
):
    inner, rows = slice(at.start // z.lev, at.stop // z.lev), at.stop - at.start
    g, we, wn = (ref[inner].reshape(rows, z.lon) for ref in (g_ref, we_ref, wn_ref))

    @pl.when(on_polar_band(z))
    def _():
        coef, sine = column_of(row_ref, EAST_COEF)[at], column_of(row_ref, SINE)[at]
        new = widen(z, we + CORIOLIS * sine * wn) - coef * east_diff(widen(z, g))
        tail = put_lane(new[:, z.ext - 128 :], 127, 0.0)
        new = jnp.concatenate([new[:, : z.ext - 128], tail], axis=1)
        forward_sums(
            z, new, basis_ref, phase_ref, lhs_ref, share_ref, slice(rows), basis_here=basis_here
        )
        cos, sin = phase_of(phase_ref, z.blocks)
        before = -coef * g[:, 0:1]
        share_ref[:rows, :HALF] += before * cos
        share_ref[:rows, HALF:] += before * sin
        pack(share_ref[...], out_ref)

    @pl.when(jnp.logical_not(on_polar_band(z)))
    def _():
        if basis_here is not None:
            basis_here()
        last = z.lon - 1
        columns = jnp.zeros((rows, 128), jnp.float32)
        edges = ((g, last - 1), (g, last), (we, last), (wn, last), (g, 0), (g, 1), (we, 0), (wn, 0))
        for n, (x, column) in enumerate(edges):
            columns = put_lane(columns, n, x[:, column : column + 1])
        out_ref[...] = jnp.zeros_like(out_ref)
        out_ref[:rows] = columns


def east_first(
    z, we_hbm, wn_hbm, g_hbm, row_hbm, phase_hbm, basis_hbm,
    share_ref, even_ref, odd_ref, we_ref, wn_ref, g_ref, row_ref, phase_ref, basis_ref, lhs_ref, sums_ref, sems,
):
    fields = ((g_hbm, g_ref), (we_hbm, we_ref), (wn_hbm, wn_ref))
    cut, rim = z.first // z.lev, z.lat - 2

    def copies(first_sem, pairs):
        return [pltpu.make_async_copy(*pair, sems.at[first_sem + n]) for n, pair in enumerate(pairs)]

    tables = copies(
        0,
        (
            (row_hbm.at[lax.axis_index("lat")], row_ref),
            (phase_hbm.at[lax.axis_index("lon")], phase_ref),
        ),
    )
    first = copies(2, [(a.at[:cut], b.at[:cut]) for a, b in fields])
    basis = copies(5, [(basis_hbm, basis_ref)])
    edge = copies(6, [(a.at[rim:], b.at[rim:]) for a, b in fields])
    between = copies(9, [(a.at[cut:rim], b.at[cut:rim]) for a, b in fields])
    for copy in first + tables + basis + edge:
        copy.start()
    for copy in first + tables:
        copy.wait()
    for copy in between:
        copy.start()

    def basis_here():
        for copy in basis + edge:
            copy.wait()

    east_shares_of(
        z, slice(0, z.first), we_ref, wn_ref, g_ref, row_ref, phase_ref, basis_ref, share_ref, lhs_ref,
        sums_ref, basis_here,
    )
    odd = lax.rem(lax.axis_index("lat"), 2) == 1
    last, flat = z.lat - 1, (z.lev, z.lon)
    far = (g_ref[last - 1], g_ref[last], we_ref[last], wn_ref[last])
    near = (g_ref[0], g_ref[1], we_ref[0], wn_ref[0])
    for n, (bottom, top) in enumerate(zip(far, near, strict=True)):
        at = slice(n * z.lev, (n + 1) * z.lev)
        even_ref[at] = jnp.where(odd, top, bottom).reshape(flat)
        odd_ref[at] = jnp.where(odd, bottom, top).reshape(flat)
    for copy in between:
        copy.wait()


def north_forward(
    z, we_ref, wn_ref, g_ref, even_ref, odd_ref, row_ref, phase_ref, basis_ref, kept_ref, slot_ref, *rest
):
    ahead_ref, rest_ref, north_ref, chosen_ref, sorted_ref, g_rows, lhs_ref, share_ref = rest
    edge, lev = 2 * z.lev, z.lev
    odd = lax.rem(lax.axis_index("lat"), 2) == 1
    below = jnp.where(odd, odd_ref[...], even_ref[...])
    above = jnp.where(odd, even_ref[...], odd_ref[...])
    coef, sine = north_factor(z), CORIOLIS * column_of(row_ref, SINE)
    own = flat_rows(z, g_ref)
    g_rows[: z.own] = own
    g_rows[z.own : z.own + lev] = below[:lev]
    g_rows[z.own + lev :] = above[lev:edge]
    g = g_rows[...]
    diff = (roll(g, -lev, 0) - roll(g, lev, 0))[: z.own]
    north_ref[: z.own] = flat_rows(z, wn_ref) - coef * diff - sine[: z.own] * flat_rows(z, we_ref)
    for at, diff, rim in (
        (z.own, below[lev:edge] - own[z.own - lev :], below),
        (z.own + lev, own[:lev] - above[:lev], above),
    ):
        we, wn = rim[edge : edge + lev], rim[edge + lev :]
        north_ref[at : at + lev] = wn - coef * diff - sine[at : at + lev] * we
    number = column_of(row_ref, NUMBER).astype(jnp.int32)
    kept = look_up(number, kept_ref)

    @pl.when(on_polar_band(z))
    def _():
        forward_sums(z, widen(z, north_ref[...]), basis_ref, phase_ref, lhs_ref, share_ref)
        share_ref[:, SPARE:HALF] = put_lane(share_ref[:, SPARE:HALF], KMAX - SPARE, kept)
        chosen = slot_order(z, number, row_ref, slot_ref)
        ordered = reorder(chosen, share_ref[...])
        pack(ordered[: z.ahead], ahead_ref)
        pack(ordered[z.ahead : z.rows], rest_ref)
        sorted_ref[...] = ordered[: z.rows, SPARE:HALF]
        chosen_ref[...] = chosen

    @pl.when(jnp.logical_not(on_polar_band(z)))
    def _():
        ahead_ref[...] = jnp.zeros_like(ahead_ref)
        chosen_ref[...] = jnp.zeros_like(chosen_ref)
        share_ref[...] = jnp.zeros_like(share_ref)
        rows = widen(z, north_ref[z.own :])
        forward_sums(z, rows, basis_ref, phase_ref, lhs_ref, share_ref, slice(z.own, z.rows))
        pack(share_ref[z.ahead :], rest_ref)
        sorted_ref[...] = jnp.broadcast_to(kept, sorted_ref.shape)


def arrival(arrived_ref, out_ref):
    out_ref[...] = arrived_ref[:8, :128]


def east_inverse(
    z, depth_ref, we_ref, wn_ref, g_ref, thick_ref, row_ref, phase_ref, kept_ref, chosen_ref, first_here,
    *rest,
):
    del first_here
    firsts, seconds, rest = rest[: z.n_lon], rest[z.n_lon : 2 * z.n_lon], rest[2 * z.n_lon :]
    basis_ref, final_ref, part_ref, keep_ref, send_ref, lhs_ref, rows_ref, sums_ref = rest
    coef, sine = column_of(row_ref, EAST_COEF)[: z.own], column_of(row_ref, SINE)[: z.own]

    @pl.when(on_polar_band(z))
    def _():
        number = column_of(row_ref, NUMBER)[: z.own].astype(jnp.int32)
        second = round_up(z.own - z.first, 8)
        sums_ref[: z.first] = unpack(sum(ref[...] for ref in firsts), z.first)
        sums_ref[z.first :] = unpack(sum(ref[...] for ref in seconds), second)[: z.own - z.first]
        waves = coefficients(z, sums_ref[...], look_up(number, kept_ref))
        part = sector_part(z, waves, lax.axis_index("lon"))
        ordered = reorder(chosen_ref[: z.own], part)
        send_ref[...] = ordered[: z.helped].reshape(send_ref.shape)
        keep_ref[...] = ordered[z.helped : 2 * z.helped].reshape(keep_ref.shape)
        inverse_rows(z, waves, basis_ref, phase_ref, lhs_ref, rows_ref)
        cos, sin = phase_of(phase_ref, z.blocks)
        before = jnp.sum(waves[:, :HALF] * cos + waves[:, HALF:] * sin, axis=1, keepdims=True)
        rows_ref[:, z.ext - 128 :] = put_lane(rows_ref[:, z.ext - 128 :], 127, before)

    @pl.when(jnp.logical_not(on_polar_band(z)))
    def _():
        send_ref[...] = jnp.zeros_like(send_ref)
        keep_ref[...] = jnp.zeros_like(keep_ref)
        left, right = (
            jnp.concatenate([firsts[n][: z.first], seconds[n][: z.own - z.first]], axis=0)
            for n in (1, -1)
        )
        at_right = z.lon - (z.ext - 128)

        def rimmed(ref, left_of, right_of):
            x = widen(z, flat_rows(z, ref))
            tail = x[:, z.ext - 128 :]
            for n, lane in enumerate(right_of):
                tail = put_lane(tail, at_right + n, right[:, lane : lane + 1])
            for n, lane in enumerate(left_of):
                tail = put_lane(tail, 127 - n, left[:, lane : lane + 1])
            return jnp.concatenate([x[:, : z.ext - 128], tail], axis=1)

        g = rimmed(g_ref, (1, 0), (4, 5))
        we, wn = rimmed(we_ref, (2,), (6,)), rimmed(wn_ref, (3,), (7,))
        rows_ref[...] = we - coef * east_diff(g) + CORIOLIS * sine * wn

    final = rows_ref[...]
    final_ref[...] = final[:, : z.lon].reshape(final_ref.shape)
    change = depths(z, depth_ref, row_ref) * coef * east_diff(final)[:, : z.lon]
    part_ref[...] = flat_rows(z, thick_ref) - change


def ahead_waves(z, shares, sorted_ref):
    sums = unpack(sum(ref[...] for ref in shares), z.ahead)
    return coefficients(z, sums, sorted_ref[: z.ahead, MORE : MORE + 1])


def send_spectra(z, east_ref, sorted_ref, *rest):
    shares, send_ref, waves_ref = rest[:-2], rest[-2], rest[-1]
    waves = ahead_waves(z, shares, sorted_ref)
    waves_ref[...] = waves
    part = sector_part(z, waves, lax.axis_index("lon"))
    send_ref[0] = east_ref[...]
    send_ref[1] = part[: z.helped].reshape(east_ref.shape)


def ahead_inverse(z, phase_ref, waves_ref, basis_ref, high_ref, low_ref, lhs_ref, rows_ref):
    @pl.when(on_polar_band(z))
    def _():
        inverse_rows(z, waves_ref[...], basis_ref, phase_ref, lhs_ref, rows_ref)
        high_ref[...], low_ref[...] = split(rows_ref[...])


def north_inverse(
    z, active, depth_ref, north_ref, part_ref, row_ref, phase_ref, chosen_ref, sorted_ref, waves_ahead,
    high_ahead, low_ahead, *rest,
):
    shares, rest = rest[: z.n_lon], rest[z.n_lon :]
    basis_ref, final_ref, thick_ref, column_ref, keep_ref, lhs_ref, rows_ref, high_ref, low_ref = rest

    @pl.when(active & on_polar_band(z))
    def _():
        more = z.ahead - 8
        sums = unpack(sum(ref[...] for ref in shares), z.rows - z.ahead)
        waves = coefficients(z, sums, sorted_ref[z.ahead :, MORE : MORE + 1])
        both = jnp.concatenate([waves_ahead[more:], waves], axis=0)
        part = sector_part(z, both, lax.axis_index("lon"))
        first = z.helped - more
        keep_ref[...] = part[first : first + z.helped].reshape(keep_ref.shape)
        inverse_rows(z, waves, basis_ref, phase_ref, lhs_ref, rows_ref, slice(z.rows - z.ahead))
        count = high_ref.shape[0] - z.ahead
        rest_high, rest_low = split(pad_rows(rows_ref[: z.rows - z.ahead], count))
        high_ref[: z.ahead], low_ref[: z.ahead] = high_ahead[...], low_ahead[...]
        high_ref[z.ahead :], low_ref[z.ahead :] = rest_high, rest_low
        chosen = chosen_ref[:, : z.mm_rows].astype(jnp.bfloat16)
        rows_ref[...] = jnp.dot(
            chosen, high_ref[...], preferred_element_type=jnp.float32
        ) + jnp.dot(chosen, low_ref[...], preferred_element_type=jnp.float32)
        beyond = slice(z.own, z.rows)
        polar = column_of(row_ref, POLAR)[beyond] > 0.0
        rows_ref[beyond, : z.lon] = jnp.where(polar, rows_ref[beyond, : z.lon], north_ref[beyond])

    @pl.when(active & jnp.logical_not(on_polar_band(z)))
    def _():
        keep_ref[...] = jnp.zeros_like(keep_ref)
        beyond = slice(z.own, z.rows)
        at = slice(z.own - z.ahead, z.rows - z.ahead)
        sums = unpack(sum(ref[...] for ref in shares), z.rows - z.ahead)
        waves = coefficients(z, sums[at], sorted_ref[beyond, MORE : MORE + 1])
        inverse_rows(z, waves, basis_ref, phase_ref, lhs_ref, rows_ref, beyond)
        polar = column_of(row_ref, POLAR)[beyond] > 0.0
        rows_ref[beyond, : z.lon] = jnp.where(polar, rows_ref[beyond, : z.lon], north_ref[beyond])
        rows_ref[: z.own, : z.lon] = north_ref[: z.own]

    @pl.when(active)
    def _():
        final = rows_ref[:, : z.lon]
        final_ref[...] = final[: z.own].reshape(final_ref.shape)
        scaled = final * column_of(row_ref, COSINE)
        diff = (roll(scaled, -z.lev, 0) - roll(scaled, z.lev, 0))[: z.own]
        scale = depths(z, depth_ref, row_ref) * column_of(row_ref, NORTH_COEF)[: z.own]
        thick_ref[...] = (part_ref[...] - scale * diff).reshape(thick_ref.shape)
        column_ref[...] = sum(thick_ref[:, lev, :] for lev in range(z.lev))


def sends_column():
    return lax.axis_index("lev") > 0


def north_deeper(z, *refs):
    north_inverse(z, sends_column(), *refs)


def north_shallowest(z, east_keep, north_keep, arrived_ref, *rest):
    *refs, spectra_ref, column_ref, keep_ref, lhs_ref, rows_ref, high_ref, low_ref = rest
    active = jnp.logical_not(sends_column())
    north_inverse(z, active, *refs, column_ref, keep_ref, lhs_ref, rows_ref, high_ref, low_ref)

    @pl.when(sends_column())
    def _():
        keep_ref[...] = north_keep[...]

    polar = on_polar_band(z)
    spectra_ref[0] = jnp.where(polar, east_keep[...], arrived_ref[0])
    spectra_ref[1] = jnp.where(polar, keep_ref[...], arrived_ref[1])


def finish(z, surface_ref, *rest):
    deeper_fields, own_fields, deeper, outs = rest[:2], rest[2:4], rest[4 : 3 + z.n_lev], rest[3 + z.n_lev :]
    spectra, (final_out, thick_out, geo_out, spectra_out, geo_ref, sems) = outs[0], outs[1:]

    def store(fields):
        copies = [
            pltpu.make_async_copy(*pair, sems.at[n])
            for n, pair in enumerate(
                ((fields[0], final_out), (fields[1], thick_out), (spectra, spectra_out))
            )
        ]
        for copy in copies:
            copy.start()
        for n in range(z.cuts):
            at = slice(n * z.lat // z.cuts, (n + 1) * z.lat // z.cuts)
            column = sum(ref[at] for ref in deeper)
            for lev in reversed(range(z.lev)):
                column = column + fields[1][at, lev, :]
                geo_ref[at, lev, :] = surface_ref[at] + GRAVITY * column
            copies.append(pltpu.make_async_copy(geo_ref.at[at], geo_out.at[at], sems.at[3 + n]))
            copies[-1].start()
        for copy in copies:
            copy.wait()

    @pl.when(sends_column())
    def _():
        store(deeper_fields)

    @pl.when(jnp.logical_not(sends_column()))
    def _():
        store(own_fields)


def call(kernel, n_in, out_shape, scratch, micros, spaces=None, in_hbm=0, vmem=24):
    vmem_spec = pl.BlockSpec(memory_space=pltpu.VMEM)
    spaces = spaces or {}
    return pl.pallas_call(
        kernel,
        in_specs=[
            pl.BlockSpec(memory_space=spaces[n]) if n in spaces else vmem_spec for n in range(n_in)
        ],
        out_specs=[pl.BlockSpec(memory_space=pltpu.HBM)] * in_hbm
        + [vmem_spec] * (len(out_shape) - in_hbm),
        out_shape=[
            jax.ShapeDtypeStruct(s, jnp.float32) if isinstance(s, tuple) else s for s in out_shape
        ],
        scratch_shapes=scratch,
        compiler_params=pltpu.CompilerParams(vmem_limit_bytes=vmem * MIB),
        cost_estimate=pl.CostEstimate(
            flops=int(micros * 1.15e9), bytes_accessed=0, transcendentals=0
        ),
    )


def shifted(block, axis, distance):
    count = lax.axis_size(axis)
    return lax.ppermute(block, axis, [(i, (i + distance) % count) for i in range(count)])


def level_inside(x):
    return jnp.swapaxes(x, -3, -2)


def local(
    wind_east, wind_north, thickness, geopot, surface_geopot, mean_depth, kept_modes, slot_table
):
    z = Sizes(thickness.shape, {axis: lax.axis_size(axis) for axis in ("lat", "lon", "lev")})
    wind_east, wind_north, thickness, geopot = (
        level_inside(x) for x in (wind_east, wind_north, thickness, geopot)
    )
    field = (z.lat, z.lev, z.lon)
    forward, inverse = (jnp.asarray(x) for x in basis_tables(z))
    phase = jnp.asarray(phase_table(z))
    per_row = jnp.asarray(row_table(z))
    kept = kept_modes[None, :]
    slots = slot_table[None, :]
    payload = (z.rows, WIDE)
    rims = (4 * z.lev, z.lon)
    spec = (z.help, z.lev, z.spec_width)
    waves_lhs = pltpu.VMEM((z.ext // z.inverse_block * z.mm_rows, 3 * WIDE), jnp.bfloat16)

    row_shape, phase_shape = per_row.shape[1:], phase.shape[1:]
    pinned = [
        pltpu.with_memory_space_constraint(x, pltpu.HBM)
        for x in (wind_east, wind_north, geopot, per_row, phase, forward)
    ]
    columns_lhs = pltpu.VMEM((z.blocks * z.mm_rows, 3 * BLOCK), jnp.bfloat16)
    waves_lhs = pltpu.VMEM((z.ext // z.inverse_block * z.mm_rows, 3 * WIDE), jnp.bfloat16)

    share_first, to_even, to_odd, wind_east, wind_north, geopot, per_row, phase, forward = call(
        functools.partial(east_first, z),
        6,
        [(packed_rows(z.first), 128), rims, rims]
        + [pltpu.VMEM(s, jnp.float32) for s in (field, field, field, row_shape, phase_shape)]
        + [pltpu.VMEM(forward.shape, forward.dtype)],
        [
            columns_lhs,
            pltpu.VMEM((z.first, WIDE), jnp.float32),
            pltpu.SemaphoreType.DMA((12,)),
        ],
        1,
        {n: pltpu.HBM for n in range(6)},
    )(*pinned)
    second = round_up(z.own - z.first, 8)
    (share_second,) = call(
        functools.partial(east_shares_of, z, slice(z.first, z.own)),
        6,
        [(packed_rows(second), 128)],
        [columns_lhs, pltpu.VMEM((second, WIDE), jnp.float32)],
        0.18,
    )(wind_east, wind_north, geopot, per_row, phase, forward)
    east_firsts, east_seconds = (
        [x] + [shifted(x, "lon", s) for s in range(1, z.n_lon)] for x in (share_first, share_second)
    )
    met = []
    for start, rim in enumerate((to_even, to_odd)):
        pairs = [(i, i + 1) for i in range(start, z.n_lat - 1, 2)]
        met.append(lax.ppermute(rim, "lat", pairs + [(b, a) for a, b in pairs]))

    places = round_up(z.rows, 128)
    north_ahead, north_rest, north_new, chosen, kept_sorted = call(
        functools.partial(north_forward, z),
        10,
        [
            (packed_rows(z.ahead), 128),
            (packed_rows(z.rows - z.ahead), 128),
            (z.rows, z.lon),
            (z.rows, places),
            (z.rows, 128),
        ],
        [
            pltpu.VMEM((z.rows, z.lon), jnp.float32),
            columns_lhs,
            pltpu.VMEM((z.rows, WIDE), jnp.float32),
        ],
        0.8,
    )(
        wind_east, wind_north, geopot, *met, per_row, phase, forward, kept, slots
    )
    north_rests = [north_rest] + [shifted(north_rest, "lon", s) for s in range(1, z.n_lon)]
    polar_bands = [i for i in range(z.n_lat) if i < z.n_lat // 4 or i >= z.n_lat - z.n_lat // 4]
    north_aheads = [north_ahead]
    for distance in range(1, z.n_lon):
        route = [
            (band * z.n_lon + lon, band * z.n_lon + (lon + distance) % z.n_lon)
            for band in polar_bands
            for lon in range(z.n_lon)
        ]
        north_aheads.append(lax.ppermute(north_ahead, ("lat", "lon"), route))

    (first_here,) = call(arrival, 1, [(8, 128)], [], 0.95)(east_firsts[1])
    east_final, thick_part, east_keep, east_send = call(
        functools.partial(east_inverse, z),
        11 + 2 * z.n_lon,
        [field, (z.own, z.lon), spec, spec],
        [
            waves_lhs,
            pltpu.VMEM((z.own, z.ext), jnp.float32),
            pltpu.VMEM((z.own, WIDE), jnp.float32),
        ],
        1,
        {0: pltpu.SMEM},
    )(
        mean_depth, wind_east, wind_north, geopot, thickness, per_row, phase, kept, chosen,
        first_here, *east_firsts, *east_seconds, inverse,
    )

    to_helper, waves_ahead = call(
        functools.partial(send_spectra, z), 2 + z.n_lon, [(2, *spec), (z.ahead, WIDE)], [], 0.1
    )(east_send, kept_sorted, *north_aheads)
    arrived = lax.ppermute(
        to_helper, "lat", [(i, (i + z.half_axis) % z.n_lat) for i in polar_bands]
    )

    ahead_rows = jax.ShapeDtypeStruct((z.ahead, z.ext), jnp.bfloat16)
    ahead_high, ahead_low = call(
        functools.partial(ahead_inverse, z),
        3,
        [ahead_rows] * 2,
        [waves_lhs, pltpu.VMEM((z.ahead, z.ext), jnp.float32)],
        0.5,
    )(phase, waves_ahead, inverse)

    operands = (
        mean_depth, north_new, thick_part, per_row, phase, chosen, kept_sorted, waves_ahead,
        ahead_high, ahead_low, *north_rests, inverse,
    )
    in_vmem = pltpu.VMEM(field, jnp.float32)
    scratch = [waves_lhs, pltpu.VMEM((z.rows, z.ext), jnp.float32)]
    scratch += [pltpu.VMEM((z.mm_rows, z.ext), jnp.bfloat16)] * 2
    final_deeper, thick_deeper, column, north_keep = call(
        functools.partial(north_deeper, z),
        len(operands),
        [in_vmem, in_vmem, (z.lat, z.lon), spec],
        scratch,
        2,
        {0: pltpu.SMEM},
    )(*operands)
    deeper = [
        lax.ppermute(column, "lev", [(i, i - distance) for i in range(distance, z.n_lev)])
        for distance in range(1, z.n_lev)
    ]
    final_own, thick_own, joined = call(
        functools.partial(north_shallowest, z),
        3 + len(operands),
        [in_vmem, in_vmem, pltpu.VMEM((2, *spec), jnp.float32)],
        [pltpu.VMEM((z.lat, z.lon), jnp.float32), pltpu.VMEM(spec, jnp.float32)] + scratch,
        3.2,
        {3: pltpu.SMEM},
    )(east_keep, north_keep, arrived, *operands)
    north_final, thick_new, geo_new, spectra = call(
        functools.partial(finish, z),
        6 + len(deeper),
        [pltpu.HBM(field, jnp.float32)] * 3 + [pltpu.HBM((2, *spec), jnp.float32)],
        [pltpu.VMEM(field, jnp.float32), pltpu.SemaphoreType.DMA((3 + z.cuts,))],
        1,
        in_hbm=4,
    )(surface_geopot, final_deeper, thick_deeper, final_own, thick_own, *deeper, joined)
    return tuple(level_inside(x) for x in (east_final, north_final, thick_new, geo_new, spectra))


def solution(mesh):
    field = P(("members", "lev"), "lat", "lon")
    return jax.shard_map(
        local,
        mesh=mesh,
        in_specs=(field, field, field, field, P("lat", "lon"), P("lev"), P(), P()),
        out_specs=(field, field, field, field, P(None, ("members", "lev"), "lat", "lon")),
        check_vma=False,
    )
```

```python
import functools
import math

import jax
import jax.numpy as jnp
import numpy as np
from jax import lax
from jax.experimental import pallas as pl
from jax.experimental.pallas import tpu as pltpu
from jax.sharding import PartitionSpec as P

KMAX = 360
HALF = 384
WIDE = 2 * HALF
SPARE = HALF - 128
MORE = KMAX - SPARE
MOVED = 128 - MORE
LEFT = MORE - MOVED
BLOCK = 256
INVERSE_BLOCK = 512

STEP_FACTOR = 0.15
CORIOLIS = 0.2
GRAVITY = 0.25

MIB = 1024 * 1024

EAST_COEF, SINE, COSINE, NORTH_COEF, LEVEL, POLAR, NUMBER, OWN = range(8)


def round_up(value, step):
    return -(-value // step) * step


class Sizes:
    def __init__(self, shape, counts):
        self.lev, self.lat, self.lon = shape
        self.n_lat, self.n_lon, self.n_lev = counts["lat"], counts["lon"], counts["lev"]
        self.nlat, self.nlon = self.lat * self.n_lat, self.lon * self.n_lon
        self.polar = self.nlat // 4
        self.help = self.lat // 2
        self.half_axis = self.n_lat // 2
        self.own = self.lat * self.lev
        self.rows = self.own + 2 * self.lev
        assert self.rows % 8 == 0
        self.mm_rows = round_up(self.rows, 16)
        self.ext = round_up(self.lon + 4, BLOCK)
        self.blocks = self.ext // BLOCK
        self.inverse_block = min(INVERSE_BLOCK, self.ext)
        assert self.ext % self.inverse_block == 0
        self.spec_width = 2 * KMAX // self.n_lon
        self.helped = self.help * self.lev
        self.ahead = round_up(self.helped, 16)
        self.cuts = 2
        self.first = min(round_up(self.own * 4 // 9, 8 * self.lev), self.own)


def high_low(x):
    x = x.astype(np.float32)
    high = x.astype(jnp.bfloat16)
    return high, (x - high.astype(np.float32)).astype(jnp.bfloat16)


def basis_tables(z):
    k = np.arange(KMAX)
    angle = (np.arange(z.inverse_block)[:, None] * k[None, :] % z.nlon) * (2.0 * np.pi / z.nlon)
    full = np.zeros((z.inverse_block, WIDE))
    full[:, :KMAX] = np.cos(angle)
    full[:, HALF : HALF + KMAX] = np.sin(angle)
    high, low = high_low(full)
    forward = np.concatenate([high[:BLOCK], high[:BLOCK], low[:BLOCK]], axis=0)
    inverse = np.concatenate([high.T, high.T, low.T], axis=0)
    return forward, inverse


def phase_table(z):
    k = np.arange(KMAX)
    table = np.zeros((z.n_lon, round_up(2 * z.blocks + 2, 8), HALF), np.float32)
    for place in range(z.n_lon):
        for n, column in enumerate([*range(0, z.ext, BLOCK), -1]):
            angle = ((place * z.lon + column) * k % z.nlon) * (2.0 * np.pi / z.nlon)
            table[place, 2 * n, :KMAX] = np.cos(angle)
            table[place, 2 * n + 1, :KMAX] = np.sin(angle)
    return table


def row_table(z):
    lam_step = np.float32(2.0 * math.pi / z.nlon)
    phi_step = np.float32(math.pi / z.nlat)
    latitude = np.float32(-0.5 * math.pi) + (
        np.arange(z.nlat, dtype=np.float32) + np.float32(0.5)
    ) * phi_step
    cosine = np.cos(latitude.astype(np.float64)).astype(np.float32)
    sine = np.sin(latitude.astype(np.float64)).astype(np.float32)
    north_coef = np.float32(STEP_FACTOR) * lam_step / phi_step
    table = np.zeros((z.n_lat, z.rows, 8), np.float32)
    for place in range(z.n_lat):
        for flat in range(z.rows):
            inner, level = flat // z.lev, flat % z.lev
            inner = -1 if inner == z.lat + 1 else inner
            row = place * z.lat + inner
            one = table[place, flat]
            one[LEVEL], one[NUMBER] = level, -1
            one[OWN] = 0 <= inner < z.lat
            if 0 <= row < z.nlat:
                one[EAST_COEF] = np.float32(STEP_FACTOR) / cosine[row]
                one[SINE], one[COSINE] = sine[row], cosine[row]
                one[NORTH_COEF] = north_coef / cosine[row]
                if row < z.polar:
                    one[POLAR], one[NUMBER] = 1, row
                elif row >= z.nlat - z.polar:
                    one[POLAR], one[NUMBER] = 1, row - (z.nlat - 2 * z.polar)
    return table


def on_polar_band(z):
    lat_index = lax.axis_index("lat")
    return (lat_index < z.n_lat // 4) | (lat_index >= z.n_lat - z.n_lat // 4)


def split(x):
    high = x.astype(jnp.bfloat16)
    return high, (x - high.astype(jnp.float32)).astype(jnp.bfloat16)


def store_split(lhs_ref, first_row, x):
    rows, width = x.shape
    high, low = split(x)
    at = slice(first_row, first_row + rows)
    lhs_ref[at, :width] = high
    lhs_ref[at, width : 2 * width] = low
    lhs_ref[at, 2 * width :] = high


def pad_rows(x, rows):
    if x.shape[0] == rows:
        return x
    return jnp.concatenate([x, jnp.zeros((rows - x.shape[0], x.shape[1]), x.dtype)], axis=0)


def phase_of(phase_ref, n):
    return phase_ref[2 * n : 2 * n + 1], phase_ref[2 * n + 1 : 2 * n + 2]


def packed_rows(rows):
    return 5 * rows + round_up(-(-rows // 2), 8) + 16


def lanes_of(x):
    return lax.broadcasted_iota(jnp.int32, x.shape, 1)


def pack(x, out_ref):
    rows = x.shape[0]
    half = round_up(-(-rows // 2), 8)
    tiles = [x[:, n : n + 128] for n in range(0, WIDE, 128)]
    left = tiles[5]
    lane = lanes_of(left)
    tiles[2] = jnp.where(lane < MORE, tiles[2], roll(left, MOVED, 1))
    for n in range(5):
        out_ref[n * rows : (n + 1) * rows] = tiles[n]
    lower = pad_rows(left[half:], half)
    out_ref[5 * rows : 5 * rows + half] = jnp.where(lane[:half] < 64, left[:half], roll(lower, 64, 1))
    out_ref[5 * rows + half :] = pad_rows(roll(left, -64, 1), 128).T[:16]


def unpack(x, rows):
    half = round_up(-(-rows // 2), 8)
    tiles = [x[n * rows : (n + 1) * rows] for n in range(5)]
    pairs = x[5 * rows : 5 * rows + half]
    ends = pad_rows(x[5 * rows + half :], 128).T[:rows]
    left = jnp.concatenate([pairs, roll(pairs, 64, 1)[: rows - half]], axis=0)
    lane = lanes_of(left)
    left = jnp.where(lane < 64, left, jnp.where(lane < LEFT, roll(ends, 64, 1), roll(tiles[2], -MOVED, 1)))
    return jnp.concatenate([*tiles, left], axis=1)


def forward_sums(
    z, x, basis_ref, phase_ref, lhs_ref, out_ref, at=slice(None), basis_here=None
):
    count = round_up(x.shape[0], 16)
    for block in range(z.blocks):
        part = pad_rows(x[:, block * BLOCK : (block + 1) * BLOCK], count)
        store_split(lhs_ref, block * count, part)
    lhs = lhs_ref[: z.blocks * count]
    if basis_here is not None:
        basis_here()
    sums = jnp.dot(lhs, basis_ref[...], preferred_element_type=jnp.float32)
    real = imag = None
    for block in range(z.blocks):
        cos, sin = phase_of(phase_ref, block)
        part = sums[block * count : block * count + x.shape[0]]
        a, b = part[:, :HALF], part[:, HALF:]
        more_real, more_imag = a * cos - b * sin, a * sin + b * cos
        real = more_real if real is None else real + more_real
        imag = more_imag if imag is None else imag + more_imag
    out_ref[at, :HALF] = real
    out_ref[at, HALF:] = imag


def inverse_blocks(z, coef, basis_ref, phase_ref, lhs_ref):
    a, b = coef[:, :HALF], coef[:, HALF:]
    count, width = round_up(coef.shape[0], 16), z.inverse_block
    blocks = range(z.ext // width)
    for block in blocks:
        cos, sin = phase_of(phase_ref, block * width // BLOCK)
        turned = jnp.concatenate([a * cos + b * sin, b * cos - a * sin], axis=1)
        store_split(lhs_ref, block * count, pad_rows(turned, count))
    lhs = lhs_ref[: len(blocks) * count]
    rows = jnp.dot(lhs, basis_ref[...], preferred_element_type=jnp.float32)
    return [rows[block * count : (block + 1) * count] for block in blocks]


def inverse_rows(z, coef, basis_ref, phase_ref, lhs_ref, out_ref, at=slice(None)):
    width = z.inverse_block
    for n, rows in enumerate(inverse_blocks(z, coef, basis_ref, phase_ref, lhs_ref)):
        out_ref[at, n * width : (n + 1) * width] = rows[: coef.shape[0]]


def inverse_split(z, coef, basis_ref, phase_ref, lhs_ref, high_ref, low_ref, first, below=0):
    width = z.inverse_block
    for n, rows in enumerate(inverse_blocks(z, coef, basis_ref, phase_ref, lhs_ref)):
        count, columns = rows.shape[0], slice(n * width, (n + 1) * width)
        high, low = split(rows)
        high_ref[first : first + count, columns] = high
        low_ref[below + first : below + first + count, columns] = low


def roll(x, shift, axis):
    return pltpu.roll(x, shift % x.shape[axis], axis)


def east_diff(x):
    return roll(x, -1, 1) - roll(x, 1, 1)


def flat_rows(z, ref):
    return ref[...].reshape(z.own, ref.shape[2])


def widen(z, x):
    return jnp.concatenate([x, jnp.zeros((x.shape[0], z.ext - x.shape[1]), x.dtype)], axis=1)


def put_lane(x, at, column):
    lane = lax.broadcasted_iota(jnp.int32, x.shape, 1)
    return jnp.where(lane == at, column, x)


def column_of(row_ref, which):
    return row_ref[:, which : which + 1]


def north_factor(z):
    return STEP_FACTOR * (2.0 * math.pi / z.nlon) / (math.pi / z.nlat)


def look_up(number, table_ref):
    table = table_ref[...].astype(jnp.float32)
    lane = lax.broadcasted_iota(jnp.int32, (number.shape[0], table.shape[1]), 1)
    return jnp.sum(jnp.where(lane == number, table, 0.0), axis=1, keepdims=True)


def coefficients(z, sums, kept):
    lane = lax.broadcasted_iota(jnp.int32, (1, WIDE), 1)
    k = jnp.where(lane < HALF, lane, lane - HALF)
    weight = jnp.where(k == 0, 1.0 / z.nlon, 2.0 / z.nlon).astype(jnp.float32)
    keep = (k.astype(jnp.float32) < kept) & (k < KMAX)
    return jnp.where(keep, sums * weight, 0.0)


def slot_order(z, number, row_ref, slot_ref):
    lat_index = lax.axis_index("lat")
    slot = look_up(number, slot_ref).astype(jnp.int32)
    theirs = slot - lax.rem(lat_index + z.half_axis, z.n_lat) * z.help
    mine = slot - lat_index * z.help
    level = column_of(row_ref, LEVEL).astype(jnp.int32)
    flat = lax.broadcasted_iota(jnp.int32, slot.shape, 0)
    place = jnp.where((mine >= 0) & (mine < z.help), z.helped + mine * z.lev + level, -1)
    place = jnp.where((theirs >= 0) & (theirs < z.help), theirs * z.lev + level, place)
    place = jnp.where(number >= 0, place, -1)
    place = jnp.where(flat < z.own, place, flat)
    lane = lax.broadcasted_iota(jnp.int32, (z.rows, round_up(z.rows, 128)), 1)
    return (lane == place).astype(jnp.float32)


def reorder(chosen, values):
    high, low = (
        lax.dot_general(
            chosen.astype(jnp.bfloat16),
            part,
            (((0,), (0,)), ((), ())),
            preferred_element_type=jnp.float32,
        )
        for part in split(values)
    )
    return high + low


def sector_part(z, coef, place):
    part = None
    for one in range(z.n_lon):
        first = one * z.spec_width
        first = first if first < KMAX else first - KMAX + HALF
        this = coef[:, first : first + z.spec_width]
        part = this if part is None else jnp.where(place == one, this, part)
    return part


def depths(z, depth_ref, row_ref):
    level = column_of(row_ref, LEVEL)[: z.own]
    depth = jnp.zeros_like(level)
    for lev in range(z.lev):
        depth = jnp.where(level == lev, depth_ref[lev], depth)
    return depth


def store_rims(z, ref, g, we, wn, last):
    edge = 2 * z.lev
    ref[:edge] = g[z.own - edge :] if last else g[:edge]
    ref[edge : edge + z.lev] = we[z.own - z.lev :] if last else we[: z.lev]
    ref[edge + z.lev :] = wn[z.own - z.lev :] if last else wn[: z.lev]


def east_shares_of(
    z, at, we_ref, wn_ref, g_ref, row_ref, phase_ref, basis_ref, out_ref, lhs_ref, share_ref,
    basis_here=None,
):
    inner, rows = slice(at.start // z.lev, at.stop // z.lev), at.stop - at.start
    g, we, wn = (ref[inner].reshape(rows, z.lon) for ref in (g_ref, we_ref, wn_ref))

    @pl.when(on_polar_band(z))
    def _():
        coef, sine = column_of(row_ref, EAST_COEF)[at], column_of(row_ref, SINE)[at]
        new = widen(z, we + CORIOLIS * sine * wn) - coef * east_diff(widen(z, g))
        tail = put_lane(new[:, z.ext - 128 :], 127, 0.0)
        new = jnp.concatenate([new[:, : z.ext - 128], tail], axis=1)
        forward_sums(
            z, new, basis_ref, phase_ref, lhs_ref, share_ref, slice(rows), basis_here=basis_here
        )
        cos, sin = phase_of(phase_ref, z.blocks)
        before = -coef * g[:, 0:1]
        share_ref[:rows, :HALF] += before * cos
        share_ref[:rows, HALF:] += before * sin
        pack(share_ref[...], out_ref)

    @pl.when(jnp.logical_not(on_polar_band(z)))
    def _():
        if basis_here is not None:
            basis_here()
        last = z.lon - 1
        columns = jnp.zeros((rows, 128), jnp.float32)
        edges = ((g, last - 1), (g, last), (we, last), (wn, last), (g, 0), (g, 1), (we, 0), (wn, 0))
        for n, (x, column) in enumerate(edges):
            columns = put_lane(columns, n, x[:, column : column + 1])
        out_ref[...] = jnp.zeros_like(out_ref)
        out_ref[:rows] = columns


def east_first(
    z, we_hbm, wn_hbm, g_hbm, row_hbm, phase_hbm, basis_hbm,
    share_ref, even_ref, odd_ref, we_ref, wn_ref, g_ref, row_ref, phase_ref, basis_ref, lhs_ref, sums_ref, sems,
):
    fields = ((g_hbm, g_ref), (we_hbm, we_ref), (wn_hbm, wn_ref))
    cut, rim = z.first // z.lev, z.lat - 2

    def copies(first_sem, pairs):
        return [pltpu.make_async_copy(*pair, sems.at[first_sem + n]) for n, pair in enumerate(pairs)]

    tables = copies(
        0,
        (
            (row_hbm.at[lax.axis_index("lat")], row_ref),
            (phase_hbm.at[lax.axis_index("lon")], phase_ref),
        ),
    )
    first = copies(2, [(a.at[:cut], b.at[:cut]) for a, b in fields])
    basis = copies(5, [(basis_hbm, basis_ref)])
    edge = copies(6, [(a.at[rim:], b.at[rim:]) for a, b in fields])
    between = copies(9, [(a.at[cut:rim], b.at[cut:rim]) for a, b in fields])
    for copy in first + tables + basis + edge:
        copy.start()
    for copy in first + tables:
        copy.wait()
    for copy in between:
        copy.start()

    def basis_here():
        for copy in basis + edge:
            copy.wait()

    east_shares_of(
        z, slice(0, z.first), we_ref, wn_ref, g_ref, row_ref, phase_ref, basis_ref, share_ref, lhs_ref,
        sums_ref, basis_here,
    )
    odd = lax.rem(lax.axis_index("lat"), 2) == 1
    last, flat = z.lat - 1, (z.lev, z.lon)
    far = (g_ref[last - 1], g_ref[last], we_ref[last], wn_ref[last])
    near = (g_ref[0], g_ref[1], we_ref[0], wn_ref[0])
    for n, (bottom, top) in enumerate(zip(far, near, strict=True)):
        at = slice(n * z.lev, (n + 1) * z.lev)
        even_ref[at] = jnp.where(odd, top, bottom).reshape(flat)
        odd_ref[at] = jnp.where(odd, bottom, top).reshape(flat)
    for copy in between:
        copy.wait()


def north_forward(
    z, we_ref, wn_ref, g_ref, even_ref, odd_ref, row_ref, phase_ref, basis_ref, kept_ref, slot_ref, *rest
):
    ahead_ref, rest_ref, north_ref, chosen_ref, sorted_ref, g_rows, lhs_ref, share_ref = rest
    edge, lev = 2 * z.lev, z.lev
    odd = lax.rem(lax.axis_index("lat"), 2) == 1
    below = jnp.where(odd, odd_ref[...], even_ref[...])
    above = jnp.where(odd, even_ref[...], odd_ref[...])
    coef, sine = north_factor(z), CORIOLIS * column_of(row_ref, SINE)
    own = flat_rows(z, g_ref)
    g_rows[: z.own] = own
    g_rows[z.own : z.own + lev] = below[:lev]
    g_rows[z.own + lev :] = above[lev:edge]
    g = g_rows[...]
    diff = (roll(g, -lev, 0) - roll(g, lev, 0))[: z.own]
    north_ref[: z.own] = flat_rows(z, wn_ref) - coef * diff - sine[: z.own] * flat_rows(z, we_ref)
    for at, diff, rim in (
        (z.own, below[lev:edge] - own[z.own - lev :], below),
        (z.own + lev, own[:lev] - above[:lev], above),
    ):
        we, wn = rim[edge : edge + lev], rim[edge + lev :]
        north_ref[at : at + lev] = wn - coef * diff - sine[at : at + lev] * we
    number = column_of(row_ref, NUMBER).astype(jnp.int32)
    kept = look_up(number, kept_ref)

    @pl.when(on_polar_band(z))
    def _():
        forward_sums(z, widen(z, north_ref[...]), basis_ref, phase_ref, lhs_ref, share_ref)
        share_ref[:, SPARE:HALF] = put_lane(share_ref[:, SPARE:HALF], KMAX - SPARE, kept)
        chosen = slot_order(z, number, row_ref, slot_ref)
        ordered = reorder(chosen, share_ref[...])
        pack(ordered[: z.ahead], ahead_ref)
        pack(ordered[z.ahead : z.rows], rest_ref)
        sorted_ref[...] = ordered[: z.rows, SPARE:HALF]
        chosen_ref[...] = chosen

    @pl.when(jnp.logical_not(on_polar_band(z)))
    def _():
        ahead_ref[...] = jnp.zeros_like(ahead_ref)
        chosen_ref[...] = jnp.zeros_like(chosen_ref)
        share_ref[...] = jnp.zeros_like(share_ref)
        rows = widen(z, north_ref[z.own :])
        forward_sums(z, rows, basis_ref, phase_ref, lhs_ref, share_ref, slice(z.own, z.rows))
        pack(share_ref[z.ahead :], rest_ref)
        sorted_ref[...] = jnp.broadcast_to(kept, sorted_ref.shape)


def arrival(arrived_ref, out_ref):
    out_ref[...] = arrived_ref[:8, :128]


def east_inverse(
    z, depth_ref, we_ref, wn_ref, g_ref, thick_ref, row_ref, phase_ref, kept_ref, chosen_ref, first_here,
    *rest,
):
    del first_here
    firsts, seconds, rest = rest[: z.n_lon], rest[z.n_lon : 2 * z.n_lon], rest[2 * z.n_lon :]
    basis_ref, final_ref, part_ref, keep_ref, send_ref, lhs_ref, rows_ref, sums_ref = rest
    coef, sine = column_of(row_ref, EAST_COEF)[: z.own], column_of(row_ref, SINE)[: z.own]

    @pl.when(on_polar_band(z))
    def _():
        number = column_of(row_ref, NUMBER)[: z.own].astype(jnp.int32)
        second = round_up(z.own - z.first, 8)
        sums_ref[: z.first] = unpack(sum(ref[...] for ref in firsts), z.first)
        sums_ref[z.first :] = unpack(sum(ref[...] for ref in seconds), second)[: z.own - z.first]
        waves = coefficients(z, sums_ref[...], look_up(number, kept_ref))
        part = sector_part(z, waves, lax.axis_index("lon"))
        ordered = reorder(chosen_ref[: z.own], part)
        send_ref[...] = ordered[: z.helped].reshape(send_ref.shape)
        keep_ref[...] = ordered[z.helped : 2 * z.helped].reshape(keep_ref.shape)
        inverse_rows(z, waves, basis_ref, phase_ref, lhs_ref, rows_ref)
        cos, sin = phase_of(phase_ref, z.blocks)
        before = jnp.sum(waves[:, :HALF] * cos + waves[:, HALF:] * sin, axis=1, keepdims=True)
        rows_ref[:, z.ext - 128 :] = put_lane(rows_ref[:, z.ext - 128 :], 127, before)

    @pl.when(jnp.logical_not(on_polar_band(z)))
    def _():
        send_ref[...] = jnp.zeros_like(send_ref)
        keep_ref[...] = jnp.zeros_like(keep_ref)
        left, right = (
            jnp.concatenate([firsts[n][: z.first], seconds[n][: z.own - z.first]], axis=0)
            for n in (1, -1)
        )
        at_right = z.lon - (z.ext - 128)

        def rimmed(ref, left_of, right_of):
            x = widen(z, flat_rows(z, ref))
            tail = x[:, z.ext - 128 :]
            for n, lane in enumerate(right_of):
                tail = put_lane(tail, at_right + n, right[:, lane : lane + 1])
            for n, lane in enumerate(left_of):
                tail = put_lane(tail, 127 - n, left[:, lane : lane + 1])
            return jnp.concatenate([x[:, : z.ext - 128], tail], axis=1)

        g = rimmed(g_ref, (1, 0), (4, 5))
        we, wn = rimmed(we_ref, (2,), (6,)), rimmed(wn_ref, (3,), (7,))
        rows_ref[...] = we - coef * east_diff(g) + CORIOLIS * sine * wn

    final = rows_ref[...]
    final_ref[...] = final[:, : z.lon].reshape(final_ref.shape)
    change = depths(z, depth_ref, row_ref) * coef * east_diff(final)[:, : z.lon]
    part_ref[...] = flat_rows(z, thick_ref) - change


def ahead_waves(z, shares, sorted_ref):
    sums = unpack(sum(ref[...] for ref in shares), z.ahead)
    return coefficients(z, sums, sorted_ref[: z.ahead, MORE : MORE + 1])


def send_spectra(z, east_ref, sorted_ref, *rest):
    shares, send_ref, waves_ref = rest[:-2], rest[-2], rest[-1]
    waves = ahead_waves(z, shares, sorted_ref)
    waves_ref[...] = waves
    part = sector_part(z, waves, lax.axis_index("lon"))
    send_ref[0] = east_ref[...]
    send_ref[1] = part[: z.helped].reshape(east_ref.shape)


def ahead_inverse(z, phase_ref, waves_ref, basis_ref, high_ref, low_ref, lhs_ref):
    @pl.when(on_polar_band(z))
    def _():
        inverse_split(z, waves_ref[...], basis_ref, phase_ref, lhs_ref, high_ref, low_ref, 0)


def north_inverse(
    z, active, depth_ref, north_ref, part_ref, row_ref, phase_ref, chosen_ref, sorted_ref, waves_ahead,
    high_ahead, low_ahead, *rest,
):
    shares, rest = rest[: z.n_lon], rest[z.n_lon :]
    basis_ref, final_ref, thick_ref, column_ref, keep_ref, lhs_ref, rows_ref, both_ref = rest

    @pl.when(active & on_polar_band(z))
    def _():
        more = z.ahead - 8
        sums = unpack(sum(ref[...] for ref in shares), z.rows - z.ahead)
        waves = coefficients(z, sums, sorted_ref[z.ahead :, MORE : MORE + 1])
        both = jnp.concatenate([waves_ahead[more:], waves], axis=0)
        part = sector_part(z, both, lax.axis_index("lon"))
        first = z.helped - more
        keep_ref[...] = part[first : first + z.helped].reshape(keep_ref.shape)
        both_ref[: z.ahead] = high_ahead[...]
        both_ref[z.mm_rows : z.mm_rows + z.ahead] = low_ahead[...]
        inverse_split(
            z, waves, basis_ref, phase_ref, lhs_ref, both_ref, both_ref, z.ahead, z.mm_rows
        )
        chosen = chosen_ref[:, : z.mm_rows].astype(jnp.bfloat16)
        rows_ref[...] = jnp.dot(
            jnp.concatenate([chosen, chosen], axis=1),
            both_ref[...],
            preferred_element_type=jnp.float32,
        )
        beyond = slice(z.own, z.rows)
        polar = column_of(row_ref, POLAR)[beyond] > 0.0
        rows_ref[beyond, : z.lon] = jnp.where(polar, rows_ref[beyond, : z.lon], north_ref[beyond])

    @pl.when(active & jnp.logical_not(on_polar_band(z)))
    def _():
        keep_ref[...] = jnp.zeros_like(keep_ref)
        beyond = slice(z.own, z.rows)
        at = slice(z.own - z.ahead, z.rows - z.ahead)
        sums = unpack(sum(ref[...] for ref in shares), z.rows - z.ahead)
        waves = coefficients(z, sums[at], sorted_ref[beyond, MORE : MORE + 1])
        inverse_rows(z, waves, basis_ref, phase_ref, lhs_ref, rows_ref, beyond)
        polar = column_of(row_ref, POLAR)[beyond] > 0.0
        rows_ref[beyond, : z.lon] = jnp.where(polar, rows_ref[beyond, : z.lon], north_ref[beyond])
        rows_ref[: z.own, : z.lon] = north_ref[: z.own]

    @pl.when(active)
    def _():
        final = rows_ref[:, : z.lon]
        final_ref[...] = final[: z.own].reshape(final_ref.shape)
        scaled = final * column_of(row_ref, COSINE)
        diff = (roll(scaled, -z.lev, 0) - roll(scaled, z.lev, 0))[: z.own]
        scale = depths(z, depth_ref, row_ref) * column_of(row_ref, NORTH_COEF)[: z.own]
        thick_ref[...] = (part_ref[...] - scale * diff).reshape(thick_ref.shape)
        column_ref[...] = sum(thick_ref[:, lev, :] for lev in range(z.lev))


def sends_column():
    return lax.axis_index("lev") > 0


def north_deeper(z, *refs):
    north_inverse(z, sends_column(), *refs)


def north_shallowest(z, east_keep, north_keep, arrived_ref, *rest):
    *refs, spectra_ref, column_ref, keep_ref, lhs_ref, rows_ref, both_ref = rest
    active = jnp.logical_not(sends_column())
    north_inverse(z, active, *refs, column_ref, keep_ref, lhs_ref, rows_ref, both_ref)

    @pl.when(sends_column())
    def _():
        keep_ref[...] = north_keep[...]

    polar = on_polar_band(z)
    spectra_ref[0] = jnp.where(polar, east_keep[...], arrived_ref[0])
    spectra_ref[1] = jnp.where(polar, keep_ref[...], arrived_ref[1])


def finish(z, surface_ref, *rest):
    deeper_fields, own_fields, deeper, outs = rest[:2], rest[2:4], rest[4 : 3 + z.n_lev], rest[3 + z.n_lev :]
    spectra, (final_out, thick_out, geo_out, spectra_out, geo_ref, sems) = outs[0], outs[1:]

    def store(fields):
        copies = [
            pltpu.make_async_copy(*pair, sems.at[n])
            for n, pair in enumerate(
                ((fields[0], final_out), (fields[1], thick_out), (spectra, spectra_out))
            )
        ]
        for copy in copies:
            copy.start()
        for n in range(z.cuts):
            at = slice(n * z.lat // z.cuts, (n + 1) * z.lat // z.cuts)
            column = sum(ref[at] for ref in deeper)
            for lev in reversed(range(z.lev)):
                column = column + fields[1][at, lev, :]
                geo_ref[at, lev, :] = surface_ref[at] + GRAVITY * column
            copies.append(pltpu.make_async_copy(geo_ref.at[at], geo_out.at[at], sems.at[3 + n]))
            copies[-1].start()
        for copy in copies:
            copy.wait()

    @pl.when(sends_column())
    def _():
        store(deeper_fields)

    @pl.when(jnp.logical_not(sends_column()))
    def _():
        store(own_fields)


def call(kernel, n_in, out_shape, scratch, micros, spaces=None, in_hbm=0, vmem=24):
    vmem_spec = pl.BlockSpec(memory_space=pltpu.VMEM)
    spaces = spaces or {}
    return pl.pallas_call(
        kernel,
        in_specs=[
            pl.BlockSpec(memory_space=spaces[n]) if n in spaces else vmem_spec for n in range(n_in)
        ],
        out_specs=[pl.BlockSpec(memory_space=pltpu.HBM)] * in_hbm
        + [vmem_spec] * (len(out_shape) - in_hbm),
        out_shape=[
            jax.ShapeDtypeStruct(s, jnp.float32) if isinstance(s, tuple) else s for s in out_shape
        ],
        scratch_shapes=scratch,
        compiler_params=pltpu.CompilerParams(vmem_limit_bytes=vmem * MIB),
        cost_estimate=pl.CostEstimate(
            flops=int(micros * 1.15e9), bytes_accessed=0, transcendentals=0
        ),
    )


def shifted(block, axis, distance):
    count = lax.axis_size(axis)
    return lax.ppermute(block, axis, [(i, (i + distance) % count) for i in range(count)])


def level_inside(x):
    return jnp.swapaxes(x, -3, -2)


def local(
    wind_east, wind_north, thickness, geopot, surface_geopot, mean_depth, kept_modes, slot_table
):
    z = Sizes(thickness.shape, {axis: lax.axis_size(axis) for axis in ("lat", "lon", "lev")})
    wind_east, wind_north, thickness, geopot = (
        level_inside(x) for x in (wind_east, wind_north, thickness, geopot)
    )
    field = (z.lat, z.lev, z.lon)
    forward, inverse = (jnp.asarray(x) for x in basis_tables(z))
    phase = jnp.asarray(phase_table(z))
    per_row = jnp.asarray(row_table(z))
    kept = kept_modes[None, :]
    slots = slot_table[None, :]
    payload = (z.rows, WIDE)
    rims = (4 * z.lev, z.lon)
    spec = (z.help, z.lev, z.spec_width)
    waves_lhs = pltpu.VMEM((z.ext // z.inverse_block * z.mm_rows, 3 * WIDE), jnp.bfloat16)

    row_shape, phase_shape = per_row.shape[1:], phase.shape[1:]
    pinned = [
        pltpu.with_memory_space_constraint(x, pltpu.HBM)
        for x in (wind_east, wind_north, geopot, per_row, phase, forward)
    ]
    columns_lhs = pltpu.VMEM((z.blocks * z.mm_rows, 3 * BLOCK), jnp.bfloat16)
    waves_lhs = pltpu.VMEM((z.ext // z.inverse_block * z.mm_rows, 3 * WIDE), jnp.bfloat16)

    share_first, to_even, to_odd, wind_east, wind_north, geopot, per_row, phase, forward = call(
        functools.partial(east_first, z),
        6,
        [(packed_rows(z.first), 128), rims, rims]
        + [pltpu.VMEM(s, jnp.float32) for s in (field, field, field, row_shape, phase_shape)]
        + [pltpu.VMEM(forward.shape, forward.dtype)],
        [
            columns_lhs,
            pltpu.VMEM((z.first, WIDE), jnp.float32),
            pltpu.SemaphoreType.DMA((12,)),
        ],
        1,
        {n: pltpu.HBM for n in range(6)},
    )(*pinned)
    second = round_up(z.own - z.first, 8)
    (share_second,) = call(
        functools.partial(east_shares_of, z, slice(z.first, z.own)),
        6,
        [(packed_rows(second), 128)],
        [columns_lhs, pltpu.VMEM((second, WIDE), jnp.float32)],
        0.18,
    )(wind_east, wind_north, geopot, per_row, phase, forward)
    east_firsts, east_seconds = (
        [x] + [shifted(x, "lon", s) for s in range(1, z.n_lon)] for x in (share_first, share_second)
    )
    met = []
    for start, rim in enumerate((to_even, to_odd)):
        pairs = [(i, i + 1) for i in range(start, z.n_lat - 1, 2)]
        met.append(lax.ppermute(rim, "lat", pairs + [(b, a) for a, b in pairs]))

    places = round_up(z.rows, 128)
    north_ahead, north_rest, north_new, chosen, kept_sorted = call(
        functools.partial(north_forward, z),
        10,
        [
            (packed_rows(z.ahead), 128),
            (packed_rows(z.rows - z.ahead), 128),
            (z.rows, z.lon),
            (z.rows, places),
            (z.rows, 128),
        ],
        [
            pltpu.VMEM((z.rows, z.lon), jnp.float32),
            columns_lhs,
            pltpu.VMEM((z.rows, WIDE), jnp.float32),
        ],
        0.8,
    )(
        wind_east, wind_north, geopot, *met, per_row, phase, forward, kept, slots
    )
    north_rests = [north_rest] + [shifted(north_rest, "lon", s) for s in range(1, z.n_lon)]
    polar_bands = [i for i in range(z.n_lat) if i < z.n_lat // 4 or i >= z.n_lat - z.n_lat // 4]
    north_aheads = [north_ahead]
    for distance in range(1, z.n_lon):
        route = [
            (band * z.n_lon + lon, band * z.n_lon + (lon + distance) % z.n_lon)
            for band in polar_bands
            for lon in range(z.n_lon)
        ]
        north_aheads.append(lax.ppermute(north_ahead, ("lat", "lon"), route))

    (first_here,) = call(arrival, 1, [(8, 128)], [], 0.95)(east_firsts[1])
    east_final, thick_part, east_keep, east_send = call(
        functools.partial(east_inverse, z),
        11 + 2 * z.n_lon,
        [field, (z.own, z.lon), spec, spec],
        [
            waves_lhs,
            pltpu.VMEM((z.own, z.ext), jnp.float32),
            pltpu.VMEM((z.own, WIDE), jnp.float32),
        ],
        1,
        {0: pltpu.SMEM},
    )(
        mean_depth, wind_east, wind_north, geopot, thickness, per_row, phase, kept, chosen,
        first_here, *east_firsts, *east_seconds, inverse,
    )

    to_helper, waves_ahead = call(
        functools.partial(send_spectra, z), 2 + z.n_lon, [(2, *spec), (z.ahead, WIDE)], [], 0.1
    )(east_send, kept_sorted, *north_aheads)
    arrived = lax.ppermute(
        to_helper, "lat", [(i, (i + z.half_axis) % z.n_lat) for i in polar_bands]
    )

    ahead_rows = jax.ShapeDtypeStruct((z.ahead, z.ext), jnp.bfloat16)
    ahead_high, ahead_low = call(
        functools.partial(ahead_inverse, z),
        3,
        [ahead_rows] * 2,
        [waves_lhs],
        0.5,
    )(phase, waves_ahead, inverse)

    operands = (
        mean_depth, north_new, thick_part, per_row, phase, chosen, kept_sorted, waves_ahead,
        ahead_high, ahead_low, *north_rests, inverse,
    )
    in_vmem = pltpu.VMEM(field, jnp.float32)
    scratch = [waves_lhs, pltpu.VMEM((z.rows, z.ext), jnp.float32)]
    scratch += [pltpu.VMEM((2 * z.mm_rows, z.ext), jnp.bfloat16)]
    final_deeper, thick_deeper, column, north_keep = call(
        functools.partial(north_deeper, z),
        len(operands),
        [in_vmem, in_vmem, (z.lat, z.lon), spec],
        scratch,
        2,
        {0: pltpu.SMEM},
    )(*operands)
    deeper = [
        lax.ppermute(column, "lev", [(i, i - distance) for i in range(distance, z.n_lev)])
        for distance in range(1, z.n_lev)
    ]
    final_own, thick_own, joined = call(
        functools.partial(north_shallowest, z),
        3 + len(operands),
        [in_vmem, in_vmem, pltpu.VMEM((2, *spec), jnp.float32)],
        [pltpu.VMEM((z.lat, z.lon), jnp.float32), pltpu.VMEM(spec, jnp.float32)] + scratch,
        3.2,
        {3: pltpu.SMEM},
    )(east_keep, north_keep, arrived, *operands)
    north_final, thick_new, geo_new, spectra = call(
        functools.partial(finish, z),
        6 + len(deeper),
        [pltpu.HBM(field, jnp.float32)] * 3 + [pltpu.HBM((2, *spec), jnp.float32)],
        [pltpu.VMEM(field, jnp.float32), pltpu.SemaphoreType.DMA((3 + z.cuts,))],
        1,
        in_hbm=4,
    )(surface_geopot, final_deeper, thick_deeper, final_own, thick_own, *deeper, joined)
    return tuple(level_inside(x) for x in (east_final, north_final, thick_new, geo_new, spectra))


def solution(mesh):
    field = P(("members", "lev"), "lat", "lon")
    return jax.shard_map(
        local,
        mesh=mesh,
        in_specs=(field, field, field, field, P("lat", "lon"), P("lev"), P(), P()),
        out_specs=(field, field, field, field, P(None, ("members", "lev"), "lat", "lon")),
        check_vma=False,
    )
```

```python
import functools
import math

import jax
import jax.numpy as jnp
import numpy as np
from jax import lax
from jax.experimental import pallas as pl
from jax.experimental.pallas import tpu as pltpu
from jax.sharding import PartitionSpec as P

KMAX = 360
HALF = 384
WIDE = 2 * HALF
SPARE = HALF - 128
MORE = KMAX - SPARE
MOVED = 128 - MORE
LEFT = MORE - MOVED
BLOCK = 256
INVERSE_BLOCK = 512

STEP_FACTOR = 0.15
CORIOLIS = 0.2
GRAVITY = 0.25

MIB = 1024 * 1024

EAST_COEF, SINE, COSINE, NORTH_COEF, LEVEL, POLAR, NUMBER, OWN = range(8)


def round_up(value, step):
    return -(-value // step) * step


class Sizes:
    def __init__(self, shape, counts):
        self.lev, self.lat, self.lon = shape
        self.n_lat, self.n_lon, self.n_lev = counts["lat"], counts["lon"], counts["lev"]
        self.nlat, self.nlon = self.lat * self.n_lat, self.lon * self.n_lon
        self.polar = self.nlat // 4
        self.help = self.lat // 2
        self.half_axis = self.n_lat // 2
        self.own = self.lat * self.lev
        self.rows = self.own + 2 * self.lev
        assert self.rows % 8 == 0
        self.mm_rows = round_up(self.rows, 16)
        self.ext = round_up(self.lon + 4, BLOCK)
        self.blocks = self.ext // BLOCK
        self.inverse_block = min(INVERSE_BLOCK, self.ext)
        assert self.ext % self.inverse_block == 0
        self.spec_width = 2 * KMAX // self.n_lon
        self.helped = self.help * self.lev
        self.ahead = round_up(self.helped, 16)
        self.cuts = 2
        self.first = min(round_up(self.own // 2, 8 * self.lev), self.own)


def high_low(x):
    x = x.astype(np.float32)
    high = x.astype(jnp.bfloat16)
    return high, (x - high.astype(np.float32)).astype(jnp.bfloat16)


def basis_tables(z):
    k = np.arange(KMAX)
    angle = (np.arange(z.inverse_block)[:, None] * k[None, :] % z.nlon) * (2.0 * np.pi / z.nlon)
    full = np.zeros((z.inverse_block, WIDE))
    full[:, :KMAX] = np.cos(angle)
    full[:, HALF : HALF + KMAX] = np.sin(angle)
    high, low = high_low(full)
    forward = np.concatenate([high[:BLOCK], high[:BLOCK], low[:BLOCK]], axis=0)
    inverse = np.concatenate([high.T, high.T, low.T], axis=0)
    return forward, inverse


def phase_table(z):
    k = np.arange(KMAX)
    table = np.zeros((z.n_lon, round_up(2 * z.blocks + 2, 8), HALF), np.float32)
    for place in range(z.n_lon):
        for n, column in enumerate([*range(0, z.ext, BLOCK), -1]):
            angle = ((place * z.lon + column) * k % z.nlon) * (2.0 * np.pi / z.nlon)
            table[place, 2 * n, :KMAX] = np.cos(angle)
            table[place, 2 * n + 1, :KMAX] = np.sin(angle)
    return table


def row_table(z):
    lam_step = np.float32(2.0 * math.pi / z.nlon)
    phi_step = np.float32(math.pi / z.nlat)
    latitude = np.float32(-0.5 * math.pi) + (
        np.arange(z.nlat, dtype=np.float32) + np.float32(0.5)
    ) * phi_step
    cosine = np.cos(latitude.astype(np.float64)).astype(np.float32)
    sine = np.sin(latitude.astype(np.float64)).astype(np.float32)
    north_coef = np.float32(STEP_FACTOR) * lam_step / phi_step
    table = np.zeros((z.n_lat, z.rows, 8), np.float32)
    for place in range(z.n_lat):
        for flat in range(z.rows):
            inner, level = flat // z.lev, flat % z.lev
            inner = -1 if inner == z.lat + 1 else inner
            row = place * z.lat + inner
            one = table[place, flat]
            one[LEVEL], one[NUMBER] = level, -1
            one[OWN] = 0 <= inner < z.lat
            if 0 <= row < z.nlat:
                one[EAST_COEF] = np.float32(STEP_FACTOR) / cosine[row]
                one[SINE], one[COSINE] = sine[row], cosine[row]
                one[NORTH_COEF] = north_coef / cosine[row]
                if row < z.polar:
                    one[POLAR], one[NUMBER] = 1, row
                elif row >= z.nlat - z.polar:
                    one[POLAR], one[NUMBER] = 1, row - (z.nlat - 2 * z.polar)
    return table


def on_polar_band(z):
    lat_index = lax.axis_index("lat")
    return (lat_index < z.n_lat // 4) | (lat_index >= z.n_lat - z.n_lat // 4)


def split(x):
    high = x.astype(jnp.bfloat16)
    return high, (x - high.astype(jnp.float32)).astype(jnp.bfloat16)


def store_split(lhs_ref, first_row, x):
    rows, width = x.shape
    high, low = split(x)
    at = slice(first_row, first_row + rows)
    lhs_ref[at, :width] = high
    lhs_ref[at, width : 2 * width] = low
    lhs_ref[at, 2 * width :] = high


def pad_rows(x, rows):
    if x.shape[0] == rows:
        return x
    return jnp.concatenate([x, jnp.zeros((rows - x.shape[0], x.shape[1]), x.dtype)], axis=0)


def phase_of(phase_ref, n):
    return phase_ref[2 * n : 2 * n + 1], phase_ref[2 * n + 1 : 2 * n + 2]


def packed_rows(rows):
    return 5 * rows + round_up(-(-rows // 2), 8) + 16


def lanes_of(x):
    return lax.broadcasted_iota(jnp.int32, x.shape, 1)


def pack(x, out_ref):
    rows = x.shape[0]
    half = round_up(-(-rows // 2), 8)
    tiles = [x[:, n : n + 128] for n in range(0, WIDE, 128)]
    left = tiles[5]
    lane = lanes_of(left)
    tiles[2] = jnp.where(lane < MORE, tiles[2], roll(left, MOVED, 1))
    for n in range(5):
        out_ref[n * rows : (n + 1) * rows] = tiles[n]
    lower = pad_rows(left[half:], half)
    out_ref[5 * rows : 5 * rows + half] = jnp.where(lane[:half] < 64, left[:half], roll(lower, 64, 1))
    out_ref[5 * rows + half :] = pad_rows(roll(left, -64, 1), 128).T[:16]


def unpack(x, rows):
    half = round_up(-(-rows // 2), 8)
    tiles = [x[n * rows : (n + 1) * rows] for n in range(5)]
    pairs = x[5 * rows : 5 * rows + half]
    ends = pad_rows(x[5 * rows + half :], 128).T[:rows]
    left = jnp.concatenate([pairs, roll(pairs, 64, 1)[: rows - half]], axis=0)
    lane = lanes_of(left)
    left = jnp.where(lane < 64, left, jnp.where(lane < LEFT, roll(ends, 64, 1), roll(tiles[2], -MOVED, 1)))
    return jnp.concatenate([*tiles, left], axis=1)


def forward_sums(
    z, x, basis_ref, phase_ref, lhs_ref, out_ref, at=slice(None), basis_here=None
):
    count = round_up(x.shape[0], 16)
    for block in range(z.blocks):
        part = pad_rows(x[:, block * BLOCK : (block + 1) * BLOCK], count)
        store_split(lhs_ref, block * count, part)
    lhs = lhs_ref[: z.blocks * count]
    if basis_here is not None:
        basis_here()
    sums = jnp.dot(lhs, basis_ref[...], preferred_element_type=jnp.float32)
    real = imag = None
    for block in range(z.blocks):
        cos, sin = phase_of(phase_ref, block)
        part = sums[block * count : block * count + x.shape[0]]
        a, b = part[:, :HALF], part[:, HALF:]
        more_real, more_imag = a * cos - b * sin, a * sin + b * cos
        real = more_real if real is None else real + more_real
        imag = more_imag if imag is None else imag + more_imag
    out_ref[at, :HALF] = real
    out_ref[at, HALF:] = imag


def inverse_rows(z, coef, basis_ref, phase_ref, lhs_ref, out_ref, at=slice(None)):
    a, b = coef[:, :HALF], coef[:, HALF:]
    count, width = round_up(coef.shape[0], 16), z.inverse_block
    blocks = range(z.ext // width)
    for block in blocks:
        cos, sin = phase_of(phase_ref, block * width // BLOCK)
        turned = jnp.concatenate([a * cos + b * sin, b * cos - a * sin], axis=1)
        store_split(lhs_ref, block * count, pad_rows(turned, count))
    lhs = lhs_ref[: len(blocks) * count]
    rows = jnp.dot(lhs, basis_ref[...], preferred_element_type=jnp.float32)
    for block in blocks:
        out_ref[at, block * width : (block + 1) * width] = rows[
            block * count : block * count + coef.shape[0]
        ]


def roll(x, shift, axis):
    return pltpu.roll(x, shift % x.shape[axis], axis)


def east_diff(x):
    return roll(x, -1, 1) - roll(x, 1, 1)


def flat_rows(z, ref):
    return ref[...].reshape(z.own, ref.shape[2])


def widen(z, x):
    return jnp.concatenate([x, jnp.zeros((x.shape[0], z.ext - x.shape[1]), x.dtype)], axis=1)


def put_lane(x, at, column):
    lane = lax.broadcasted_iota(jnp.int32, x.shape, 1)
    return jnp.where(lane == at, column, x)


def column_of(row_ref, which):
    return row_ref[:, which : which + 1]


def north_factor(z):
    return STEP_FACTOR * (2.0 * math.pi / z.nlon) / (math.pi / z.nlat)


def look_up(number, table_ref):
    table = table_ref[...].astype(jnp.float32)
    lane = lax.broadcasted_iota(jnp.int32, (number.shape[0], table.shape[1]), 1)
    return jnp.sum(jnp.where(lane == number, table, 0.0), axis=1, keepdims=True)


def coefficients(z, sums, kept):
    lane = lax.broadcasted_iota(jnp.int32, (1, WIDE), 1)
    k = jnp.where(lane < HALF, lane, lane - HALF)
    weight = jnp.where(k == 0, 1.0 / z.nlon, 2.0 / z.nlon).astype(jnp.float32)
    keep = (k.astype(jnp.float32) < kept) & (k < KMAX)
    return jnp.where(keep, sums * weight, 0.0)


def slot_order(z, number, row_ref, slot_ref):
    lat_index = lax.axis_index("lat")
    slot = look_up(number, slot_ref).astype(jnp.int32)
    theirs = slot - lax.rem(lat_index + z.half_axis, z.n_lat) * z.help
    mine = slot - lat_index * z.help
    level = column_of(row_ref, LEVEL).astype(jnp.int32)
    flat = lax.broadcasted_iota(jnp.int32, slot.shape, 0)
    place = jnp.where((mine >= 0) & (mine < z.help), z.helped + mine * z.lev + level, -1)
    place = jnp.where((theirs >= 0) & (theirs < z.help), theirs * z.lev + level, place)
    place = jnp.where(number >= 0, place, -1)
    place = jnp.where(flat < z.own, place, flat)
    lane = lax.broadcasted_iota(jnp.int32, (z.rows, round_up(z.rows, 128)), 1)
    return (lane == place).astype(jnp.float32)


def reorder(chosen, values):
    high, low = (
        lax.dot_general(
            chosen.astype(jnp.bfloat16),
            part,
            (((0,), (0,)), ((), ())),
            preferred_element_type=jnp.float32,
        )
        for part in split(values)
    )
    return high + low


def sector_part(z, coef, place):
    part = None
    for one in range(z.n_lon):
        first = one * z.spec_width
        first = first if first < KMAX else first - KMAX + HALF
        this = coef[:, first : first + z.spec_width]
        part = this if part is None else jnp.where(place == one, this, part)
    return part


def depths(z, depth_ref, row_ref):
    level = column_of(row_ref, LEVEL)[: z.own]
    depth = jnp.zeros_like(level)
    for lev in range(z.lev):
        depth = jnp.where(level == lev, depth_ref[lev], depth)
    return depth


def store_rims(z, ref, g, we, wn, last):
    edge = 2 * z.lev
    ref[:edge] = g[z.own - edge :] if last else g[:edge]
    ref[edge : edge + z.lev] = we[z.own - z.lev :] if last else we[: z.lev]
    ref[edge + z.lev :] = wn[z.own - z.lev :] if last else wn[: z.lev]


def east_shares_of(
    z, at, we_ref, wn_ref, g_ref, row_ref, phase_ref, basis_ref, out_ref, lhs_ref, share_ref,
    basis_here=None,
):
    inner, rows = slice(at.start // z.lev, at.stop // z.lev), at.stop - at.start
    g, we, wn = (ref[inner].reshape(rows, z.lon) for ref in (g_ref, we_ref, wn_ref))

    @pl.when(on_polar_band(z))
    def _():
        coef, sine = column_of(row_ref, EAST_COEF)[at], column_of(row_ref, SINE)[at]
        new = widen(z, we + CORIOLIS * sine * wn) - coef * east_diff(widen(z, g))
        tail = put_lane(new[:, z.ext - 128 :], 127, 0.0)
        new = jnp.concatenate([new[:, : z.ext - 128], tail], axis=1)
        forward_sums(
            z, new, basis_ref, phase_ref, lhs_ref, share_ref, slice(rows), basis_here=basis_here
        )
        cos, sin = phase_of(phase_ref, z.blocks)
        before = -coef * g[:, 0:1]
        share_ref[:rows, :HALF] += before * cos
        share_ref[:rows, HALF:] += before * sin
        pack(share_ref[...], out_ref)

    @pl.when(jnp.logical_not(on_polar_band(z)))
    def _():
        if basis_here is not None:
            basis_here()
        last = z.lon - 1
        columns = jnp.zeros((rows, 128), jnp.float32)
        edges = ((g, last - 1), (g, last), (we, last), (wn, last), (g, 0), (g, 1), (we, 0), (wn, 0))
        for n, (x, column) in enumerate(edges):
            columns = put_lane(columns, n, x[:, column : column + 1])
        out_ref[...] = jnp.zeros_like(out_ref)
        out_ref[:rows] = columns


def east_first(
    z, we_hbm, wn_hbm, g_hbm, row_hbm, phase_hbm, basis_hbm,
    share_ref, even_ref, odd_ref, we_ref, wn_ref, g_ref, row_ref, phase_ref, basis_ref, lhs_ref, sums_ref, sems,
):
    fields = ((g_hbm, g_ref), (we_hbm, we_ref), (wn_hbm, wn_ref))
    cut, rim = z.first // z.lev, z.lat - 2

    def copies(first_sem, pairs):
        return [pltpu.make_async_copy(*pair, sems.at[first_sem + n]) for n, pair in enumerate(pairs)]

    tables = copies(
        0,
        (
            (row_hbm.at[lax.axis_index("lat")], row_ref),
            (phase_hbm.at[lax.axis_index("lon")], phase_ref),
        ),
    )
    first = copies(2, [(a.at[:cut], b.at[:cut]) for a, b in fields])
    basis = copies(5, [(basis_hbm, basis_ref)])
    edge = copies(6, [(a.at[rim:], b.at[rim:]) for a, b in fields])
    between = copies(9, [(a.at[cut:rim], b.at[cut:rim]) for a, b in fields])
    for copy in first + tables + basis + edge:
        copy.start()
    for copy in first + tables:
        copy.wait()
    for copy in between:
        copy.start()

    def basis_here():
        for copy in basis + edge:
            copy.wait()

    east_shares_of(
        z, slice(0, z.first), we_ref, wn_ref, g_ref, row_ref, phase_ref, basis_ref, share_ref, lhs_ref,
        sums_ref, basis_here,
    )
    odd = lax.rem(lax.axis_index("lat"), 2) == 1
    last, flat = z.lat - 1, (z.lev, z.lon)
    far = (g_ref[last - 1], g_ref[last], we_ref[last], wn_ref[last])
    near = (g_ref[0], g_ref[1], we_ref[0], wn_ref[0])
    for n, (bottom, top) in enumerate(zip(far, near, strict=True)):
        at = slice(n * z.lev, (n + 1) * z.lev)
        even_ref[at] = jnp.where(odd, top, bottom).reshape(flat)
        odd_ref[at] = jnp.where(odd, bottom, top).reshape(flat)
    for copy in between:
        copy.wait()


def north_forward(
    z, we_ref, wn_ref, g_ref, even_ref, odd_ref, row_ref, phase_ref, basis_ref, kept_ref, slot_ref, *rest
):
    ahead_ref, rest_ref, north_ref, chosen_ref, sorted_ref, g_rows, lhs_ref, share_ref = rest
    edge, lev = 2 * z.lev, z.lev
    odd = lax.rem(lax.axis_index("lat"), 2) == 1
    below = jnp.where(odd, odd_ref[...], even_ref[...])
    above = jnp.where(odd, even_ref[...], odd_ref[...])
    coef, sine = north_factor(z), CORIOLIS * column_of(row_ref, SINE)
    own = flat_rows(z, g_ref)
    g_rows[: z.own] = own
    g_rows[z.own : z.own + lev] = below[:lev]
    g_rows[z.own + lev :] = above[lev:edge]
    g = g_rows[...]
    diff = (roll(g, -lev, 0) - roll(g, lev, 0))[: z.own]
    north_ref[: z.own] = flat_rows(z, wn_ref) - coef * diff - sine[: z.own] * flat_rows(z, we_ref)
    for at, diff, rim in (
        (z.own, below[lev:edge] - own[z.own - lev :], below),
        (z.own + lev, own[:lev] - above[:lev], above),
    ):
        we, wn = rim[edge : edge + lev], rim[edge + lev :]
        north_ref[at : at + lev] = wn - coef * diff - sine[at : at + lev] * we
    number = column_of(row_ref, NUMBER).astype(jnp.int32)
    kept = look_up(number, kept_ref)

    @pl.when(on_polar_band(z))
    def _():
        forward_sums(z, widen(z, north_ref[...]), basis_ref, phase_ref, lhs_ref, share_ref)
        share_ref[:, SPARE:HALF] = put_lane(share_ref[:, SPARE:HALF], KMAX - SPARE, kept)
        chosen = slot_order(z, number, row_ref, slot_ref)
        ordered = reorder(chosen, share_ref[...])
        pack(ordered[: z.ahead], ahead_ref)
        pack(ordered[z.ahead : z.rows], rest_ref)
        sorted_ref[...] = ordered[: z.rows, SPARE:HALF]
        chosen_ref[...] = chosen

    @pl.when(jnp.logical_not(on_polar_band(z)))
    def _():
        ahead_ref[...] = jnp.zeros_like(ahead_ref)
        chosen_ref[...] = jnp.zeros_like(chosen_ref)
        share_ref[...] = jnp.zeros_like(share_ref)
        rows = widen(z, north_ref[z.own :])
        forward_sums(z, rows, basis_ref, phase_ref, lhs_ref, share_ref, slice(z.own, z.rows))
        pack(share_ref[z.ahead :], rest_ref)
        sorted_ref[...] = jnp.broadcast_to(kept, sorted_ref.shape)


def arrival(arrived_ref, out_ref):
    out_ref[...] = arrived_ref[:8, :128]


def east_inverse(
    z, depth_ref, we_ref, wn_ref, g_ref, thick_ref, row_ref, phase_ref, kept_ref, chosen_ref, first_here,
    *rest,
):
    del first_here
    firsts, seconds, rest = rest[: z.n_lon], rest[z.n_lon : 2 * z.n_lon], rest[2 * z.n_lon :]
    basis_ref, final_ref, part_ref, keep_ref, send_ref, lhs_ref, rows_ref, sums_ref = rest
    coef, sine = column_of(row_ref, EAST_COEF)[: z.own], column_of(row_ref, SINE)[: z.own]

    @pl.when(on_polar_band(z))
    def _():
        number = column_of(row_ref, NUMBER)[: z.own].astype(jnp.int32)
        second = round_up(z.own - z.first, 8)
        sums_ref[: z.first] = unpack(sum(ref[...] for ref in firsts), z.first)
        sums_ref[z.first :] = unpack(sum(ref[...] for ref in seconds), second)[: z.own - z.first]
        waves = coefficients(z, sums_ref[...], look_up(number, kept_ref))
        part = sector_part(z, waves, lax.axis_index("lon"))
        ordered = reorder(chosen_ref[: z.own], part)
        send_ref[...] = ordered[: z.helped].reshape(send_ref.shape)
        keep_ref[...] = ordered[z.helped : 2 * z.helped].reshape(keep_ref.shape)
        inverse_rows(z, waves, basis_ref, phase_ref, lhs_ref, rows_ref)
        cos, sin = phase_of(phase_ref, z.blocks)
        before = jnp.sum(waves[:, :HALF] * cos + waves[:, HALF:] * sin, axis=1, keepdims=True)
        rows_ref[:, z.ext - 128 :] = put_lane(rows_ref[:, z.ext - 128 :], 127, before)

    @pl.when(jnp.logical_not(on_polar_band(z)))
    def _():
        send_ref[...] = jnp.zeros_like(send_ref)
        keep_ref[...] = jnp.zeros_like(keep_ref)
        left, right = (
            jnp.concatenate([firsts[n][: z.first], seconds[n][: z.own - z.first]], axis=0)
            for n in (1, -1)
        )
        at_right = z.lon - (z.ext - 128)

        def rimmed(ref, left_of, right_of):
            x = widen(z, flat_rows(z, ref))
            tail = x[:, z.ext - 128 :]
            for n, lane in enumerate(right_of):
                tail = put_lane(tail, at_right + n, right[:, lane : lane + 1])
            for n, lane in enumerate(left_of):
                tail = put_lane(tail, 127 - n, left[:, lane : lane + 1])
            return jnp.concatenate([x[:, : z.ext - 128], tail], axis=1)

        g = rimmed(g_ref, (1, 0), (4, 5))
        we, wn = rimmed(we_ref, (2,), (6,)), rimmed(wn_ref, (3,), (7,))
        rows_ref[...] = we - coef * east_diff(g) + CORIOLIS * sine * wn

    final = rows_ref[...]
    final_ref[...] = final[:, : z.lon].reshape(final_ref.shape)
    change = depths(z, depth_ref, row_ref) * coef * east_diff(final)[:, : z.lon]
    part_ref[...] = flat_rows(z, thick_ref) - change


def ahead_waves(z, shares, sorted_ref):
    sums = unpack(sum(ref[...] for ref in shares), z.ahead)
    return coefficients(z, sums, sorted_ref[: z.ahead, MORE : MORE + 1])


def send_spectra(z, east_ref, sorted_ref, *rest):
    shares, send_ref, waves_ref = rest[:-2], rest[-2], rest[-1]
    waves = ahead_waves(z, shares, sorted_ref)
    waves_ref[...] = waves
    part = sector_part(z, waves, lax.axis_index("lon"))
    send_ref[0] = east_ref[...]
    send_ref[1] = part[: z.helped].reshape(east_ref.shape)


def ahead_inverse(z, phase_ref, waves_ref, basis_ref, high_ref, low_ref, lhs_ref, rows_ref):
    @pl.when(on_polar_band(z))
    def _():
        inverse_rows(z, waves_ref[...], basis_ref, phase_ref, lhs_ref, rows_ref)
        high_ref[...], low_ref[...] = split(rows_ref[...])


def north_inverse(
    z, active, depth_ref, north_ref, part_ref, row_ref, phase_ref, chosen_ref, sorted_ref, waves_ahead,
    high_ahead, low_ahead, *rest,
):
    shares, rest = rest[: z.n_lon], rest[z.n_lon :]
    basis_ref, final_ref, thick_ref, column_ref, keep_ref, lhs_ref, rows_ref, high_ref, low_ref = rest

    @pl.when(active & on_polar_band(z))
    def _():
        more = z.ahead - 8
        sums = unpack(sum(ref[...] for ref in shares), z.rows - z.ahead)
        waves = coefficients(z, sums, sorted_ref[z.ahead :, MORE : MORE + 1])
        both = jnp.concatenate([waves_ahead[more:], waves], axis=0)
        part = sector_part(z, both, lax.axis_index("lon"))
        first = z.helped - more
        keep_ref[...] = part[first : first + z.helped].reshape(keep_ref.shape)
        inverse_rows(z, waves, basis_ref, phase_ref, lhs_ref, rows_ref, slice(z.rows - z.ahead))
        count = high_ref.shape[0] - z.ahead
        rest_high, rest_low = split(pad_rows(rows_ref[: z.rows - z.ahead], count))
        high_ref[: z.ahead], low_ref[: z.ahead] = high_ahead[...], low_ahead[...]
        high_ref[z.ahead :], low_ref[z.ahead :] = rest_high, rest_low
        chosen = chosen_ref[:, : z.mm_rows].astype(jnp.bfloat16)
        rows_ref[...] = jnp.dot(
            chosen, high_ref[...], preferred_element_type=jnp.float32
        ) + jnp.dot(chosen, low_ref[...], preferred_element_type=jnp.float32)
        beyond = slice(z.own, z.rows)
        polar = column_of(row_ref, POLAR)[beyond] > 0.0
        rows_ref[beyond, : z.lon] = jnp.where(polar, rows_ref[beyond, : z.lon], north_ref[beyond])

    @pl.when(active & jnp.logical_not(on_polar_band(z)))
    def _():
        keep_ref[...] = jnp.zeros_like(keep_ref)
        beyond = slice(z.own, z.rows)
        at = slice(z.own - z.ahead, z.rows - z.ahead)
        sums = unpack(sum(ref[...] for ref in shares), z.rows - z.ahead)
        waves = coefficients(z, sums[at], sorted_ref[beyond, MORE : MORE + 1])
        inverse_rows(z, waves, basis_ref, phase_ref, lhs_ref, rows_ref, beyond)
        polar = column_of(row_ref, POLAR)[beyond] > 0.0
        rows_ref[beyond, : z.lon] = jnp.where(polar, rows_ref[beyond, : z.lon], north_ref[beyond])
        rows_ref[: z.own, : z.lon] = north_ref[: z.own]

    @pl.when(active)
    def _():
        final = rows_ref[:, : z.lon]
        final_ref[...] = final[: z.own].reshape(final_ref.shape)
        scaled = final * column_of(row_ref, COSINE)
        diff = (roll(scaled, -z.lev, 0) - roll(scaled, z.lev, 0))[: z.own]
        scale = depths(z, depth_ref, row_ref) * column_of(row_ref, NORTH_COEF)[: z.own]
        thick_ref[...] = (part_ref[...] - scale * diff).reshape(thick_ref.shape)
        column_ref[...] = sum(thick_ref[:, lev, :] for lev in range(z.lev))


def sends_column():
    return lax.axis_index("lev") > 0


def north_deeper(z, *refs):
    north_inverse(z, sends_column(), *refs)


def north_shallowest(z, east_keep, north_keep, arrived_ref, *rest):
    *refs, spectra_ref, column_ref, keep_ref, lhs_ref, rows_ref, high_ref, low_ref = rest
    active = jnp.logical_not(sends_column())
    north_inverse(z, active, *refs, column_ref, keep_ref, lhs_ref, rows_ref, high_ref, low_ref)

    @pl.when(sends_column())
    def _():
        keep_ref[...] = north_keep[...]

    polar = on_polar_band(z)
    spectra_ref[0] = jnp.where(polar, east_keep[...], arrived_ref[0])
    spectra_ref[1] = jnp.where(polar, keep_ref[...], arrived_ref[1])


def finish(z, surface_ref, *rest):
    deeper_fields, own_fields, deeper, outs = rest[:2], rest[2:4], rest[4 : 3 + z.n_lev], rest[3 + z.n_lev :]
    spectra, (final_out, thick_out, geo_out, spectra_out, geo_ref, sems) = outs[0], outs[1:]

    def store(fields):
        copies = [
            pltpu.make_async_copy(*pair, sems.at[n])
            for n, pair in enumerate(
                ((fields[0], final_out), (fields[1], thick_out), (spectra, spectra_out))
            )
        ]
        for copy in copies:
            copy.start()
        for n in range(z.cuts):
            at = slice(n * z.lat // z.cuts, (n + 1) * z.lat // z.cuts)
            column = sum(ref[at] for ref in deeper)
            for lev in reversed(range(z.lev)):
                column = column + fields[1][at, lev, :]
                geo_ref[at, lev, :] = surface_ref[at] + GRAVITY * column
            copies.append(pltpu.make_async_copy(geo_ref.at[at], geo_out.at[at], sems.at[3 + n]))
            copies[-1].start()
        for copy in copies:
            copy.wait()

    @pl.when(sends_column())
    def _():
        store(deeper_fields)

    @pl.when(jnp.logical_not(sends_column()))
    def _():
        store(own_fields)


def call(kernel, n_in, out_shape, scratch, micros, spaces=None, in_hbm=0, vmem=24):
    vmem_spec = pl.BlockSpec(memory_space=pltpu.VMEM)
    spaces = spaces or {}
    return pl.pallas_call(
        kernel,
        in_specs=[
            pl.BlockSpec(memory_space=spaces[n]) if n in spaces else vmem_spec for n in range(n_in)
        ],
        out_specs=[pl.BlockSpec(memory_space=pltpu.HBM)] * in_hbm
        + [vmem_spec] * (len(out_shape) - in_hbm),
        out_shape=[
            jax.ShapeDtypeStruct(s, jnp.float32) if isinstance(s, tuple) else s for s in out_shape
        ],
        scratch_shapes=scratch,
        compiler_params=pltpu.CompilerParams(vmem_limit_bytes=vmem * MIB),
        cost_estimate=pl.CostEstimate(
            flops=int(micros * 1.15e9), bytes_accessed=0, transcendentals=0
        ),
    )


def shifted(block, axis, distance):
    count = lax.axis_size(axis)
    return lax.ppermute(block, axis, [(i, (i + distance) % count) for i in range(count)])


def level_inside(x):
    return jnp.swapaxes(x, -3, -2)


def local(
    wind_east, wind_north, thickness, geopot, surface_geopot, mean_depth, kept_modes, slot_table
):
    z = Sizes(thickness.shape, {axis: lax.axis_size(axis) for axis in ("lat", "lon", "lev")})
    wind_east, wind_north, thickness, geopot = (
        level_inside(x) for x in (wind_east, wind_north, thickness, geopot)
    )
    field = (z.lat, z.lev, z.lon)
    forward, inverse = (jnp.asarray(x) for x in basis_tables(z))
    phase = jnp.asarray(phase_table(z))
    per_row = jnp.asarray(row_table(z))
    kept = kept_modes[None, :]
    slots = slot_table[None, :]
    payload = (z.rows, WIDE)
    rims = (4 * z.lev, z.lon)
    spec = (z.help, z.lev, z.spec_width)
    waves_lhs = pltpu.VMEM((z.ext // z.inverse_block * z.mm_rows, 3 * WIDE), jnp.bfloat16)

    row_shape, phase_shape = per_row.shape[1:], phase.shape[1:]
    pinned = [
        pltpu.with_memory_space_constraint(x, pltpu.HBM)
        for x in (wind_east, wind_north, geopot, per_row, phase, forward)
    ]
    columns_lhs = pltpu.VMEM((z.blocks * z.mm_rows, 3 * BLOCK), jnp.bfloat16)
    waves_lhs = pltpu.VMEM((z.ext // z.inverse_block * z.mm_rows, 3 * WIDE), jnp.bfloat16)

    share_first, to_even, to_odd, wind_east, wind_north, geopot, per_row, phase, forward = call(
        functools.partial(east_first, z),
        6,
        [(packed_rows(z.first), 128), rims, rims]
        + [pltpu.VMEM(s, jnp.float32) for s in (field, field, field, row_shape, phase_shape)]
        + [pltpu.VMEM(forward.shape, forward.dtype)],
        [
            columns_lhs,
            pltpu.VMEM((z.first, WIDE), jnp.float32),
            pltpu.SemaphoreType.DMA((12,)),
        ],
        1,
        {n: pltpu.HBM for n in range(6)},
    )(*pinned)
    second = round_up(z.own - z.first, 8)
    (share_second,) = call(
        functools.partial(east_shares_of, z, slice(z.first, z.own)),
        6,
        [(packed_rows(second), 128)],
        [columns_lhs, pltpu.VMEM((second, WIDE), jnp.float32)],
        0.18,
    )(wind_east, wind_north, geopot, per_row, phase, forward)
    east_firsts, east_seconds = (
        [x] + [shifted(x, "lon", s) for s in range(1, z.n_lon)] for x in (share_first, share_second)
    )
    met = []
    for start, rim in enumerate((to_even, to_odd)):
        pairs = [(i, i + 1) for i in range(start, z.n_lat - 1, 2)]
        met.append(lax.ppermute(rim, "lat", pairs + [(b, a) for a, b in pairs]))

    places = round_up(z.rows, 128)
    north_ahead, north_rest, north_new, chosen, kept_sorted = call(
        functools.partial(north_forward, z),
        10,
        [
            (packed_rows(z.ahead), 128),
            (packed_rows(z.rows - z.ahead), 128),
            (z.rows, z.lon),
            (z.rows, places),
            (z.rows, 128),
        ],
        [
            pltpu.VMEM((z.rows, z.lon), jnp.float32),
            columns_lhs,
            pltpu.VMEM((z.rows, WIDE), jnp.float32),
        ],
        0.8,
    )(
        wind_east, wind_north, geopot, *met, per_row, phase, forward, kept, slots
    )
    north_rests = [north_rest] + [shifted(north_rest, "lon", s) for s in range(1, z.n_lon)]
    polar_bands = [i for i in range(z.n_lat) if i < z.n_lat // 4 or i >= z.n_lat - z.n_lat // 4]
    north_aheads = [north_ahead]
    for distance in range(1, z.n_lon):
        route = [
            (band * z.n_lon + lon, band * z.n_lon + (lon + distance) % z.n_lon)
            for band in polar_bands
            for lon in range(z.n_lon)
        ]
        north_aheads.append(lax.ppermute(north_ahead, ("lat", "lon"), route))

    (first_here,) = call(arrival, 1, [(8, 128)], [], 0.95)(east_firsts[1])
    east_final, thick_part, east_keep, east_send = call(
        functools.partial(east_inverse, z),
        11 + 2 * z.n_lon,
        [field, (z.own, z.lon), spec, spec],
        [
            waves_lhs,
            pltpu.VMEM((z.own, z.ext), jnp.float32),
            pltpu.VMEM((z.own, WIDE), jnp.float32),
        ],
        1,
        {0: pltpu.SMEM},
    )(
        mean_depth, wind_east, wind_north, geopot, thickness, per_row, phase, kept, chosen,
        first_here, *east_firsts, *east_seconds, inverse,
    )

    to_helper, waves_ahead = call(
        functools.partial(send_spectra, z), 2 + z.n_lon, [(2, *spec), (z.ahead, WIDE)], [], 0.1
    )(east_send, kept_sorted, *north_aheads)
    arrived = lax.ppermute(
        to_helper, "lat", [(i, (i + z.half_axis) % z.n_lat) for i in polar_bands]
    )

    ahead_rows = jax.ShapeDtypeStruct((z.ahead, z.ext), jnp.bfloat16)
    ahead_high, ahead_low = call(
        functools.partial(ahead_inverse, z),
        3,
        [ahead_rows] * 2,
        [waves_lhs, pltpu.VMEM((z.ahead, z.ext), jnp.float32)],
        0.5,
    )(phase, waves_ahead, inverse)

    operands = (
        mean_depth, north_new, thick_part, per_row, phase, chosen, kept_sorted, waves_ahead,
        ahead_high, ahead_low, *north_rests, inverse,
    )
    in_vmem = pltpu.VMEM(field, jnp.float32)
    scratch = [waves_lhs, pltpu.VMEM((z.rows, z.ext), jnp.float32)]
    scratch += [pltpu.VMEM((z.mm_rows, z.ext), jnp.bfloat16)] * 2
    final_deeper, thick_deeper, column, north_keep = call(
        functools.partial(north_deeper, z),
        len(operands),
        [in_vmem, in_vmem, (z.lat, z.lon), spec],
        scratch,
        2,
        {0: pltpu.SMEM},
    )(*operands)
    deeper = [
        lax.ppermute(column, "lev", [(i, i - distance) for i in range(distance, z.n_lev)])
        for distance in range(1, z.n_lev)
    ]
    final_own, thick_own, joined = call(
        functools.partial(north_shallowest, z),
        3 + len(operands),
        [in_vmem, in_vmem, pltpu.VMEM((2, *spec), jnp.float32)],
        [pltpu.VMEM((z.lat, z.lon), jnp.float32), pltpu.VMEM(spec, jnp.float32)] + scratch,
        3.2,
        {3: pltpu.SMEM},
    )(east_keep, north_keep, arrived, *operands)
    north_final, thick_new, geo_new, spectra = call(
        functools.partial(finish, z),
        6 + len(deeper),
        [pltpu.HBM(field, jnp.float32)] * 3 + [pltpu.HBM((2, *spec), jnp.float32)],
        [pltpu.VMEM(field, jnp.float32), pltpu.SemaphoreType.DMA((3 + z.cuts,))],
        1,
        in_hbm=4,
    )(surface_geopot, final_deeper, thick_deeper, final_own, thick_own, *deeper, joined)
    return tuple(level_inside(x) for x in (east_final, north_final, thick_new, geo_new, spectra))


def solution(mesh):
    field = P(("members", "lev"), "lat", "lon")
    return jax.shard_map(
        local,
        mesh=mesh,
        in_specs=(field, field, field, field, P("lat", "lon"), P("lev"), P(), P()),
        out_specs=(field, field, field, field, P(None, ("members", "lev"), "lat", "lon")),
        check_vma=False,
    )
```
